512 devices in a mesh: gx: 4 (over y), gy: 8 (over x, core), gz: 16 (over z).
Axes of the slice: x: 4, y: 4, z: 16, core: 2. Of those that a mesh axis runs over, the one named last changes fastest.
Arguments:
- source: float32 [256, 256, 512], P('gz', 'gy', 'gx'), may hold values from -4 to 4
- labels: int32 [256, 256, 512], P('gz', 'gy', 'gx'), may hold values from 0 to 2
Outputs:
- potential: float32 [256, 256, 512], P('gz', 'gy', 'gx')
The draws below stay inside these ranges and needn't reach their ends.
All inputs are finite; a program needn't handle non-finite values.
Results may differ from the reference program's by a relative error of at most 0.00002.
Values sent between devices are 32-bit elements; how exact they have to be, the bound alone decides.
A program may use at most 128 MiB of HBM per device.

```python
import jax
import jax.numpy as jnp
from jax import lax

LEVELS = 4
PRE = 2
POST = 2
COARSE = 6
NZ = 256
NY = 256
NX = 512


def draw_source(key, part):
    key = jax.random.fold_in(key, 11)
    return jnp.clip(jax.random.normal(key, (NZ, NY, NX), jnp.float32), -4.0, 4.0)


def draw_labels(key, part):
    key = jax.random.fold_in(key, 23)
    key_z, key_y, key_x, key_radius, key_present = jax.random.split(key, 5)
    blocks_z = NZ // 4
    blocks_y = NY // 4
    blocks_x = NX // 4
    extent = (blocks_z, blocks_y, blocks_x)
    centre_z = jax.random.randint(key_z, extent, 0, 4) + 4 * lax.broadcasted_iota(jnp.int32, extent, 0)
    centre_y = jax.random.randint(key_y, extent, 0, 4) + 4 * lax.broadcasted_iota(jnp.int32, extent, 1)
    centre_x = jax.random.randint(key_x, extent, 0, 4) + 4 * lax.broadcasted_iota(jnp.int32, extent, 2)
    present = jax.random.randint(key_present, extent, 0, 5) < 3
    radius_sq = jnp.where(present, jax.random.randint(key_radius, extent, 2, 10), -100)
    cell_shape = (blocks_z, 4, blocks_y, 4, blocks_x, 4)
    cell_z = 4 * lax.broadcasted_iota(jnp.int32, cell_shape, 0) + lax.broadcasted_iota(jnp.int32, cell_shape, 1)
    cell_y = 4 * lax.broadcasted_iota(jnp.int32, cell_shape, 2) + lax.broadcasted_iota(jnp.int32, cell_shape, 3)
    cell_x = 4 * lax.broadcasted_iota(jnp.int32, cell_shape, 4) + lax.broadcasted_iota(jnp.int32, cell_shape, 5)
    solute = jnp.zeros(cell_shape, jnp.bool_)
    shell = jnp.zeros(cell_shape, jnp.bool_)
    for step_z in (-1, 0, 1):
        for step_y in (-1, 0, 1):
            for step_x in (-1, 0, 1):
                moved = []
                for table in (centre_z, centre_y, centre_x, radius_sq):
                    rolled = jnp.roll(table, (step_z, step_y, step_x), (0, 1, 2))
                    moved.append(rolled.reshape(blocks_z, 1, blocks_y, 1, blocks_x, 1))
                distance = (cell_z - moved[0]) ** 2 + (cell_y - moved[1]) ** 2 + (cell_x - moved[2]) ** 2
                solute = solute | (distance <= moved[3])
                shell = shell | (distance <= moved[3] + 5)
    labels = jnp.where(solute, 1, jnp.where(shell, 2, 0)).astype(jnp.int32)
    return labels.reshape(NZ, NY, NX)


def setup_inputs(seed: int = 0) -> dict:
    keys = jax.random.split(jax.random.key(seed), 3)
    source = draw_source(jax.random.fold_in(keys[2], 71), 0)
    labels = draw_labels(jax.random.fold_in(keys[2], 71), 0)
    return dict(source=source, labels=labels)


SOLUTE_PERMITTIVITY = 0.1
SOLVENT_SCREENING = 0.004


def neighbour_sum(padded):
    summed = padded[2:, 1:-1, 1:-1] + padded[:-2, 1:-1, 1:-1]
    summed = summed + padded[1:-1, 2:, 1:-1] + padded[1:-1, :-2, 1:-1]
    summed = summed + padded[1:-1, 1:-1, 2:] + padded[1:-1, 1:-1, :-2]
    return summed


def parity_grid(extent):
    total_index = lax.broadcasted_iota(jnp.int32, extent, 0)
    total_index = total_index + lax.broadcasted_iota(jnp.int32, extent, 1)
    total_index = total_index + lax.broadcasted_iota(jnp.int32, extent, 2)
    return total_index % 2


def coarsen(field):
    depth_z, depth_y, depth_x = field.shape
    blocks = field.reshape(depth_z // 2, 2, depth_y // 2, 2, depth_x // 2, 2)
    return blocks.sum(axis=(1, 3, 5)) * 0.125


def refine(field):
    return jnp.repeat(jnp.repeat(jnp.repeat(field, 2, 0), 2, 1), 2, 2)


def smooth(field, right, weight, diagonal, parity, sweeps):
    for sweep in range(sweeps):
        for colour in (0, 1):
            summed = neighbour_sum(jnp.pad(field, 1))
            field = jnp.where(parity == colour, (right + weight * summed) / diagonal, field)
    return field


def cycle(grid_level, right, permittivity, screening):
    weight = permittivity * (0.25 ** grid_level)
    diagonal = 6.0 * weight + screening
    parity = parity_grid(right.shape)
    field = jnp.zeros_like(right)
    if grid_level == LEVELS:
        return smooth(field, right, weight, diagonal, parity, COARSE)
    field = smooth(field, right, weight, diagonal, parity, PRE)
    residual = right - (diagonal * field - weight * neighbour_sum(jnp.pad(field, 1)))
    correction = cycle(grid_level + 1, coarsen(residual), coarsen(permittivity), coarsen(screening))
    field = field + refine(correction)
    return smooth(field, right, weight, diagonal, parity, POST)


def reference(source, labels):
    permittivity = jnp.where(labels == 1, SOLUTE_PERMITTIVITY, 1.0).astype(jnp.float32)
    screening = jnp.where(labels == 0, SOLVENT_SCREENING, 0.0).astype(jnp.float32)
    return cycle(0, source, permittivity, screening)
```

```python
import functools

import jax
import jax.numpy as jnp
from jax import lax
from jax.experimental import pallas as pl
from jax.experimental.pallas import tpu as pltpu
from jax.sharding import PartitionSpec as P

COARSE = 6
SOLUTE_PERMITTIVITY = 0.1
SOLVENT_SCREENING = 0.004

MESH = pl.DeviceIdType.MESH
HIGHEST = lax.Precision.HIGHEST
F32 = jnp.float32
COPIES = 176

NZ, NY, NX = 16, 32, 128


def iota(shape, dim):
    return lax.broadcasted_iota(jnp.int32, shape, dim)


def tiled(tile, rows, lanes):
    tile = jnp.concatenate([tile] * (rows // 8), axis=0)
    return jnp.concatenate([tile] * (lanes // 128), axis=1)


def dot(a, b):
    return jnp.dot(a, b, precision=HIGHEST, preferred_element_type=F32)


def neighbours(v, p, edges):
    c = v[p]
    rows, lanes = c.shape
    below, above, left, right = edges
    s = v[p - 1] + v[p + 1]
    shifted = pltpu.roll(c, 1, 0)
    s = s + (shifted if below is None else jnp.where(below, 0.0, shifted))
    shifted = pltpu.roll(c, rows - 1, 0)
    s = s + (shifted if above is None else jnp.where(above, 0.0, shifted))
    shifted = pltpu.roll(c, 1, 1)
    s = s + (shifted if left is None else jnp.where(left, 0.0, shifted))
    shifted = pltpu.roll(c, lanes - 1, 1)
    s = s + (shifted if right is None else jnp.where(right, 0.0, shifted))
    return c, s


def parity_of(rows, lanes):
    return tiled((iota((8, 128), 0) + iota((8, 128), 1)) & 1, rows, lanes)


def pairs(start, stop, body):
    def step(i, carry):
        p = start + 2 * i
        body(p, start & 1)
        body(p + 1, (start + 1) & 1)
        return carry

    lax.fori_loop(0, (stop - start) // 2, step, 0)


def half_sweep(v, bd, wd, start, stop, colour, edges, shift=0):
    par = parity_of(*v.shape[1:])

    def body(p, odd):
        c, s = neighbours(v, p, edges)
        new = bd(p - shift) + wd(p - shift) * s
        v[p] = jnp.where(par == ((odd + colour + shift) & 1), new, c)

    pairs(start, stop, body)


def first_half(v, bd, start, stop, shift=0):
    par = parity_of(*v.shape[1:])

    def body(p, odd):
        v[p] = jnp.where(par == ((odd + shift) & 1), bd(p - shift), 0.0)

    pairs(start, stop, body)


def kernel(sizes, *refs):
    (source, labels, out, bdw0, v0, vp0, d0, tt, ee, tv, ev, sy, syv, sxm, sxc, sxmv, sxcv, pk, pkc, g1, g1c,
     c1, r1, v1, vp1, bd1, wd1, in1, c2, r2, v2, vp2, bd2, wd2, in2, z3, z3c, y3s, y3cs, y3, y3c, p3, p3c,
     c3, v3, bd3, wd3, in3, c4, v4, bd4, wd4, in4, work, work2, ssem, rsem) = refs
    count = dict(gx=sizes[0], gy=sizes[1], gz=sizes[2])
    gx, gy, gz = lax.axis_index("gx"), lax.axis_index("gy"), lax.axis_index("gz")
    number = [0]

    def device(offset):
        return tuple(
            lax.rem(here + (step + size) % size, size)
            for here, step, size in zip((gx, gy, gz), offset, sizes)
        )

    def send(source_ref, target_ref, offset):
        i = number[0]
        number[0] += 1
        copy = pltpu.make_async_remote_copy(
            src_ref=source_ref,
            dst_ref=target_ref,
            send_sem=ssem.at[i],
            recv_sem=rsem.at[i],
            device_id=device(offset),
            device_id_type=MESH,
        )
        copy.start()
        return copy

    def finish(copies):
        for copy in copies:
            copy.wait()

    peers = set()
    for a in (-1, 0, 1):
        for b in (-1, 0, 1):
            for c in (-1, 0, 1):
                peers.add((a, b, c))
    for b in (-1, 0, 1):
        for c in (-2, 2):
            peers.add((0, b, c))
    for i in range(1, sizes[0]):
        peers.add((i, 0, 0))
    for i in range(1, sizes[1]):
        peers.add((0, i, 0))
    for i in range(1, sizes[2]):
        peers.add((0, 0, i))
    peers = sorted({tuple(step % size for step, size in zip(o, sizes)) for o in peers} - {(0, 0, 0)})
    barrier = pltpu.get_barrier_semaphore()
    for offset in peers:
        pl.semaphore_signal(barrier, inc=1, device_id=device(offset), device_id_type=MESH)

    lane = iota((8, 128), 1)
    sub = iota((8, 128), 0)
    low4 = sub < 4
    x_lo, x_hi = gx > 0, gx < sizes[0] - 1
    y_lo, y_hi = gy > 0, gy < sizes[1] - 1
    z_lo, z_hi = gz > 0, gz < sizes[2] - 1

    ee[...] = jnp.zeros(ee.shape, F32)

    def prepare(z, carry):
        label = labels[z]
        permittivity = jnp.where(label == 1, SOLUTE_PERMITTIVITY, 1.0).astype(F32)
        screening = jnp.where(label == 0, SOLVENT_SCREENING, 0.0).astype(F32)
        diagonal = 6.0 * permittivity + screening
        inverse = 1.0 / diagonal
        d0[z] = diagonal
        for f, value in enumerate((source[z] * inverse, permittivity * inverse)):
            bdw0[f, z + 4, 0:NY, 0:NX] = value
            pack_edges(value, tt, ee, f, z)
        return carry

    def pack_edges(value, t_ref, e_ref, f, z):
        t_ref[f, z] = jnp.where(low4, value[0:8], value[NY - 8 : NY])
        group = tiled(lane >> 3, NY, 128)
        rolled = pltpu.roll(value, 8 * z + 4, 1)
        e_ref[f, 0:NY] = jnp.where(group == z, rolled, e_ref[f, 0:NY])

    def pack_corner(e_ref, f):
        e_ref[f, NY : NY + 8] = jnp.where(low4, e_ref[f, 0:8], e_ref[f, NY - 8 : NY])

    lax.fori_loop(0, NZ, prepare, 0)
    for f in (0, 1):
        pack_corner(ee, f)

    def slot(step):
        return 1 - step

    def send_halo0(own, target, t_ref, e_ref, y_ref, xm_ref, xc_ref):
        copies = []
        for c in (1, -1):
            first = 16 if c == 1 else 4
            copies.append(
                send(
                    own.at[:, pl.ds(first, 4), pl.ds(0, NY), pl.ds(0, NX)],
                    target.at[:, pl.ds(0 if c == 1 else 20, 4), pl.ds(0, NY), pl.ds(0, NX)],
                    (0, 0, c),
                )
            )
        for b in (1, -1):
            side = 0 if b == 1 else 1
            for c in (0, 1, -1):
                first, size, to = {0: (0, 16, 4), 1: (12, 4, 0), -1: (0, 4, 20)}[c]
                copies.append(
                    send(t_ref.at[:, pl.ds(first, size)], y_ref.at[side, :, pl.ds(to, size)], (0, b, c))
                )
        for a in (1, -1):
            side = 0 if a == 1 else 1
            for c in (0, 1, -1):
                copies.append(send(e_ref.at[:, pl.ds(0, NY)], xm_ref.at[side, slot(c)], (a, 0, c)))
                for b in (1, -1):
                    copies.append(
                        send(
                            e_ref.at[:, pl.ds(NY, 8)],
                            xc_ref.at[side, slot(c), 0 if b == 1 else 1],
                            (a, b, c),
                        )
                    )
        return copies

    in_low_half = (lane & 7) >= 4

    def fill_halo0(target, f, y_ref, xm_ref, xc_ref):
        x_valid = jnp.where(in_low_half, x_hi.astype(jnp.int32), x_lo.astype(jnp.int32))
        y_valid = jnp.where(low4, y_hi.astype(jnp.int32), y_lo.astype(jnp.int32))
        xy_valid = x_valid * y_valid
        edge_lanes = ((lane < 4) | (lane >= 124)).astype(jnp.int32)
        lane_main = tiled(in_low_half.astype(jnp.int32), NY, 128) > 0
        valid_main = tiled(x_valid, NY, 128) > 0
        edges = tiled(edge_lanes, NY + 8, 128)
        for part, (first, size, z_first, z_valid) in enumerate(
            ((0, 4, 12, z_lo), (4, 16, 0, None), (20, 4, 0, z_hi))
        ):
            ok = jnp.int32(1) if z_valid is None else z_valid.astype(jnp.int32)
            main = jnp.where(lane_main, xm_ref[1, part, f], xm_ref[0, part, f])
            main = jnp.where(valid_main, main, 0.0)
            below = jnp.where(in_low_half, xc_ref[1, part, 0, f], xc_ref[0, part, 0, f])
            above = jnp.where(in_low_half, xc_ref[1, part, 1, f], xc_ref[0, part, 1, f])
            corner = jnp.where(xy_valid > 0, jnp.where(low4, above, below), 0.0)
            packed = jnp.concatenate([main, corner], axis=0)

            def plane(i, carry):
                p = first + i
                rolled = pltpu.roll(packed, 252 - 8 * (z_first + i), 1)
                target[f, p, :, NX : 2 * NX] = jnp.where(edges * ok > 0, rolled, 0.0)
                rows = jnp.where(low4, y_ref[1, f, p], y_ref[0, f, p])
                target[f, p, NY : NY + 8, 0:NX] = jnp.where(y_valid * ok > 0, rows, 0.0)
                if z_valid is not None:
                    whole = target[f, p, 0:NY, 0:NX]
                    target[f, p, 0:NY, 0:NX] = jnp.where(tiled(0 * lane + ok, NY, NX) > 0, whole, 0.0)
                return carry

            lax.fori_loop(0, size, plane, 0)

    pl.semaphore_wait(barrier, len(peers))
    halo0 = send_halo0(bdw0, bdw0, tt, ee, sy, sxm, sxc)

    row_i, lane_i = iota((128, 128), 0), iota((128, 128), 1)
    to_low = jnp.where((row_i >> 1) == lane_i, 0.125, 0.0).astype(F32)
    to_high = jnp.where((row_i >> 1) == lane_i - 64, 0.125, 0.0).astype(F32)

    def rows_summed(size):
        half = size // 2
        return work[pl.ds(0, half, stride=2), :] + work[pl.ds(1, half, stride=2), :]

    def pack_level1(target, f):
        summed = rows_summed(256)
        target[f] = dot(summed[0:64], to_low) + dot(summed[64:128], to_high)

    def gather_gx(packed, slots):
        slots[gx] = packed[...]
        return [send(packed, slots.at[gx], (i, 0, 0)) for i in range(1, sizes[0])]

    def unpack_level1(slots, target, f):
        low = tiled((lane < 64).astype(jnp.int32), 16, 128) > 0
        for pair in range(2):
            for p in range(4):
                a = slots[2 * pair, f, pl.ds(16 * p, 16)]
                b = slots[2 * pair + 1, f, pl.ds(16 * p, 16)]
                lanes = slice(128 * pair, 128 * pair + 128)
                target(p, lanes, jnp.where(low, a, pltpu.roll(b, 64, 1)))
                target(p + 4, lanes, jnp.where(low, pltpu.roll(a, 64, 1), b))

    def coefficient(f, z):
        label = labels[z]
        if f == 0:
            return jnp.where(label == 1, SOLUTE_PERMITTIVITY, 1.0).astype(F32)
        return jnp.where(label == 0, SOLVENT_SCREENING, 0.0).astype(F32)

    for f in (0, 1):
        for k in range(8):
            work[32 * k : 32 * k + 32, :] = coefficient(f, 2 * k) + coefficient(f, 2 * k + 1)
        pack_level1(pkc, f)
    coef1 = gather_gx(pkc, g1c)

    finish(halo0)
    for f in (0, 1):
        fill_halo0(bdw0, f, sy, sxm, sxc)

    def send_halo1(own, target, width):
        copies = []
        for c in (0, 1, -1):
            planes = {0: (8, 8, 8), 1: (16 - width, width, 8 - width), -1: (8, width, 16)}[c]
            for b in (0, 1, -1):
                rows = {0: (0, 16, 0), 1: (8, 8, 24), -1: (0, 8, 16)}[b]
                if (b, c) != (0, 0):
                    copies.append(
                        send(
                            own(pl.ds(planes[0], planes[1]), pl.ds(rows[0], rows[1])),
                            target(pl.ds(planes[2], planes[1]), pl.ds(rows[2], rows[1])),
                            (0, b, c),
                        )
                    )
        return copies

    def send_halo2(own, target, steps):
        copies = []
        for c in steps:
            for b in (0, 1, -1):
                if (b, c) != (0, 0):
                    copies.append(
                        send(
                            own(pl.ds(8, 4), pl.ds(0, 8)),
                            target(pl.ds(8 - 4 * c, 4), pl.ds({0: 0, 1: 16, -1: 8}[b], 8)),
                            (0, b, c),
                        )
                    )
        return copies

    finish(coef1)
    for f in (0, 1):

        def put(p, lanes, value):
            c1[f, 8 + p, 0:16, lanes] = value

        unpack_level1(g1c, put, f)
    view1 = lambda a, b: c1.at[:, a, b]
    coef1 = send_halo1(view1, view1, 5)

    bd0_at = lambda p: bdw0[0, p]
    wd0_at = lambda p: bdw0[1, p]
    no_edges = (None,) * 4
    first_half(v0.at[0], bd0_at, 0, 24)
    half_sweep(v0.at[0], bd0_at, wd0_at, 1, 23, 1, no_edges)
    half_sweep(v0.at[0], bd0_at, wd0_at, 2, 22, 0, no_edges)
    half_sweep(v0.at[0], bd0_at, wd0_at, 3, 21, 1, no_edges)

    def residual0(k, carry):
        total = None
        for p in (4 + 2 * k, 5 + 2 * k):
            c, s = neighbours(v0.at[0], p, no_edges)
            value = bdw0[0, p, 0:NY, 0:NX] - c[0:NY, 0:NX] + bdw0[1, p, 0:NY, 0:NX] * s[0:NY, 0:NX]
            value = d0[p - 4] * value
            total = value if total is None else total + value
        work[pl.ds(pl.multiple_of(32 * k, 32), 32), :] = total
        return carry

    lax.fori_loop(0, 8, residual0, 0)
    pack_level1(pk, 0)
    right1 = gather_gx(pk, g1)

    ev[...] = jnp.zeros(ev.shape, F32)

    def pack_v(z, carry):
        value = v0[0, z + 4, 0:NY, 0:NX]
        pack_edges(value, tv, ev, 0, z)
        vp0[0, z + 4, 0:NY, 0:NX] = value
        return carry

    lax.fori_loop(0, NZ, pack_v, 0)
    pack_corner(ev, 0)
    halo_v0 = send_halo0(v0, vp0, tv, ev, syv, sxmv, sxcv)

    finish(coef1)

    def row_valid(rows, own):
        tiles = [jnp.ones((8, 128), jnp.int32)] * (own // 8)
        tiles += [0 * lane + y_hi.astype(jnp.int32), 0 * lane + y_lo.astype(jnp.int32)]
        return jnp.concatenate(tiles, axis=0)

    def plane_valid(p, below, size):
        before = jnp.where(p < below, z_lo.astype(jnp.int32), 1)
        behind = jnp.where(p >= below + size, z_hi.astype(jnp.int32), 1)
        return before * behind

    def coefficients(c_at, wd_at, in_at, planes, scale, valid):
        def body(p, carry):
            weight = c_at(0, p) * scale
            diagonal = 6.0 * weight + c_at(1, p)
            ok = diagonal > 0.0
            if valid is not None:
                ok = ok & (valid(p) > 0)
            inverse = jnp.where(ok, 1.0 / jnp.where(ok, diagonal, 1.0), 0.0)
            in_at[p] = inverse
            wd_at[p] = weight * inverse
            return carry

        lax.fori_loop(planes[0], planes[1], body, 0)

    rows1 = jnp.concatenate([row_valid(32, 16)] * 2, axis=1)
    rows2 = row_valid(24, 8)

    def valid1(p):
        return rows1 * plane_valid(p, 8, 8)

    def valid2(p):
        z = gz * 4 + p - 8
        ok = jnp.where(z >= 0, 1, 0) * jnp.where(z < 4 * sizes[2], 1, 0)
        return rows2 * ok

    coefficients(lambda f, p: c1[f, p], wd1, in1, (3, 21), 0.25, valid1)

    half_i, half_l = iota((256, 128), 0), iota((256, 128), 1)
    to_half = jnp.where((half_i >> 1) == half_l, 0.125, 0.0).astype(F32)

    def coarsen_level1(pair):
        for k in range(4):
            total = pair(k)
            for h in (0, 1):
                work2[h, 16 * k : 16 * k + 16, :] = total[:, 128 * h : 128 * h + 128]
        halves = [work2[h, pl.ds(0, 32, stride=2), :] + work2[h, pl.ds(1, 32, stride=2), :] for h in (0, 1)]
        return dot(jnp.concatenate(halves, axis=1), to_half)

    for f in (0, 1):
        coarse = coarsen_level1(lambda k: c1[f, 8 + 2 * k, 0:16] + c1[f, 9 + 2 * k, 0:16])
        for k in range(4):
            c2[f, 8 + k, 0:8] = coarse[8 * k : 8 * k + 8]
    view2 = lambda a, b: c2.at[:, a, b]
    coef2 = send_halo2(view2, view2, (0, 1, -1, 2, -2))

    finish(right1)

    def put_right(p, lanes, value):
        r1[8 + p, 0:16, lanes] = value

    unpack_level1(g1, put_right, 0)
    view_r1 = lambda a, b: r1.at[a, b]
    right1 = send_halo1(view_r1, view_r1, 5)

    finish(coef2)
    coefficients(lambda f, p: c2[f, p], wd2, in2, (2, 18), 0.0625, valid2)

    third_lane = lane_i - jnp.where(gz >= sizes[2] // 2, 64, 0)
    to_third = jnp.where(((row_i >> 1) == third_lane) & (third_lane >= 0) & (third_lane < 64), 0.125, 0.0)
    to_third = to_third.astype(F32)

    def coarsen_level2(pair):
        for k in range(2):
            work[8 * k : 8 * k + 8, :] = pair(k)
        return dot(rows_summed(16), to_third)

    def gather_gz(piece, slots):
        slots[gz] = piece[...]
        return [send(piece, slots.at[gz], (0, 0, i)) for i in range(1, sizes[2])]

    def gather_gy(slots, packed, target, fields):
        for f in range(fields):
            for k in range(8):
                packed[f, k] = slots[k, f] + slots[k + 8, f]
        target[gy] = packed[...]
        return [send(packed, target.at[gy], (0, i, 0)) for i in range(1, sizes[1])]

    for f in (0, 1):
        p3c[f] = coarsen_level2(lambda k: c2[f, 8 + 2 * k, 0:8] + c2[f, 9 + 2 * k, 0:8])
    coef3 = gather_gz(p3c, z3c)

    finish(halo_v0)
    fill_halo0(vp0, 0, syv, sxmv, sxcv)

    finish(right1)

    def scaled(target, right, inverse, start, stop):
        def body(p, carry):
            target[p] = right[p] * inverse[p]
            return carry

        lax.fori_loop(start, stop, body, 0)

    scaled(bd1, r1, in1, 3, 21)
    lanes1 = jnp.concatenate([lane, lane + 128], axis=1)
    lanes1 = jnp.concatenate([lanes1] * 4, axis=0)
    edges1 = (None, None, lanes1 == 0, lanes1 == 255)
    bd1_at = lambda p: bd1[p]
    wd1_at = lambda p: wd1[p]
    first_half(v1, bd1_at, 4, 20)
    half_sweep(v1, bd1_at, wd1_at, 5, 19, 1, edges1)
    half_sweep(v1, bd1_at, wd1_at, 6, 18, 0, edges1)
    half_sweep(v1, bd1_at, wd1_at, 7, 17, 1, edges1)

    def residual1(k):
        total = None
        for p in (8 + 2 * k, 9 + 2 * k):
            c, s = neighbours(v1, p, edges1)
            diagonal = 1.5 * c1[0, p, 0:16] + c1[1, p, 0:16]
            value = diagonal * (bd1[p, 0:16] - c[0:16] + wd1[p, 0:16] * s[0:16])
            total = value if total is None else total + value
        return total

    coarse = coarsen_level1(residual1)
    for k in range(4):
        r2[8 + k, 0:8] = coarse[8 * k : 8 * k + 8]
    view_r2 = lambda a, b: r2.at[a, b]
    right2 = send_halo2(view_r2, view_r2, (0, 1, -1))
    right2_far = send_halo2(view_r2, view_r2, (2, -2))
    for k in range(8):
        vp1[8 + k, 0:16] = v1[8 + k, 0:16]
    halo_v1 = send_halo1(lambda a, b: v1.at[a, b], lambda a, b: vp1.at[a, b], 6)
    finish(coef3)
    coef3 = gather_gy(z3c, y3cs, y3c, 2)

    finish(right2)
    scaled(bd2, r2, in2, 4, 16)
    lanes2 = jnp.concatenate([lane] * 3, axis=0)
    edges2 = (None, None, lanes2 == 0, lanes2 == 127)
    bd2_at = lambda p: bd2[p]
    wd2_at = lambda p: wd2[p]
    first_half(v2, bd2_at, 4, 16)
    half_sweep(v2, bd2_at, wd2_at, 5, 15, 1, edges2)
    half_sweep(v2, bd2_at, wd2_at, 6, 14, 0, edges2)
    half_sweep(v2, bd2_at, wd2_at, 7, 13, 1, edges2)

    def residual2(k):
        total = None
        for p in (8 + 2 * k, 9 + 2 * k):
            c, s = neighbours(v2, p, edges2)
            diagonal = 0.375 * c2[0, p, 0:8] + c2[1, p, 0:8]
            value = diagonal * (bd2[p, 0:8] - c[0:8] + wd2[p, 0:8] * s[0:8])
            total = value if total is None else total + value
        return total

    p3[0] = coarsen_level2(residual2)
    right3 = gather_gz(p3, z3)
    for k in range(4):
        vp2[8 + k, 0:8] = v2[8 + k, 0:8]
    halo_v2 = send_halo2(lambda a, b: v2.at[a, b], lambda a, b: vp2.at[a, b], (0, 1, -1, 2, -2))

    finish(coef3)

    def unpack_level3(slots, f, put):
        for k in range(8):
            for t in range(4):
                a, b = slots[2 * t, f, k], slots[2 * t + 1, f, k]
                put(2 * k, slice(8 * t, 8 * t + 8), jnp.where(low4, a, pltpu.roll(b, 4, 0)))
                put(2 * k + 1, slice(8 * t, 8 * t + 8), jnp.where(low4, pltpu.roll(a, 4, 0), b))

    for f in (0, 1):

        def put3(p, rows, value):
            c3[f, p, rows] = value

        unpack_level3(y3c, f, put3)
    coefficients(lambda f, p: c3[f, p], wd3, in3, (0, 16), 0.25**3, None)

    to_fourth = jnp.where(
        ((row_i >> 6) == (lane_i >> 6)) & (((row_i & 63) >> 1) == (lane_i & 63)), 0.125, 0.0
    ).astype(F32)

    def coarsen_level3(pair):
        for k in range(8):
            work[32 * k : 32 * k + 32, :] = pair(k)
        return dot(rows_summed(256), to_fourth)

    for f in (0, 1):
        coarse = coarsen_level3(lambda k: c3[f, 2 * k] + c3[f, 2 * k + 1])
        for k in range(8):
            c4[f, k] = coarse[16 * k : 16 * k + 16]
    coefficients(lambda f, p: c4[f, p], wd4, in4, (0, 8), 0.25**4, None)
    finish(right2_far)
    scaled(bd2, r2, in2, 2, 4)
    scaled(bd2, r2, in2, 16, 18)
    finish(halo_v1)

    def clean(target, valid, start, stop):
        def body(p, carry):
            target[p] = jnp.where(valid(p) > 0, target[p], 0.0)
            return carry

        lax.fori_loop(start, stop, body, 0)

    clean(vp1, valid1, 2, 22)

    finish(right3)
    right3 = gather_gy(z3, y3s, y3, 1)
    finish(halo_v2)
    clean(vp2, valid2, 0, 20)
    finish(right3)

    def put_bd3(p, rows, value):
        bd3[p, rows] = value * in3[p, rows]

    unpack_level3(y3, 0, put_bd3)

    def ends(v, planes):
        low = tiled((lane < 64).astype(jnp.int32), v.shape[1], 128) > 0
        v[0] = jnp.where(low, 0.0, pltpu.roll(v[planes], 64, 1))
        v[planes + 1] = jnp.where(low, pltpu.roll(v[1], 64, 1), 0.0)

    lanes3 = jnp.concatenate([lane & 63] * 4, axis=0)
    rows3 = iota((32, 128), 0)
    edges3 = (rows3 == 0, rows3 == 31, lanes3 == 0, lanes3 == 63)
    rows4 = iota((16, 128), 0)
    edges4 = (rows4 == 0, rows4 == 15, None, None)
    bd3_at = lambda p: bd3[p]
    wd3_at = lambda p: wd3[p]
    bd4_at = lambda p: bd4[p]
    wd4_at = lambda p: wd4[p]

    def half3(colour):
        ends(v3, 16)
        half_sweep(v3, bd3_at, wd3_at, 1, 17, colour, edges3, 1)

    def half4(colour):
        ends(v4, 8)
        half_sweep(v4, bd4_at, wd4_at, 1, 9, colour, edges4, 1)

    first_half(v3, bd3_at, 1, 17, 1)
    half3(1)
    half3(0)
    half3(1)
    ends(v3, 16)

    def residual3(k):
        total = None
        for p in (2 * k, 2 * k + 1):
            c, s = neighbours(v3, p + 1, edges3)
            diagonal = 6.0 * 0.25**3 * c3[0, p] + c3[1, p]
            value = diagonal * (bd3[p] - c + wd3[p] * s)
            total = value if total is None else total + value
        return total

    coarse = coarsen_level3(residual3)
    for k in range(8):
        bd4[k] = coarse[16 * k : 16 * k + 16] * in4[k]
    first_half(v4, bd4_at, 1, 9, 1)
    half4(1)

    def sweep4(i, carry):
        half4(0)
        half4(1)
        return carry

    lax.fori_loop(1, COARSE, sweep4, 0)

    from_fourth = jnp.where(
        ((row_i >> 6) == (lane_i >> 6)) & (((lane_i & 63) >> 1) == (row_i & 63)), 1.0, 0.0
    ).astype(F32)
    wide = jnp.concatenate([v4[1 + k] for k in range(8)], axis=0)
    wide = dot(wide, from_fourth)
    work[pl.ds(0, 128, stride=2), :] = wide
    work[pl.ds(1, 128, stride=2), :] = wide

    def add3(k, carry):
        correction = work[pl.ds(pl.multiple_of(32 * k, 32), 32), :]
        v3[1 + 2 * k] = v3[1 + 2 * k] + correction
        v3[2 + 2 * k] = v3[2 + 2 * k] + correction
        return carry

    lax.fori_loop(0, 8, add3, 0)
    half3(0)
    half3(1)
    half3(0)
    half3(1)

    from_third = jnp.where((lane_i >> 1) == (row_i & 63), 1.0, 0.0).astype(F32)
    lane_half = tiled(lane >> 6, 32, 128)
    picked = []
    for i in range(10):
        z = 2 * gz - 4 + i
        inside = jnp.where(z >= 0, 1, 0) * jnp.where(z < 32, 1, 0)
        z = jnp.clip(z, 0, 31)
        index, half = z & 15, z >> 4
        keep = jnp.where(lane_half == half, inside, 0) > 0
        picked.append(jnp.where(keep, v3[1 + index], 0.0))
    wide = dot(jnp.concatenate(picked, axis=0), from_third)
    work[pl.ds(0, 320, stride=2), :] = wide
    work[pl.ds(1, 320, stride=2), :] = wide
    own_row = pl.multiple_of(8 * gy, 8)
    next_row = pl.multiple_of(8 * jnp.minimum(gy + 1, sizes[1] - 1), 8)
    before_row = pl.multiple_of(8 * jnp.maximum(gy - 1, 0), 8)

    def add2(i, carry):
        base = pl.multiple_of(64 * i, 64)
        parts = [work[pl.ds(base + row, 8), :] for row in (own_row, next_row, before_row)]
        correction = jnp.where(rows2 > 0, jnp.concatenate(parts, axis=0), 0.0)
        vp2[2 * i] = vp2[2 * i] + correction
        vp2[2 * i + 1] = vp2[2 * i + 1] + correction
        return carry

    lax.fori_loop(0, 10, add2, 0)
    half_sweep(vp2, bd2_at, wd2_at, 2, 18, 0, edges2)
    half_sweep(vp2, bd2_at, wd2_at, 3, 17, 1, edges2)
    half_sweep(vp2, bd2_at, wd2_at, 4, 16, 0, edges2)
    half_sweep(vp2, bd2_at, wd2_at, 5, 15, 1, edges2)

    def spread(wide, rows):
        for h in (0, 1):
            part = wide[:, 128 * h : 128 * h + 128]
            work2[h, pl.ds(0, rows, stride=2), :] = part
            work2[h, pl.ds(1, rows, stride=2), :] = part

    def copied(base, rows):
        return jnp.concatenate([work2[h, pl.ds(base, rows), :] for h in (0, 1)], axis=1)

    wide_i, wide_l = iota((128, 256), 0), iota((128, 256), 1)
    from_second = jnp.where((wide_l >> 1) == wide_i, 1.0, 0.0).astype(F32)
    picked = []
    for p in range(5, 15):
        picked += [vp2[p, 0:8], jnp.where(low4, vp2[p, 8:16], vp2[p, 16:24])]
    wide = dot(jnp.concatenate(picked, axis=0), from_second)
    spread(wide, 160)

    def add1(i, carry):
        correction = copied(pl.multiple_of(32 * i, 32), 32)
        vp1[2 + 2 * i] = vp1[2 + 2 * i] + correction
        vp1[3 + 2 * i] = vp1[3 + 2 * i] + correction
        return carry

    lax.fori_loop(0, 10, add1, 0)
    half_sweep(vp1, bd1_at, wd1_at, 3, 21, 0, edges1)
    half_sweep(vp1, bd1_at, wd1_at, 4, 20, 1, edges1)
    half_sweep(vp1, bd1_at, wd1_at, 5, 19, 0, edges1)
    half_sweep(vp1, bd1_at, wd1_at, 6, 18, 1, edges1)

    first_i, first_l = iota((256, 256), 0), iota((256, 256), 1)
    column = jnp.where(first_l < NX + 4, first_l, jnp.where(first_l >= 2 * NX - 4, first_l - 2 * NX, -1024))
    from_first = jnp.where(((gx * NX + column) >> 1) == first_i, 1.0, 0.0).astype(F32)
    tile_low2 = jnp.concatenate([sub, sub], axis=1) < 2
    picked = []
    for p in range(6, 18):
        picked += [vp1[p, 0:16], jnp.where(tile_low2, vp1[p, 16:24], pltpu.roll(vp1[p, 24:32], 4, 0))]
    wide = dot(jnp.concatenate(picked, axis=0), from_first)
    spread(wide, 288)

    def add0(i, carry):
        correction = copied(pl.multiple_of(48 * i, 16), 40)
        vp0[0, 2 * i] = vp0[0, 2 * i] + correction
        vp0[0, 2 * i + 1] = vp0[0, 2 * i + 1] + correction
        return carry

    lax.fori_loop(0, 12, add0, 0)
    half_sweep(vp0.at[0], bd0_at, wd0_at, 1, 23, 0, no_edges)
    half_sweep(vp0.at[0], bd0_at, wd0_at, 2, 22, 1, no_edges)
    half_sweep(vp0.at[0], bd0_at, wd0_at, 3, 21, 0, no_edges)
    par = parity_of(NY, NX)

    def last(p, odd):
        c, s = neighbours(vp0.at[0], p, no_edges)
        new = bdw0[0, p, 0:NY, 0:NX] + bdw0[1, p, 0:NY, 0:NX] * s[0:NY, 0:NX]
        out[p - 4] = jnp.where(par == ((odd + 1) & 1), new, c[0:NY, 0:NX])

    pairs(4, 20, last)


def local(sizes, source, labels):
    vmem = lambda *shape: pltpu.VMEM(shape, F32)
    scratch = [
        vmem(2, 24, 40, 256),
        vmem(1, 24, 40, 256),
        vmem(1, 24, 40, 256),
        vmem(16, 32, 128),
        vmem(2, 16, 8, 128),
        vmem(2, 40, 128),
        vmem(1, 16, 8, 128),
        vmem(1, 40, 128),
        vmem(2, 2, 24, 8, 128),
        vmem(2, 1, 24, 8, 128),
        vmem(2, 3, 2, 32, 128),
        vmem(2, 3, 2, 2, 8, 128),
        vmem(2, 3, 1, 32, 128),
        vmem(2, 3, 2, 1, 8, 128),
        vmem(1, 64, 128),
        vmem(2, 64, 128),
        vmem(sizes[0], 1, 64, 128),
        vmem(sizes[0], 2, 64, 128),
        vmem(2, 24, 32, 256),
        vmem(24, 32, 256),
        vmem(24, 32, 256),
        vmem(24, 32, 256),
        vmem(24, 32, 256),
        vmem(24, 32, 256),
        vmem(24, 32, 256),
        vmem(2, 20, 24, 128),
        vmem(20, 24, 128),
        vmem(20, 24, 128),
        vmem(20, 24, 128),
        vmem(20, 24, 128),
        vmem(20, 24, 128),
        vmem(20, 24, 128),
        vmem(sizes[2], 1, 8, 128),
        vmem(sizes[2], 2, 8, 128),
        vmem(1, 8, 8, 128),
        vmem(2, 8, 8, 128),
        vmem(sizes[1], 1, 8, 8, 128),
        vmem(sizes[1], 2, 8, 8, 128),
        vmem(1, 8, 128),
        vmem(2, 8, 128),
        vmem(2, 16, 32, 128),
        vmem(18, 32, 128),
        vmem(16, 32, 128),
        vmem(16, 32, 128),
        vmem(16, 32, 128),
        vmem(2, 8, 16, 128),
        vmem(10, 16, 128),
        vmem(8, 16, 128),
        vmem(8, 16, 128),
        vmem(8, 16, 128),
        vmem(640, 128),
        vmem(2, 576, 128),
        pltpu.SemaphoreType.DMA((COPIES,)),
        pltpu.SemaphoreType.DMA((COPIES,)),
    ]
    return pl.pallas_call(
        functools.partial(kernel, sizes),
        out_shape=jax.ShapeDtypeStruct(source.shape, F32),
        in_specs=[pl.BlockSpec(memory_space=pltpu.VMEM)] * 2,
        out_specs=pl.BlockSpec(memory_space=pltpu.VMEM),
        scratch_shapes=scratch,
        compiler_params=pltpu.CompilerParams(
            collective_id=0, has_side_effects=True, vmem_limit_bytes=48 * 2**20
        ),
        name="v_cycle",
    )(source, labels)


def solution(mesh):
    sizes = tuple(mesh.shape[name] for name in ("gx", "gy", "gz"))
    return jax.shard_map(
        functools.partial(local, sizes),
        mesh=mesh,
        in_specs=(P("gz", "gy", "gx"), P("gz", "gy", "gx")),
        out_specs=P("gz", "gy", "gx"),
        check_vma=False,
    )
```

```python
import functools

import jax
import jax.numpy as jnp
import numpy as np
from jax import lax
from jax.experimental import pallas as pl
from jax.experimental.pallas import tpu as pltpu
from jax.sharding import PartitionSpec as P

COARSE = 6
SOLUTE_PERMITTIVITY = 0.1
SOLVENT_SCREENING = 0.004

MESH = pl.DeviceIdType.MESH
HIGHEST = lax.Precision.HIGHEST
F32 = jnp.float32
COPIES = 176

B0, B1, B2 = 8, 10, 16

NZ, NY, NX = 16, 32, 128


def iota(shape, dim):
    return lax.broadcasted_iota(jnp.int32, shape, dim)


def tiled(tile, rows, lanes):
    tile = jnp.concatenate([tile] * (rows // 8), axis=0)
    return jnp.concatenate([tile] * (lanes // 128), axis=1)


def dot(a, b):
    return jnp.dot(a, b, precision=HIGHEST, preferred_element_type=F32)


def neighbour_sum(before, c, behind, edges):
    rows, lanes = c.shape
    below, above, left, right = edges
    s = before + behind
    shifted = pltpu.roll(c, 1, 0)
    s = s + (shifted if below is None else jnp.where(below, 0.0, shifted))
    shifted = pltpu.roll(c, rows - 1, 0)
    s = s + (shifted if above is None else jnp.where(above, 0.0, shifted))
    shifted = pltpu.roll(c, 1, 1)
    s = s + (shifted if left is None else jnp.where(left, 0.0, shifted))
    shifted = pltpu.roll(c, lanes - 1, 1)
    s = s + (shifted if right is None else jnp.where(right, 0.0, shifted))
    return s


def neighbours(v, p, edges):
    c = v[p]
    return c, neighbour_sum(v[p - 1], c, v[p + 1], edges)


def parity_of(rows, lanes):
    return tiled((iota((8, 128), 0) + iota((8, 128), 1)) & 1, rows, lanes)


def far_first(size):
    return sorted(range(1, size), key=lambda step: -min(step, size - step))


def blocks(start, stop, block, body):
    count = (stop - start) // block

    def step(i, carry):
        body(start + block * i, start & 1, block)
        return carry

    if count > 1:
        lax.fori_loop(0, count, step, 0)
    elif count == 1:
        body(start, start & 1, block)
    if start + count * block < stop:
        first = start + count * block
        body(first, first & 1, stop - first)


def half_sweep(v, bd, wd, start, stop, colour, edges, block, shift=0):
    par = parity_of(*v.shape[1:])

    def body(first, odd, size):
        before, c = v[first - 1], v[first]
        for i in range(size):
            p = first + i
            behind = v[p + 1]
            s = neighbour_sum(before, c, behind, edges)
            new = bd(p - shift) + wd(p - shift) * s
            v[p] = jnp.where(par == ((odd + i + colour + shift) & 1), new, c)
            before, c = c, behind

    blocks(start, stop, block, body)


def first_half(v, bd, start, stop, block, shift=0):
    par = parity_of(*v.shape[1:])

    def body(first, odd, size):
        for i in range(size):
            p = first + i
            v[p] = jnp.where(par == ((odd + i + shift) & 1), bd(p - shift), 0.0)

    blocks(start, stop, block, body)


def kernel(sizes, *refs):
    (source_hbm, labels_hbm, out, source, labels, isem, bdw0, v0, vp0, d0, tt, ee, tv, ev, sy, syv, sxm0, sxm1, sxm2, sxc0, sxc1, sxc2, *rest) = refs
    (sxmv0, sxmv1, sxmv2, sxcv0, sxcv1, sxcv2, pk, pkc, g1, g1c,
     c1, r1, v1, vp1, bd1, wd1, in1, c2, r2, v2, vp2, bd2, wd2, in2, z3, z3c, y3s, y3cs, y3, y3c, p3, p3c,
     c3, v3, bd3, wd3, in3, c4, v4, bd4, wd4, in4, work, work2, ssem, rsem) = rest
    sxmv, sxcv = (sxmv0, sxmv1, sxmv2), (sxcv0, sxcv1, sxcv2)
    count = dict(gx=sizes[0], gy=sizes[1], gz=sizes[2])
    gx, gy, gz = lax.axis_index("gx"), lax.axis_index("gy"), lax.axis_index("gz")
    number = [0]

    def device(offset):
        return tuple(
            lax.rem(here + (step + size) % size, size)
            for here, step, size in zip((gx, gy, gz), offset, sizes)
        )

    def send(source_ref, target_ref, offset):
        i = number[0]
        number[0] += 1
        copy = pltpu.make_async_remote_copy(
            src_ref=source_ref,
            dst_ref=target_ref,
            send_sem=ssem.at[i],
            recv_sem=rsem.at[i],
            device_id=device(offset),
            device_id_type=MESH,
        )
        copy.start()
        return copy

    def finish(copies):
        for copy in copies:
            copy.wait()

    peers = set()
    for a in (-1, 0, 1):
        for b in (-1, 0, 1):
            for c in (-1, 0, 1):
                peers.add((a, b, c))
    for b in (-1, 0, 1):
        for c in (-2, 2):
            peers.add((0, b, c))
    for i in range(1, sizes[0]):
        peers.add((i, 0, 0))
    for i in range(1, sizes[1]):
        peers.add((0, i, 0))
    for i in range(1, sizes[2]):
        peers.add((0, 0, i))
    peers = sorted({tuple(step % size for step, size in zip(o, sizes)) for o in peers} - {(0, 0, 0)})
    barrier = pltpu.get_barrier_semaphore()
    for offset in peers:
        pl.semaphore_signal(barrier, inc=1, device_id=device(offset), device_id_type=MESH)

    loads = [
        pltpu.make_async_copy(labels_hbm, labels, isem.at[0]),
        pltpu.make_async_copy(source_hbm, source, isem.at[1]),
    ]
    for load in loads:
        load.start()

    lane = iota((8, 128), 1)
    sub = iota((8, 128), 0)
    low4 = sub < 4
    x_lo, x_hi = gx > 0, gx < sizes[0] - 1
    y_lo, y_hi = gy > 0, gy < sizes[1] - 1
    z_lo, z_hi = gz > 0, gz < sizes[2] - 1

    def constants(label):
        permittivity = np.array([1.0, SOLUTE_PERMITTIVITY, 1.0], np.float32)
        screening = np.array([SOLVENT_SCREENING, 0.0, 0.0], np.float32)
        diagonal = np.float32(6.0) * permittivity + screening
        inverse = np.float32(1.0) / diagonal
        choose = lambda t: jnp.where(label == 1, t[1], jnp.where(label == 0, t[0], t[2])).astype(F32)
        return choose(inverse), choose(permittivity * inverse), choose(diagonal)

    group = tiled(lane >> 3, NY, 128)

    def gathered_edges(plane):
        total = jnp.zeros((NY, 128), F32)
        for z in range(NZ):
            total = jnp.where(group == z, pltpu.roll(plane(z), 8 * z + 4, 1), total)
        return jnp.concatenate([total, jnp.where(low4, total[0:8], total[NY - 8 : NY])], axis=0)

    for load in loads:
        load.wait()
    for z in range(NZ):
        inverse, relative, diagonal = constants(labels[z])
        bd = source[z] * inverse
        d0[z] = diagonal
        bdw0[0, z + 4, 0:NY, 0:NX] = bd
        bdw0[1, z + 4, 0:NY, 0:NX] = relative
        tt[0, z] = jnp.where(low4, bd[0:8], pltpu.roll(relative[0:8], 4, 0))
        tt[1, z] = jnp.where(low4, pltpu.roll(relative[NY - 8 : NY], 4, 0), bd[NY - 8 : NY])
    edge_bd = gathered_edges(lambda z: bdw0[0, z + 4, 0:NY, 0:NX])
    edge_wd = gathered_edges(lambda z: bdw0[1, z + 4, 0:NY, 0:NX])
    ee[0], ee[1] = edge_bd, edge_wd
    quarter = tiled(lane >> 5, NY + 8, 128)
    inner = jnp.where(quarter == 1, pltpu.roll(edge_wd, 32, 1), pltpu.roll(edge_wd, 96, 1))
    ee[2] = jnp.where((quarter == 0) | (quarter == 3), edge_bd, inner)

    def slot(step):
        return 1 - step

    def send_halo0(own, target, t_of, same_of, other_of, y_ref, xm_ref, xc_ref):
        copies = []
        for c in (1, -1):
            first = 16 if c == 1 else 4
            copies.append(
                send(
                    own.at[:, pl.ds(first, 4), pl.ds(0, NY), pl.ds(0, NX)],
                    target.at[:, pl.ds(0 if c == 1 else 20, 4), pl.ds(0, NY), pl.ds(0, NX)],
                    (0, 0, c),
                )
            )
        for c in (1, -1, 0):
            edges = other_of if c else same_of
            to = slot(c)
            for a in (1, -1):
                side = 0 if a == 1 else 1
                for b in (1, -1):
                    copies.append(
                        send(
                            edges(pl.ds(NY, 8)),
                            xc_ref[to].at[side, 0 if b == 1 else 1],
                            (a, b, c),
                        )
                    )
            for b in (1, -1):
                side = 0 if b == 1 else 1
                first, size, start = {0: (0, 16, 4), 1: (12, 4, 0), -1: (0, 4, 20)}[c]
                copies.append(send(t_of(b, pl.ds(first, size)), y_ref.at[side, pl.ds(start, size)], (0, b, c)))
            for a in (1, -1):
                side = 0 if a == 1 else 1
                copies.append(send(edges(pl.ds(0, NY)), xm_ref[to].at[side], (a, 0, c)))
        return copies

    in_low_half = (lane & 7) >= 4

    def fill_halo0(target, f, rows_of, columns, starts):
        x_valid = jnp.where(in_low_half, x_hi.astype(jnp.int32), x_lo.astype(jnp.int32))
        y_valid = jnp.where(low4, y_hi.astype(jnp.int32), y_lo.astype(jnp.int32))
        xy_valid = x_valid * y_valid
        edge_lanes = ((lane < 4) | (lane >= 124)).astype(jnp.int32)
        lane_main = tiled(in_low_half.astype(jnp.int32), NY, 128) > 0
        for part, (first, size, z_valid) in enumerate(((0, 4, z_lo), (4, 16, None), (20, 4, z_hi))):
            ok = jnp.int32(1) if z_valid is None else z_valid.astype(jnp.int32)
            (main_right, above_right, below_right), (main_left, above_left, below_left) = columns(part)
            main = jnp.where(lane_main, main_right, main_left)
            main = jnp.where(tiled(x_valid * ok, NY, 128) > 0, main, 0.0)
            above = jnp.where(in_low_half, above_right, above_left)
            below = jnp.where(in_low_half, below_right, below_left)
            corner = jnp.where(xy_valid * ok > 0, jnp.where(low4, above, below), 0.0)
            packed = jnp.concatenate([main, corner], axis=0)
            edges = tiled(edge_lanes, NY + 8, 128) > 0
            row_ok = y_valid * ok > 0
            for i in range(size):
                p = first + i
                rolled = pltpu.roll(packed, (252 - 8 * (starts[part] + i)) % 128, 1)
                target[f, p, :, NX : 2 * NX] = jnp.where(edges, rolled, 0.0)
                target[f, p, NY : NY + 8, 0:NX] = jnp.where(row_ok, rows_of(p), 0.0)
            if z_valid is not None:

                @pl.when(jnp.logical_not(z_valid))
                def _():
                    for i in range(size):
                        target[f, first + i, 0:NY, 0:NX] = jnp.zeros((NY, NX), F32)

    def fill_coefficients0():
        for f in (0, 1):

            def rows_of(p):
                if f == 0:
                    return jnp.where(low4, sy[1, p], sy[0, p])
                return pltpu.roll(jnp.where(low4, sy[0, p], sy[1, p]), 4, 0)

            def columns(part):
                if part == 1:
                    return [(sxm1[s, f], sxc1[s, 1, f], sxc1[s, 0, f]) for s in (1, 0)]
                m, c = (sxm0, sxc0) if part == 0 else (sxm2, sxc2)
                return [(m[s], c[s, 1], c[s, 0]) for s in (1, 0)]

            fill_halo0(bdw0, f, rows_of, columns, ((12, 0, 0), (8, 0, 4))[f])

    def fill_v0():
        def columns(part):
            m, c = sxmv[part], sxcv[part]
            return [(m[s], c[s, 1], c[s, 0]) for s in (1, 0)]

        fill_halo0(vp0, 0, lambda p: jnp.where(low4, syv[1, p], syv[0, p]), columns, (12, 0, 0))


    row_i, lane_i = iota((128, 128), 0), iota((128, 128), 1)
    to_low = jnp.where((row_i >> 1) == lane_i, 0.125, 0.0).astype(F32)
    to_high = jnp.where((row_i >> 1) == lane_i - 64, 0.125, 0.0).astype(F32)

    def rows_summed(size):
        half = size // 2
        return work[pl.ds(0, half, stride=2), :] + work[pl.ds(1, half, stride=2), :]

    def pack_level1(target, f):
        summed = rows_summed(256)
        target[f] = dot(summed[0:64], to_low) + dot(summed[64:128], to_high)

    def gather_gx(packed, slots):
        slots[gx] = packed[...]
        return [send(packed, slots.at[gx], (i, 0, 0)) for i in far_first(sizes[0])]

    def unpack_level1(slots, target, f):
        low = tiled((lane < 64).astype(jnp.int32), 16, 128) > 0
        for pair in range(2):
            for p in range(4):
                a = slots[2 * pair, f, pl.ds(16 * p, 16)]
                b = slots[2 * pair + 1, f, pl.ds(16 * p, 16)]
                lanes = slice(128 * pair, 128 * pair + 128)
                target(p, lanes, jnp.where(low, a, pltpu.roll(b, 64, 1)))
                target(p + 4, lanes, jnp.where(low, pltpu.roll(a, 64, 1), b))

    def coefficient(f, z):
        label = labels[z]
        if f == 0:
            return jnp.where(label == 1, SOLUTE_PERMITTIVITY, 1.0).astype(F32)
        return jnp.where(label == 0, SOLVENT_SCREENING, 0.0).astype(F32)

    for f in (0, 1):
        for k in range(8):
            work[32 * k : 32 * k + 32, :] = coefficient(f, 2 * k) + coefficient(f, 2 * k + 1)
        pack_level1(pkc, f)
    pl.semaphore_wait(barrier, len(peers))
    halo0 = send_halo0(
        bdw0,
        bdw0,
        lambda b, planes: tt.at[0 if b == -1 else 1, planes],
        lambda rows: ee.at[pl.ds(0, 2), rows],
        lambda rows: ee.at[2, rows],
        sy,
        (sxm0, sxm1, sxm2),
        (sxc0, sxc1, sxc2),
    )
    coef1 = gather_gx(pkc, g1c)

    def send_halo1(own, target, width):
        copies = []
        for c in (0, 1, -1):
            planes = {0: (8, 8, 8), 1: (16 - width, width, 8 - width), -1: (8, width, 16)}[c]
            for b in (0, 1, -1):
                rows = {0: (0, 16, 0), 1: (8, 8, 24), -1: (0, 8, 16)}[b]
                if (b, c) != (0, 0):
                    copies.append(
                        send(
                            own(pl.ds(planes[0], planes[1]), pl.ds(rows[0], rows[1])),
                            target(pl.ds(planes[2], planes[1]), pl.ds(rows[2], rows[1])),
                            (0, b, c),
                        )
                    )
        return copies

    def send_halo2(own, target, steps):
        copies = []
        for c in steps:
            for b in (0, 1, -1):
                if (b, c) != (0, 0):
                    copies.append(
                        send(
                            own(pl.ds(8, 4), pl.ds(0, 8)),
                            target(pl.ds(8 - 4 * c, 4), pl.ds({0: 0, 1: 16, -1: 8}[b], 8)),
                            (0, b, c),
                        )
                    )
        return copies

    finish(coef1)
    for f in (0, 1):

        def put(p, lanes, value):
            c1[f, 8 + p, 0:16, lanes] = value

        unpack_level1(g1c, put, f)
    view1 = lambda a, b: c1.at[:, a, b]
    coef1 = send_halo1(view1, view1, 5)
    half_i, half_l = iota((256, 128), 0), iota((256, 128), 1)
    to_half = jnp.where((half_i >> 1) == half_l, 0.125, 0.0).astype(F32)

    def coarsen_level1(pair):
        for k in range(4):
            total = pair(k)
            for h in (0, 1):
                work2[h, 16 * k : 16 * k + 16, :] = total[:, 128 * h : 128 * h + 128]
        halves = [work2[h, pl.ds(0, 32, stride=2), :] + work2[h, pl.ds(1, 32, stride=2), :] for h in (0, 1)]
        return dot(jnp.concatenate(halves, axis=1), to_half)

    for f in (0, 1):
        coarse = coarsen_level1(lambda k: c1[f, 8 + 2 * k, 0:16] + c1[f, 9 + 2 * k, 0:16])
        for k in range(4):
            c2[f, 8 + k, 0:8] = coarse[8 * k : 8 * k + 8]
    view2 = lambda a, b: c2.at[:, a, b]
    coef2 = send_halo2(view2, view2, (0, 1, -1, 2, -2))

    third_lane = lane_i - jnp.where(gz >= sizes[2] // 2, 64, 0)
    to_third = jnp.where(((row_i >> 1) == third_lane) & (third_lane >= 0) & (third_lane < 64), 0.125, 0.0)
    to_third = to_third.astype(F32)

    def coarsen_level2(pair):
        for k in range(2):
            work[8 * k : 8 * k + 8, :] = pair(k)
        return dot(rows_summed(16), to_third)

    def gather_gz(piece, slots):
        slots[gz] = piece[...]
        return [send(piece, slots.at[gz], (0, 0, i)) for i in far_first(sizes[2])]

    def gather_gy(slots, packed, target, fields):
        for f in range(fields):
            for k in range(8):
                packed[f, k] = slots[k, f] + slots[k + 8, f]
        target[gy] = packed[...]
        return [send(packed, target.at[gy], (0, i, 0)) for i in far_first(sizes[1])]

    for f in (0, 1):
        p3c[f] = coarsen_level2(lambda k: c2[f, 8 + 2 * k, 0:8] + c2[f, 9 + 2 * k, 0:8])
    coef3 = gather_gz(p3c, z3c)

    finish(halo0)
    fill_coefficients0()

    bd0_at = lambda p: bdw0[0, p]
    wd0_at = lambda p: bdw0[1, p]
    no_edges = (None,) * 4
    first_half(v0.at[0], bd0_at, 0, 24, B0)
    half_sweep(v0.at[0], bd0_at, wd0_at, 1, 23, 1, no_edges, B0)
    half_sweep(v0.at[0], bd0_at, wd0_at, 2, 22, 0, no_edges, B0)
    half_sweep(v0.at[0], bd0_at, wd0_at, 3, 21, 1, no_edges, B0)

    def residual0(k, carry):
        total = None
        for p in (4 + 2 * k, 5 + 2 * k):
            c, s = neighbours(v0.at[0], p, no_edges)
            value = bdw0[0, p, 0:NY, 0:NX] - c[0:NY, 0:NX] + bdw0[1, p, 0:NY, 0:NX] * s[0:NY, 0:NX]
            value = d0[p - 4] * value
            total = value if total is None else total + value
        work[pl.ds(pl.multiple_of(32 * k, 32), 32), :] = total
        return carry

    lax.fori_loop(0, 8, residual0, 0)
    pack_level1(pk, 0)
    right1 = gather_gx(pk, g1)

    for z in range(NZ):
        value = v0[0, z + 4, 0:NY, 0:NX]
        tv[z] = jnp.where(low4, value[0:8], value[NY - 8 : NY])
        vp0[0, z + 4, 0:NY, 0:NX] = value
    ev[...] = gathered_edges(lambda z: v0[0, z + 4, 0:NY, 0:NX])

    finish(coef1)

    def row_valid(rows, own):
        tiles = [jnp.ones((8, 128), jnp.int32)] * (own // 8)
        tiles += [0 * lane + y_hi.astype(jnp.int32), 0 * lane + y_lo.astype(jnp.int32)]
        return jnp.concatenate(tiles, axis=0)

    def plane_valid(p, below, size):
        before = jnp.where(p < below, z_lo.astype(jnp.int32), 1)
        behind = jnp.where(p >= below + size, z_hi.astype(jnp.int32), 1)
        return before * behind

    def coefficients(c_at, wd_at, in_at, planes, scale, valid):
        def body(p, carry):
            weight = c_at(0, p) * scale
            diagonal = 6.0 * weight + c_at(1, p)
            ok = diagonal > 0.0
            if valid is not None:
                ok = ok & (valid(p) > 0)
            inverse = jnp.where(ok, 1.0 / jnp.where(ok, diagonal, 1.0), 0.0)
            in_at[p] = inverse
            wd_at[p] = weight * inverse
            return carry

        lax.fori_loop(planes[0], planes[1], body, 0)

    rows1 = jnp.concatenate([row_valid(32, 16)] * 2, axis=1)
    rows2 = row_valid(24, 8)

    def valid1(p):
        return rows1 * plane_valid(p, 8, 8)

    def valid2(p):
        z = gz * 4 + p - 8
        ok = jnp.where(z >= 0, 1, 0) * jnp.where(z < 4 * sizes[2], 1, 0)
        return rows2 * ok

    coefficients(lambda f, p: c1[f, p], wd1, in1, (3, 21), 0.25, valid1)

    finish(right1)

    def put_right(p, lanes, value):
        r1[8 + p, 0:16, lanes] = value

    unpack_level1(g1, put_right, 0)
    view_r1 = lambda a, b: r1.at[a, b]
    right1 = send_halo1(view_r1, view_r1, 5)
    halo_v0 = send_halo0(
        v0,
        vp0,
        lambda b, planes: tv.at[planes],
        lambda rows: ev.at[rows],
        lambda rows: ev.at[rows],
        syv,
        sxmv,
        sxcv,
    )

    finish(coef2)
    coefficients(lambda f, p: c2[f, p], wd2, in2, (2, 18), 0.0625, valid2)

    finish(right1)

    def scaled(target, right, inverse, start, stop):
        def body(p, carry):
            target[p] = right[p] * inverse[p]
            return carry

        lax.fori_loop(start, stop, body, 0)

    scaled(bd1, r1, in1, 3, 21)
    lanes1 = jnp.concatenate([lane, lane + 128], axis=1)
    lanes1 = jnp.concatenate([lanes1] * 4, axis=0)
    edges1 = (None, None, lanes1 == 0, lanes1 == 255)
    bd1_at = lambda p: bd1[p]
    wd1_at = lambda p: wd1[p]
    first_half(v1, bd1_at, 4, 20, B1)
    half_sweep(v1, bd1_at, wd1_at, 5, 19, 1, edges1, B1)
    half_sweep(v1, bd1_at, wd1_at, 6, 18, 0, edges1, B1)
    half_sweep(v1, bd1_at, wd1_at, 7, 17, 1, edges1, B1)

    def residual1(k):
        total = None
        for p in (8 + 2 * k, 9 + 2 * k):
            c, s = neighbours(v1, p, edges1)
            diagonal = 1.5 * c1[0, p, 0:16] + c1[1, p, 0:16]
            value = diagonal * (bd1[p, 0:16] - c[0:16] + wd1[p, 0:16] * s[0:16])
            total = value if total is None else total + value
        return total

    coarse = coarsen_level1(residual1)
    for k in range(4):
        r2[8 + k, 0:8] = coarse[8 * k : 8 * k + 8]
    view_r2 = lambda a, b: r2.at[a, b]
    right2 = send_halo2(view_r2, view_r2, (0, 1, -1))
    right2_far = send_halo2(view_r2, view_r2, (2, -2))
    for k in range(8):
        vp1[8 + k, 0:16] = v1[8 + k, 0:16]
    halo_v1 = send_halo1(lambda a, b: v1.at[a, b], lambda a, b: vp1.at[a, b], 6)
    finish(coef3)
    coef3 = gather_gy(z3c, y3cs, y3c, 2)
    finish(halo_v0)
    fill_v0()

    finish(right2)
    scaled(bd2, r2, in2, 4, 16)
    lanes2 = jnp.concatenate([lane] * 3, axis=0)
    edges2 = (None, None, lanes2 == 0, lanes2 == 127)
    bd2_at = lambda p: bd2[p]
    wd2_at = lambda p: wd2[p]
    first_half(v2, bd2_at, 4, 16, B2)
    half_sweep(v2, bd2_at, wd2_at, 5, 15, 1, edges2, B2)
    half_sweep(v2, bd2_at, wd2_at, 6, 14, 0, edges2, B2)
    half_sweep(v2, bd2_at, wd2_at, 7, 13, 1, edges2, B2)

    def residual2(k):
        total = None
        for p in (8 + 2 * k, 9 + 2 * k):
            c, s = neighbours(v2, p, edges2)
            diagonal = 0.375 * c2[0, p, 0:8] + c2[1, p, 0:8]
            value = diagonal * (bd2[p, 0:8] - c[0:8] + wd2[p, 0:8] * s[0:8])
            total = value if total is None else total + value
        return total

    p3[0] = coarsen_level2(residual2)
    right3 = gather_gz(p3, z3)
    for k in range(4):
        vp2[8 + k, 0:8] = v2[8 + k, 0:8]
    halo_v2 = send_halo2(lambda a, b: v2.at[a, b], lambda a, b: vp2.at[a, b], (0, 1, -1, 2, -2))

    finish(coef3)

    def unpack_level3(slots, f, put):
        for k in range(8):
            for t in range(4):
                a, b = slots[2 * t, f, k], slots[2 * t + 1, f, k]
                put(2 * k, slice(8 * t, 8 * t + 8), jnp.where(low4, a, pltpu.roll(b, 4, 0)))
                put(2 * k + 1, slice(8 * t, 8 * t + 8), jnp.where(low4, pltpu.roll(a, 4, 0), b))

    for f in (0, 1):

        def put3(p, rows, value):
            c3[f, p, rows] = value

        unpack_level3(y3c, f, put3)
    coefficients(lambda f, p: c3[f, p], wd3, in3, (0, 16), 0.25**3, None)

    to_fourth = jnp.where(
        ((row_i >> 6) == (lane_i >> 6)) & (((row_i & 63) >> 1) == (lane_i & 63)), 0.125, 0.0
    ).astype(F32)

    def coarsen_level3(pair):
        for k in range(8):
            work[32 * k : 32 * k + 32, :] = pair(k)
        return dot(rows_summed(256), to_fourth)

    for f in (0, 1):
        coarse = coarsen_level3(lambda k: c3[f, 2 * k] + c3[f, 2 * k + 1])
        for k in range(8):
            c4[f, k] = coarse[16 * k : 16 * k + 16]
    coefficients(lambda f, p: c4[f, p], wd4, in4, (0, 8), 0.25**4, None)
    finish(right2_far)
    scaled(bd2, r2, in2, 2, 4)
    scaled(bd2, r2, in2, 16, 18)
    finish(halo_v1)

    def clean(target, valid, start, stop):
        def body(p, carry):
            target[p] = jnp.where(valid(p) > 0, target[p], 0.0)
            return carry

        lax.fori_loop(start, stop, body, 0)

    clean(vp1, valid1, 2, 22)

    finish(right3)
    right3 = gather_gy(z3, y3s, y3, 1)
    finish(halo_v2)
    clean(vp2, valid2, 0, 20)
    finish(right3)

    def put_bd3(p, rows, value):
        bd3[p, rows] = value * in3[p, rows]

    unpack_level3(y3, 0, put_bd3)

    def ends(v, planes):
        low = tiled((lane < 64).astype(jnp.int32), v.shape[1], 128) > 0
        v[0] = jnp.where(low, 0.0, pltpu.roll(v[planes], 64, 1))
        v[planes + 1] = jnp.where(low, pltpu.roll(v[1], 64, 1), 0.0)

    lanes3 = jnp.concatenate([lane & 63] * 4, axis=0)
    rows3 = iota((32, 128), 0)
    edges3 = (rows3 == 0, rows3 == 31, lanes3 == 0, lanes3 == 63)
    rows4 = iota((16, 128), 0)
    edges4 = (rows4 == 0, rows4 == 15, None, None)
    bd3_at = lambda p: bd3[p]
    wd3_at = lambda p: wd3[p]
    bd4_at = lambda p: bd4[p]
    wd4_at = lambda p: wd4[p]

    def half3(colour):
        ends(v3, 16)
        half_sweep(v3, bd3_at, wd3_at, 1, 17, colour, edges3, 16, 1)

    def half4(colour):
        ends(v4, 8)
        half_sweep(v4, bd4_at, wd4_at, 1, 9, colour, edges4, 8, 1)

    first_half(v3, bd3_at, 1, 17, 16, 1)
    half3(1)
    half3(0)
    half3(1)
    ends(v3, 16)

    def residual3(k):
        total = None
        for p in (2 * k, 2 * k + 1):
            c, s = neighbours(v3, p + 1, edges3)
            diagonal = 6.0 * 0.25**3 * c3[0, p] + c3[1, p]
            value = diagonal * (bd3[p] - c + wd3[p] * s)
            total = value if total is None else total + value
        return total

    coarse = coarsen_level3(residual3)
    for k in range(8):
        bd4[k] = coarse[16 * k : 16 * k + 16] * in4[k]
    first_half(v4, bd4_at, 1, 9, 8, 1)
    half4(1)

    def sweep4(i, carry):
        half4(0)
        half4(1)
        return carry

    lax.fori_loop(1, COARSE, sweep4, 0)

    from_fourth = jnp.where(
        ((row_i >> 6) == (lane_i >> 6)) & (((lane_i & 63) >> 1) == (row_i & 63)), 1.0, 0.0
    ).astype(F32)
    wide = jnp.concatenate([v4[1 + k] for k in range(8)], axis=0)
    wide = dot(wide, from_fourth)
    work[pl.ds(0, 128, stride=2), :] = wide
    work[pl.ds(1, 128, stride=2), :] = wide

    def add3(k, carry):
        correction = work[pl.ds(pl.multiple_of(32 * k, 32), 32), :]
        v3[1 + 2 * k] = v3[1 + 2 * k] + correction
        v3[2 + 2 * k] = v3[2 + 2 * k] + correction
        return carry

    lax.fori_loop(0, 8, add3, 0)
    half3(0)
    half3(1)
    half3(0)
    half3(1)

    from_third = jnp.where((lane_i >> 1) == (row_i & 63), 1.0, 0.0).astype(F32)
    lane_half = tiled(lane >> 6, 32, 128)
    picked = []
    for i in range(10):
        z = 2 * gz - 4 + i
        inside = jnp.where(z >= 0, 1, 0) * jnp.where(z < 32, 1, 0)
        z = jnp.clip(z, 0, 31)
        index, half = z & 15, z >> 4
        keep = jnp.where(lane_half == half, inside, 0) > 0
        picked.append(jnp.where(keep, v3[1 + index], 0.0))
    wide = dot(jnp.concatenate(picked, axis=0), from_third)
    work[pl.ds(0, 320, stride=2), :] = wide
    work[pl.ds(1, 320, stride=2), :] = wide
    own_row = pl.multiple_of(8 * gy, 8)
    next_row = pl.multiple_of(8 * jnp.minimum(gy + 1, sizes[1] - 1), 8)
    before_row = pl.multiple_of(8 * jnp.maximum(gy - 1, 0), 8)

    def add2(i, carry):
        base = pl.multiple_of(64 * i, 64)
        parts = [work[pl.ds(base + row, 8), :] for row in (own_row, next_row, before_row)]
        correction = jnp.where(rows2 > 0, jnp.concatenate(parts, axis=0), 0.0)
        vp2[2 * i] = vp2[2 * i] + correction
        vp2[2 * i + 1] = vp2[2 * i + 1] + correction
        return carry

    lax.fori_loop(0, 10, add2, 0)
    half_sweep(vp2, bd2_at, wd2_at, 2, 18, 0, edges2, B2)
    half_sweep(vp2, bd2_at, wd2_at, 3, 17, 1, edges2, B2)
    half_sweep(vp2, bd2_at, wd2_at, 4, 16, 0, edges2, B2)
    half_sweep(vp2, bd2_at, wd2_at, 5, 15, 1, edges2, B2)

    def spread(wide, rows):
        for h in (0, 1):
            part = wide[:, 128 * h : 128 * h + 128]
            work2[h, pl.ds(0, rows, stride=2), :] = part
            work2[h, pl.ds(1, rows, stride=2), :] = part

    def copied(base, rows):
        return jnp.concatenate([work2[h, pl.ds(base, rows), :] for h in (0, 1)], axis=1)

    wide_i, wide_l = iota((128, 256), 0), iota((128, 256), 1)
    from_second = jnp.where((wide_l >> 1) == wide_i, 1.0, 0.0).astype(F32)
    picked = []
    for p in range(5, 15):
        picked += [vp2[p, 0:8], jnp.where(low4, vp2[p, 8:16], vp2[p, 16:24])]
    wide = dot(jnp.concatenate(picked, axis=0), from_second)
    spread(wide, 160)

    def add1(i, carry):
        correction = copied(pl.multiple_of(32 * i, 32), 32)
        vp1[2 + 2 * i] = vp1[2 + 2 * i] + correction
        vp1[3 + 2 * i] = vp1[3 + 2 * i] + correction
        return carry

    lax.fori_loop(0, 10, add1, 0)
    half_sweep(vp1, bd1_at, wd1_at, 3, 21, 0, edges1, B1)
    half_sweep(vp1, bd1_at, wd1_at, 4, 20, 1, edges1, B1)
    half_sweep(vp1, bd1_at, wd1_at, 5, 19, 0, edges1, B1)
    half_sweep(vp1, bd1_at, wd1_at, 6, 18, 1, edges1, B1)

    first_i, first_l = iota((256, 256), 0), iota((256, 256), 1)
    column = jnp.where(first_l < NX + 4, first_l, jnp.where(first_l >= 2 * NX - 4, first_l - 2 * NX, -1024))
    from_first = jnp.where(((gx * NX + column) >> 1) == first_i, 1.0, 0.0).astype(F32)
    tile_low2 = jnp.concatenate([sub, sub], axis=1) < 2
    picked = []
    for p in range(6, 18):
        picked += [vp1[p, 0:16], jnp.where(tile_low2, vp1[p, 16:24], pltpu.roll(vp1[p, 24:32], 4, 0))]
    wide = dot(jnp.concatenate(picked, axis=0), from_first)
    spread(wide, 288)

    def add0(i, carry):
        correction = copied(pl.multiple_of(48 * i, 16), 40)
        vp0[0, 2 * i] = vp0[0, 2 * i] + correction
        vp0[0, 2 * i + 1] = vp0[0, 2 * i + 1] + correction
        return carry

    lax.fori_loop(0, 12, add0, 0)
    half_sweep(vp0.at[0], bd0_at, wd0_at, 1, 23, 0, no_edges, B0)
    half_sweep(vp0.at[0], bd0_at, wd0_at, 2, 22, 1, no_edges, B0)
    half_sweep(vp0.at[0], bd0_at, wd0_at, 3, 21, 0, no_edges, B0)
    par = parity_of(NY, NX)

    def last(first, odd, size):
        before, c = vp0[0, first - 1], vp0[0, first]
        for i in range(size):
            p = first + i
            behind = vp0[0, p + 1]
            s = neighbour_sum(before, c, behind, no_edges)
            new = bdw0[0, p, 0:NY, 0:NX] + bdw0[1, p, 0:NY, 0:NX] * s[0:NY, 0:NX]
            out[p - 4] = jnp.where(par == ((odd + i + 1) & 1), new, c[0:NY, 0:NX])
            before, c = c, behind

    blocks(4, 20, B0, last)


def local(sizes, source, labels):
    vmem = lambda *shape: pltpu.VMEM(shape, F32)
    scratch = [
        vmem(16, 32, 128),
        pltpu.VMEM((16, 32, 128), jnp.int32),
        pltpu.SemaphoreType.DMA((2,)),
        vmem(2, 24, 40, 256),
        vmem(1, 24, 40, 256),
        vmem(1, 24, 40, 256),
        vmem(16, 32, 128),
        vmem(2, 16, 8, 128),
        vmem(3, 40, 128),
        vmem(16, 8, 128),
        vmem(40, 128),
        vmem(2, 24, 8, 128),
        vmem(2, 24, 8, 128),
        vmem(2, 32, 128),
        vmem(2, 2, 32, 128),
        vmem(2, 32, 128),
        vmem(2, 2, 8, 128),
        vmem(2, 2, 2, 8, 128),
        vmem(2, 2, 8, 128),
        *[vmem(2, 32, 128)] * 3,
        *[vmem(2, 2, 8, 128)] * 3,
        vmem(1, 64, 128),
        vmem(2, 64, 128),
        vmem(sizes[0], 1, 64, 128),
        vmem(sizes[0], 2, 64, 128),
        vmem(2, 24, 32, 256),
        vmem(24, 32, 256),
        vmem(24, 32, 256),
        vmem(24, 32, 256),
        vmem(24, 32, 256),
        vmem(24, 32, 256),
        vmem(24, 32, 256),
        vmem(2, 20, 24, 128),
        vmem(20, 24, 128),
        vmem(20, 24, 128),
        vmem(20, 24, 128),
        vmem(20, 24, 128),
        vmem(20, 24, 128),
        vmem(20, 24, 128),
        vmem(sizes[2], 1, 8, 128),
        vmem(sizes[2], 2, 8, 128),
        vmem(1, 8, 8, 128),
        vmem(2, 8, 8, 128),
        vmem(sizes[1], 1, 8, 8, 128),
        vmem(sizes[1], 2, 8, 8, 128),
        vmem(1, 8, 128),
        vmem(2, 8, 128),
        vmem(2, 16, 32, 128),
        vmem(18, 32, 128),
        vmem(16, 32, 128),
        vmem(16, 32, 128),
        vmem(16, 32, 128),
        vmem(2, 8, 16, 128),
        vmem(10, 16, 128),
        vmem(8, 16, 128),
        vmem(8, 16, 128),
        vmem(8, 16, 128),
        vmem(640, 128),
        vmem(2, 576, 128),
        pltpu.SemaphoreType.DMA((COPIES,)),
        pltpu.SemaphoreType.DMA((COPIES,)),
    ]
    return pl.pallas_call(
        functools.partial(kernel, sizes),
        out_shape=jax.ShapeDtypeStruct(source.shape, F32),
        in_specs=[pl.BlockSpec(memory_space=pltpu.HBM)] * 2,
        out_specs=pl.BlockSpec(memory_space=pltpu.VMEM),
        scratch_shapes=scratch,
        compiler_params=pltpu.CompilerParams(
            collective_id=0, has_side_effects=True, vmem_limit_bytes=48 * 2**20
        ),
        name="v_cycle",
    )(source, labels)


def solution(mesh):
    sizes = tuple(mesh.shape[name] for name in ("gx", "gy", "gz"))
    return jax.shard_map(
        functools.partial(local, sizes),
        mesh=mesh,
        in_specs=(P("gz", "gy", "gx"), P("gz", "gy", "gx")),
        out_specs=P("gz", "gy", "gx"),
        check_vma=False,
    )
```

```python
import functools

import jax
import jax.numpy as jnp
import numpy as np
from jax import lax
from jax.experimental import pallas as pl
from jax.experimental.pallas import tpu as pltpu
from jax.sharding import PartitionSpec as P

COARSE = 6
SOLUTE_PERMITTIVITY = 0.1
SOLVENT_SCREENING = 0.004

MESH = pl.DeviceIdType.MESH
HIGHEST = lax.Precision.HIGHEST
F32 = jnp.float32
COPIES = 128

B0, B1, B2 = 8, 10, 16

NZ, NY, NX = 16, 32, 128


def iota(shape, dim):
    return lax.broadcasted_iota(jnp.int32, shape, dim)


def tiled(tile, rows, lanes):
    tile = jnp.concatenate([tile] * (rows // 8), axis=0)
    return jnp.concatenate([tile] * (lanes // 128), axis=1)


def dot(a, b):
    return jnp.dot(a, b, precision=HIGHEST, preferred_element_type=F32)


def neighbour_sum(before, c, behind, edges):
    rows, lanes = c.shape
    below, above, left, right = edges
    s = before + behind
    shifted = pltpu.roll(c, 1, 0)
    s = s + (shifted if below is None else jnp.where(below, 0.0, shifted))
    shifted = pltpu.roll(c, rows - 1, 0)
    s = s + (shifted if above is None else jnp.where(above, 0.0, shifted))
    shifted = pltpu.roll(c, 1, 1)
    s = s + (shifted if left is None else jnp.where(left, 0.0, shifted))
    shifted = pltpu.roll(c, lanes - 1, 1)
    s = s + (shifted if right is None else jnp.where(right, 0.0, shifted))
    return s


def neighbours(v, p, edges):
    c = v[p]
    return c, neighbour_sum(v[p - 1], c, v[p + 1], edges)


def parity_of(rows, lanes):
    return tiled((iota((8, 128), 0) + iota((8, 128), 1)) & 1, rows, lanes)


def far_first(size):
    return sorted(range(1, size), key=lambda step: -min(step, size - step))


def blocks(start, stop, block, body):
    count = (stop - start) // block

    def step(i, carry):
        body(start + block * i, start & 1, block)
        return carry

    if count > 1:
        lax.fori_loop(0, count, step, 0)
    elif count == 1:
        body(start, start & 1, block)
    if start + count * block < stop:
        first = start + count * block
        body(first, first & 1, stop - first)


def half_sweep(v, bd, wd, start, stop, colour, edges, block, shift=0):
    par = parity_of(*v.shape[1:])

    def body(first, odd, size):
        before, c = v[first - 1], v[first]
        for i in range(size):
            p = first + i
            behind = v[p + 1]
            s = neighbour_sum(before, c, behind, edges)
            new = bd(p - shift) + wd(p - shift) * s
            v[p] = jnp.where(par == ((odd + i + colour + shift) & 1), new, c)
            before, c = c, behind

    blocks(start, stop, block, body)


def first_half(v, bd, start, stop, block, shift=0):
    par = parity_of(*v.shape[1:])

    def body(first, odd, size):
        for i in range(size):
            p = first + i
            v[p] = jnp.where(par == ((odd + i + shift) & 1), bd(p - shift), 0.0)

    blocks(start, stop, block, body)


def kernel(sizes, *refs):
    (source_hbm, labels_hbm, out, source, labels, isem, bdw0, v0, vp0, d0, tt, ee, tv, ev, sy, syv, sxm0, sxm1, sxm2, sxc0, sxc1, sxc2, sxv, *rest) = refs
    ( pk, pkc, g1, g1c,
     c1, r1, v1, vp1, bd1, wd1, in1, c2, r2, v2, vp2, bd2, wd2, in2, z3, z3c, y3s, y3cs, y3, y3c, p3, p3c,
     c3, v3, bd3, wd3, in3, c4, v4, bd4, wd4, in4, work, work2, token, ssem, rsem) = rest
    count = dict(gx=sizes[0], gy=sizes[1], gz=sizes[2])
    gx, gy, gz = lax.axis_index("gx"), lax.axis_index("gy"), lax.axis_index("gz")
    number = [0]

    def device(offset):
        return tuple(
            lax.rem(here + (step + size) % size, size)
            for here, step, size in zip((gx, gy, gz), offset, sizes)
        )

    def send(source_ref, target_ref, offset):
        return send_to(source_ref, target_ref, device(offset))

    def send_to(source_ref, target_ref, target):
        i = number[0]
        number[0] += 1
        copy = pltpu.make_async_remote_copy(
            src_ref=source_ref,
            dst_ref=target_ref,
            send_sem=ssem.at[i],
            recv_sem=rsem.at[i],
            device_id=target,
            device_id_type=MESH,
        )
        copy.start()
        return copy

    def finish(copies):
        for copy in copies:
            copy.wait()

    peers = set()
    for a in (-1, 0, 1):
        for b in (-1, 0, 1):
            for c in (-1, 0, 1):
                peers.add((a, b, c))
    for b in (-1, 0, 1):
        for c in (-2, 2):
            peers.add((0, b, c))
    for i in range(1, sizes[0]):
        peers.add((i, 0, 0))
    for i in range(1, sizes[1]):
        peers.add((0, i, 0))
    peers = sorted({tuple(step % size for step, size in zip(o, sizes)) for o in peers} - {(0, 0, 0)})
    barrier = pltpu.get_barrier_semaphore()
    for offset in peers:
        pl.semaphore_signal(barrier, inc=1, device_id=device(offset), device_id_type=MESH)

    def tokens(level):
        for step in (2 << level, -(2 << level)):
            pl.semaphore_signal(token.at[level], inc=1, device_id=device((0, 0, step)), device_id_type=MESH)

    def wait_tokens(level):
        pl.semaphore_wait(token.at[level], 2)

    loads = [
        pltpu.make_async_copy(labels_hbm, labels, isem.at[0]),
        pltpu.make_async_copy(source_hbm, source, isem.at[1]),
    ]
    for load in loads:
        load.start()

    lane = iota((8, 128), 1)
    sub = iota((8, 128), 0)
    low4 = sub < 4
    x_lo, x_hi = gx > 0, gx < sizes[0] - 1
    y_lo, y_hi = gy > 0, gy < sizes[1] - 1
    z_lo, z_hi = gz > 0, gz < sizes[2] - 1

    def constants(label):
        permittivity = np.array([1.0, SOLUTE_PERMITTIVITY, 1.0], np.float32)
        screening = np.array([SOLVENT_SCREENING, 0.0, 0.0], np.float32)
        diagonal = np.float32(6.0) * permittivity + screening
        inverse = np.float32(1.0) / diagonal
        choose = lambda t: jnp.where(label == 1, t[1], jnp.where(label == 0, t[0], t[2])).astype(F32)
        return choose(inverse), choose(permittivity * inverse), choose(diagonal)

    def gathered_edges(plane, rows=NY, planes=NZ):
        group = tiled(lane >> 3, rows, 128)
        total = jnp.zeros((rows, 128), F32)
        for z in range(planes):
            total = jnp.where(group == z, pltpu.roll(plane(z), (8 * z + 4) % 128, 1), total)
        return total

    def with_corners(edges):
        return jnp.concatenate([edges, jnp.where(low4, edges[0:8], edges[NY - 8 : NY])], axis=0)

    for load in loads:
        load.wait()
    for z in range(NZ):
        inverse, relative, diagonal = constants(labels[z])
        bd = source[z] * inverse
        d0[z] = diagonal
        bdw0[0, z + 4, 0:NY, 0:NX] = bd
        bdw0[1, z + 4, 0:NY, 0:NX] = relative
        tt[0, z] = jnp.where(low4, bd[0:8], pltpu.roll(relative[0:8], 4, 0))
        tt[1, z] = jnp.where(low4, pltpu.roll(relative[NY - 8 : NY], 4, 0), bd[NY - 8 : NY])
    edge_bd = with_corners(gathered_edges(lambda z: bdw0[0, z + 4, 0:NY, 0:NX]))
    edge_wd = with_corners(gathered_edges(lambda z: bdw0[1, z + 4, 0:NY, 0:NX]))
    ee[0], ee[1] = edge_bd, edge_wd
    quarter = tiled(lane >> 5, NY + 8, 128)
    inner = jnp.where(quarter == 1, pltpu.roll(edge_wd, 32, 1), pltpu.roll(edge_wd, 96, 1))
    ee[2] = jnp.where((quarter == 0) | (quarter == 3), edge_bd, inner)

    def slot(step):
        return 1 - step

    def send_halo0(own, target, t_of, same_of, other_of, y_ref, xm_ref, xc_ref):
        copies = []
        for c in (1, -1):
            first = 16 if c == 1 else 4
            copies.append(
                send(
                    own.at[:, pl.ds(first, 4), pl.ds(0, NY), pl.ds(0, NX)],
                    target.at[:, pl.ds(0 if c == 1 else 20, 4), pl.ds(0, NY), pl.ds(0, NX)],
                    (0, 0, c),
                )
            )
        for c in (1, -1, 0):
            edges = other_of if c else same_of
            to = slot(c)
            for a in (1, -1):
                side = 0 if a == 1 else 1
                for b in (1, -1):
                    copies.append(
                        send(
                            edges(pl.ds(NY, 8)),
                            xc_ref[to].at[side, 0 if b == 1 else 1],
                            (a, b, c),
                        )
                    )
            for b in (1, -1):
                side = 0 if b == 1 else 1
                first, size, start = {0: (0, 16, 4), 1: (12, 4, 0), -1: (0, 4, 20)}[c]
                copies.append(send(t_of(b, pl.ds(first, size)), y_ref.at[side, pl.ds(start, size)], (0, b, c)))
            for a in (1, -1):
                side = 0 if a == 1 else 1
                copies.append(send(edges(pl.ds(0, NY)), xm_ref[to].at[side], (a, 0, c)))
        return copies

    in_low_half = (lane & 7) >= 4

    def fill_halo0(target, f, rows_of, columns, starts):
        x_valid = jnp.where(in_low_half, x_hi.astype(jnp.int32), x_lo.astype(jnp.int32))
        y_valid = jnp.where(low4, y_hi.astype(jnp.int32), y_lo.astype(jnp.int32))
        xy_valid = x_valid * y_valid
        edge_lanes = ((lane < 4) | (lane >= 124)).astype(jnp.int32)
        lane_main = tiled(in_low_half.astype(jnp.int32), NY, 128) > 0
        for part, (first, size, z_valid) in enumerate(((0, 4, z_lo), (4, 16, None), (20, 4, z_hi))):
            ok = jnp.int32(1) if z_valid is None else z_valid.astype(jnp.int32)
            (main_right, above_right, below_right), (main_left, above_left, below_left) = columns(part)
            main = jnp.where(lane_main, main_right, main_left)
            main = jnp.where(tiled(x_valid * ok, NY, 128) > 0, main, 0.0)
            above = jnp.where(in_low_half, above_right, above_left)
            below = jnp.where(in_low_half, below_right, below_left)
            corner = jnp.where(xy_valid * ok > 0, jnp.where(low4, above, below), 0.0)
            packed = jnp.concatenate([main, corner], axis=0)
            edges = tiled(edge_lanes, NY + 8, 128) > 0
            row_ok = y_valid * ok > 0
            for i in range(size):
                p = first + i
                rolled = pltpu.roll(packed, (252 - 8 * (starts[part] + i)) % 128, 1)
                target[f, p, :, NX : 2 * NX] = jnp.where(edges, rolled, 0.0)
                target[f, p, NY : NY + 8, 0:NX] = jnp.where(row_ok, rows_of(p), 0.0)
            if z_valid is not None:

                @pl.when(jnp.logical_not(z_valid))
                def _():
                    for i in range(size):
                        target[f, first + i, 0:NY, 0:NX] = jnp.zeros((NY, NX), F32)

    def fill_coefficients0():
        for f in (0, 1):

            def rows_of(p):
                if f == 0:
                    return jnp.where(low4, sy[1, p], sy[0, p])
                return pltpu.roll(jnp.where(low4, sy[0, p], sy[1, p]), 4, 0)

            def columns(part):
                if part == 1:
                    return [(sxm1[s, f], sxc1[s, 1, f], sxc1[s, 0, f]) for s in (1, 0)]
                m, c = (sxm0, sxc0) if part == 0 else (sxm2, sxc2)
                return [(m[s], c[s, 1], c[s, 0]) for s in (1, 0)]

            fill_halo0(bdw0, f, rows_of, columns, ((12, 0, 0), (8, 0, 4))[f])

    x_side = jnp.where(in_low_half, x_hi.astype(jnp.int32), x_lo.astype(jnp.int32))
    y_side = jnp.where(low4, y_hi.astype(jnp.int32), y_lo.astype(jnp.int32))

    def fill_v0():
        right = tiled(in_low_half.astype(jnp.int32), NY + 8, 128) > 0
        valid = tiled(x_side, NY + 8, 128) > 0
        edges = tiled(((lane < 4) | (lane >= 124)).astype(jnp.int32), NY + 8, 128) > 0
        packed = [jnp.where(valid, jnp.where(right, sxv[1, j], sxv[0, j]), 0.0) for j in (0, 1)]
        for p in range(NZ + 8):
            rolled = pltpu.roll(packed[p // 16], 124 - 8 * (p % 16), 1)
            vp0[0, p, :, NX : 2 * NX] = jnp.where(edges, rolled, 0.0)
        for first, inside in ((0, z_lo), (NZ + 4, z_hi)):

            @pl.when(jnp.logical_not(inside))
            def _():
                for p in range(first, first + 4):
                    vp0[0, p] = jnp.zeros((NY + 8, 2 * NX), F32)

    row_i, lane_i = iota((128, 128), 0), iota((128, 128), 1)
    to_low = jnp.where((row_i >> 1) == lane_i, 0.125, 0.0).astype(F32)
    to_high = jnp.where((row_i >> 1) == lane_i - 64, 0.125, 0.0).astype(F32)

    def rows_summed(size):
        half = size // 2
        return work[pl.ds(0, half, stride=2), :] + work[pl.ds(1, half, stride=2), :]

    def pack_level1(target, f):
        summed = rows_summed(256)
        target[f] = dot(summed[0:64], to_low) + dot(summed[64:128], to_high)

    def gather_gx(packed, slots):
        slots[gx] = packed[...]
        return [send(packed, slots.at[gx], (i, 0, 0)) for i in far_first(sizes[0])]

    def unpack_level1(slots, target, f):
        low = tiled((lane < 64).astype(jnp.int32), 16, 128) > 0
        for pair in range(2):
            for p in range(4):
                a = slots[2 * pair, f, pl.ds(16 * p, 16)]
                b = slots[2 * pair + 1, f, pl.ds(16 * p, 16)]
                lanes = slice(128 * pair, 128 * pair + 128)
                target(p, lanes, jnp.where(low, a, pltpu.roll(b, 64, 1)))
                target(p + 4, lanes, jnp.where(low, pltpu.roll(a, 64, 1), b))

    def coefficient(f, z):
        label = labels[z]
        if f == 0:
            return jnp.where(label == 1, SOLUTE_PERMITTIVITY, 1.0).astype(F32)
        return jnp.where(label == 0, SOLVENT_SCREENING, 0.0).astype(F32)

    for f in (0, 1):
        for k in range(8):
            work[32 * k : 32 * k + 32, :] = coefficient(f, 2 * k) + coefficient(f, 2 * k + 1)
        pack_level1(pkc, f)
    pl.semaphore_wait(barrier, len(peers))
    halo0 = send_halo0(
        bdw0,
        bdw0,
        lambda b, planes: tt.at[0 if b == -1 else 1, planes],
        lambda rows: ee.at[pl.ds(0, 2), rows],
        lambda rows: ee.at[2, rows],
        sy,
        (sxm0, sxm1, sxm2),
        (sxc0, sxc1, sxc2),
    )
    coef1 = gather_gx(pkc, g1c)
    tokens(0)

    def send_halo1(own, target, width):
        copies = []
        for c in (0, 1, -1):
            planes = {0: (8, 8, 8), 1: (16 - width, width, 8 - width), -1: (8, width, 16)}[c]
            for b in (0, 1, -1):
                rows = {0: (0, 16, 0), 1: (8, 8, 24), -1: (0, 8, 16)}[b]
                if (b, c) != (0, 0):
                    copies.append(
                        send(
                            own(pl.ds(planes[0], planes[1]), pl.ds(rows[0], rows[1])),
                            target(pl.ds(planes[2], planes[1]), pl.ds(rows[2], rows[1])),
                            (0, b, c),
                        )
                    )
        return copies

    def send_z1(own, target, width):
        return [
            send(
                own(pl.ds(16 - width if c == 1 else 8, width), pl.ds(0, 16)),
                target(pl.ds(8 - width if c == 1 else 16, width), pl.ds(0, 16)),
                (0, 0, c),
            )
            for c in (1, -1)
        ]

    def send_y1(view, width):
        planes = pl.ds(8 - width, 8 + 2 * width)
        return [
            send(view(planes, pl.ds(8 if b == 1 else 0, 8)), view(planes, pl.ds(24 if b == 1 else 16, 8)), (0, b, 0))
            for b in (1, -1)
        ]

    def send_z2(own, target):
        return [
            send(own(pl.ds(8, 4), pl.ds(0, 8)), target(pl.ds(8 - 4 * c, 4), pl.ds(0, 8)), (0, 0, c))
            for c in (2, -2, 1, -1)
        ]

    def send_y2(view):
        planes = pl.ds(0, 20)
        return [
            send(view(planes, pl.ds(0, 8)), view(planes, pl.ds(16 if b == 1 else 8, 8)), (0, b, 0)) for b in (1, -1)
        ]

    def send_halo2(own, target, steps):
        copies = []
        for c in steps:
            for b in (0, 1, -1):
                if (b, c) != (0, 0):
                    copies.append(
                        send(
                            own(pl.ds(8, 4), pl.ds(0, 8)),
                            target(pl.ds(8 - 4 * c, 4), pl.ds({0: 0, 1: 16, -1: 8}[b], 8)),
                            (0, b, c),
                        )
                    )
        return copies

    finish(coef1)
    for f in (0, 1):

        def put(p, lanes, value):
            c1[f, 8 + p, 0:16, lanes] = value

        unpack_level1(g1c, put, f)
    view1 = lambda a, b: c1.at[:, a, b]
    coef1 = send_z1(view1, view1, 5)
    half_i, half_l = iota((256, 128), 0), iota((256, 128), 1)
    to_half = jnp.where((half_i >> 1) == half_l, 0.125, 0.0).astype(F32)

    def coarsen_level1(pair):
        for k in range(4):
            total = pair(k)
            for h in (0, 1):
                work2[h, 16 * k : 16 * k + 16, :] = total[:, 128 * h : 128 * h + 128]
        halves = [work2[h, pl.ds(0, 32, stride=2), :] + work2[h, pl.ds(1, 32, stride=2), :] for h in (0, 1)]
        return dot(jnp.concatenate(halves, axis=1), to_half)

    for f in (0, 1):
        coarse = coarsen_level1(lambda k: c1[f, 8 + 2 * k, 0:16] + c1[f, 9 + 2 * k, 0:16])
        for k in range(4):
            c2[f, 8 + k, 0:8] = coarse[8 * k : 8 * k + 8]

    half_gz = jnp.where(gz >= sizes[2] // 2, 64, 0)

    def to_third(offset):
        return jnp.where((row_i >> 1) == lane_i - offset, 0.125, 0.0).astype(F32)

    def coarsen_level2(pair, matrix):
        for k in range(2):
            work[8 * k : 8 * k + 8, :] = pair(k)
        return dot(rows_summed(16), matrix)

    def gather_gz(piece, slots):
        slots[gz] = piece[...]
        return [send(piece, slots.at[gz], (0, 0, i)) for i in far_first(sizes[2])]

    def gather_gy(packed, target):
        target[gy] = packed[...]
        return [send(packed, target.at[gy], (0, i, 0)) for i in far_first(sizes[1])]

    view2 = lambda a, b: c2.at[:, a, b]
    coef2 = send_z2(view2, view2)
    p3c[...] = coarsen_level2(lambda k: c2[0, 8 + 2 * k, 0:8] + c2[0, 9 + 2 * k, 0:8], to_third(0)) + coarsen_level2(
        lambda k: c2[1, 8 + 2 * k, 0:8] + c2[1, 9 + 2 * k, 0:8], to_third(64)
    )

    finish(halo0)
    wait_tokens(0)
    tokens(1)
    fill_coefficients0()

    bd0_at = lambda p: bdw0[0, p]
    wd0_at = lambda p: bdw0[1, p]
    no_edges = (None,) * 4
    first_half(v0.at[0], bd0_at, 0, 24, B0)
    half_sweep(v0.at[0], bd0_at, wd0_at, 1, 23, 1, no_edges, B0)
    half_sweep(v0.at[0], bd0_at, wd0_at, 2, 22, 0, no_edges, B0)
    half_sweep(v0.at[0], bd0_at, wd0_at, 3, 21, 1, no_edges, B0)

    def residual0(k, carry):
        total = None
        for p in (4 + 2 * k, 5 + 2 * k):
            c, s = neighbours(v0.at[0], p, no_edges)
            value = bdw0[0, p, 0:NY, 0:NX] - c[0:NY, 0:NX] + bdw0[1, p, 0:NY, 0:NX] * s[0:NY, 0:NX]
            value = d0[p - 4] * value
            total = value if total is None else total + value
        work[pl.ds(32 * k, 32), :] = total
        return carry

    for k in range(8):
        residual0(k, 0)
    pack_level1(pk, 0)
    right1 = gather_gx(pk, g1)

    view_v0 = lambda ref, first: ref.at[0, pl.ds(first, 4), pl.ds(0, NY), pl.ds(0, NX)]
    halo_v0 = [
        send(view_v0(v0, 16), view_v0(vp0, 0), (0, 0, 1)),
        send(view_v0(v0, 4), view_v0(vp0, 20), (0, 0, -1)),
    ]
    finish(coef1)
    coef1 = send_y1(view1, 5)
    finish(coef2)
    coef2 = send_y2(view2)
    wait_tokens(1)
    coef3 = gather_gz(p3c, z3c)
    for z in range(NZ):
        vp0[0, z + 4, 0:NY, 0:NX] = v0[0, z + 4, 0:NY, 0:NX]


    def row_valid(rows, own):
        tiles = [jnp.ones((8, 128), jnp.int32)] * (own // 8)
        tiles += [0 * lane + y_hi.astype(jnp.int32), 0 * lane + y_lo.astype(jnp.int32)]
        return jnp.concatenate(tiles, axis=0)

    def plane_valid(p, below, size):
        before = jnp.where(p < below, z_lo.astype(jnp.int32), 1)
        behind = jnp.where(p >= below + size, z_hi.astype(jnp.int32), 1)
        return before * behind

    def coefficients(c_at, wd_at, in_at, planes, scale, valid):
        def body(p, carry):
            weight = c_at(0, p) * scale
            diagonal = 6.0 * weight + c_at(1, p)
            ok = diagonal > 0.0
            if valid is not None:
                ok = ok & (valid(p) > 0)
            inverse = jnp.where(ok, 1.0 / jnp.where(ok, diagonal, 1.0), 0.0)
            in_at[p] = inverse
            wd_at[p] = weight * inverse
            return carry

        for p in range(*planes):
            body(p, 0)

    rows1 = jnp.concatenate([row_valid(32, 16)] * 2, axis=1)
    rows2 = row_valid(24, 8)

    def valid1(p):
        return rows1 * plane_valid(p, 8, 8)

    def valid2(p):
        z = gz * 4 + p - 8
        ok = jnp.where(z >= 0, 1, 0) * jnp.where(z < 4 * sizes[2], 1, 0)
        return rows2 * ok

    finish(right1)

    def put_right(p, lanes, value):
        r1[8 + p, 0:16, lanes] = value

    unpack_level1(g1, put_right, 0)
    view_r1 = lambda a, b: r1.at[a, b]
    right1 = send_halo1(view_r1, view_r1, 5)

    finish(halo_v0)
    for z in range(NZ + 8):
        tv[z] = jnp.where(low4, vp0[0, z, 0:8, 0:NX], vp0[0, z, NY - 8 : NY, 0:NX])
    halo_v0 = [send(tv, syv.at[0 if b == 1 else 1], (0, b, 0)) for b in (1, -1)]
    finish(coef1)
    coefficients(lambda f, p: c1[f, p], wd1, in1, (3, 21), 0.25, valid1)
    finish(coef2)
    coefficients(lambda f, p: c2[f, p], wd2, in2, (2, 18), 0.0625, valid2)

    finish(right1)

    def scaled(target, right, inverse, start, stop):
        def body(p, carry):
            target[p] = right[p] * inverse[p]
            return carry

        for p in range(start, stop):
            body(p, 0)

    scaled(bd1, r1, in1, 3, 21)
    lanes1 = jnp.concatenate([lane, lane + 128], axis=1)
    lanes1 = jnp.concatenate([lanes1] * 4, axis=0)
    edges1 = (None, None, lanes1 == 0, lanes1 == 255)
    bd1_at = lambda p: bd1[p]
    wd1_at = lambda p: wd1[p]
    first_half(v1, bd1_at, 4, 20, B1)
    half_sweep(v1, bd1_at, wd1_at, 5, 19, 1, edges1, B1)
    half_sweep(v1, bd1_at, wd1_at, 6, 18, 0, edges1, B1)
    half_sweep(v1, bd1_at, wd1_at, 7, 17, 1, edges1, B1)

    def residual1(k):
        total = None
        for p in (8 + 2 * k, 9 + 2 * k):
            c, s = neighbours(v1, p, edges1)
            diagonal = 1.5 * c1[0, p, 0:16] + c1[1, p, 0:16]
            value = diagonal * (bd1[p, 0:16] - c[0:16] + wd1[p, 0:16] * s[0:16])
            total = value if total is None else total + value
        return total

    to_third_own = jnp.where((lane_i - half_gz >= 0) & (lane_i - half_gz < 64), to_third(half_gz), 0.0)
    coarse = coarsen_level1(residual1)
    for k in range(4):
        r2[8 + k, 0:8] = coarse[8 * k : 8 * k + 8]
    view_r2 = lambda a, b: r2.at[a, b]
    right2 = send_halo2(view_r2, view_r2, (0, 1, -1))
    right2_far = send_halo2(view_r2, view_r2, (2, -2))
    for k in range(8):
        vp1[8 + k, 0:16] = v1[8 + k, 0:16]
    halo_v1 = send_z1(lambda a, b: v1.at[a, b], lambda a, b: vp1.at[a, b], 6)
    finish(coef3)
    low8 = lane < 64
    for k in range(8):
        a, b = z3c[k], z3c[k + 8]
        y3cs[0, k] = jnp.where(low8, a, pltpu.roll(b, 64, 1))
        y3cs[1, k] = jnp.where(low8, pltpu.roll(a, 64, 1), b)
    coef3 = gather_gy(y3cs, y3c)
    finish(halo_v0)
    for p in range(NZ + 8):
        rows = jnp.where(low4, syv[1, p], syv[0, p])
        vp0[0, p, NY : NY + 8, 0:NX] = jnp.where(y_side > 0, rows, 0.0)
    ev[0] = gathered_edges(lambda z: vp0[0, z, :, 0:NX], NY + 8, 16)
    ev[1] = gathered_edges(lambda z: vp0[0, z + 16, :, 0:NX], NY + 8, 8)
    halo_v0 = [send(ev, sxv.at[0 if a == 1 else 1], (a, 0, 0)) for a in (1, -1)]

    finish(right2)
    scaled(bd2, r2, in2, 4, 16)
    lanes2 = jnp.concatenate([lane] * 3, axis=0)
    edges2 = (None, None, lanes2 == 0, lanes2 == 127)
    bd2_at = lambda p: bd2[p]
    wd2_at = lambda p: wd2[p]
    first_half(v2, bd2_at, 4, 16, B2)
    half_sweep(v2, bd2_at, wd2_at, 5, 15, 1, edges2, B2)
    half_sweep(v2, bd2_at, wd2_at, 6, 14, 0, edges2, B2)
    half_sweep(v2, bd2_at, wd2_at, 7, 13, 1, edges2, B2)

    def residual2(k):
        total = None
        for p in (8 + 2 * k, 9 + 2 * k):
            c, s = neighbours(v2, p, edges2)
            diagonal = 0.375 * c2[0, p, 0:8] + c2[1, p, 0:8]
            value = diagonal * (bd2[p, 0:8] - c[0:8] + wd2[p, 0:8] * s[0:8])
            total = value if total is None else total + value
        return total

    p3[...] = coarsen_level2(residual2, to_third_own)
    right3 = gather_gz(p3, z3)
    for k in range(4):
        vp2[8 + k, 0:8] = v2[8 + k, 0:8]
    halo_v2 = send_z2(lambda a, b: v2.at[a, b], lambda a, b: vp2.at[a, b])
    finish(halo_v1)
    halo_v1 = send_y1(lambda a, b: vp1.at[a, b], 6)

    finish(coef3)

    def unpack_level3(slots, f, put):
        for k in range(8):
            for t in range(4):
                a, b = slots[2 * t, f, k], slots[2 * t + 1, f, k]
                put(2 * k, slice(8 * t, 8 * t + 8), jnp.where(low4, a, pltpu.roll(b, 4, 0)))
                put(2 * k + 1, slice(8 * t, 8 * t + 8), jnp.where(low4, pltpu.roll(a, 4, 0), b))

    for f in (0, 1):

        def put3(p, rows, value):
            c3[f, p, rows] = value

        unpack_level3(y3c, f, put3)
    coefficients(lambda f, p: c3[f, p], wd3, in3, (0, 16), 0.25**3, None)

    to_fourth = jnp.where(
        ((row_i >> 6) == (lane_i >> 6)) & (((row_i & 63) >> 1) == (lane_i & 63)), 0.125, 0.0
    ).astype(F32)

    def coarsen_level3(pair):
        for k in range(8):
            work[32 * k : 32 * k + 32, :] = pair(k)
        return dot(rows_summed(256), to_fourth)

    for f in (0, 1):
        coarse = coarsen_level3(lambda k: c3[f, 2 * k] + c3[f, 2 * k + 1])
        for k in range(8):
            c4[f, k] = coarse[16 * k : 16 * k + 16]
    coefficients(lambda f, p: c4[f, p], wd4, in4, (0, 8), 0.25**4, None)
    finish(right2_far)
    scaled(bd2, r2, in2, 2, 4)
    scaled(bd2, r2, in2, 16, 18)

    def clean(target, valid, start, stop):
        def body(p, carry):
            target[p] = jnp.where(valid(p) > 0, target[p], 0.0)
            return carry

        for p in range(start, stop):
            body(p, 0)

    finish(halo_v0)
    fill_v0()
    finish(halo_v2)
    halo_v2 = send_y2(lambda a, b: vp2.at[a, b])
    finish(halo_v1)
    clean(vp1, valid1, 2, 22)

    finish(right3)
    for k in range(8):
        y3s[0, k] = z3[k] + z3[k + 8]
    right3 = gather_gy(y3s, y3)
    finish(halo_v2)
    clean(vp2, valid2, 0, 20)
    finish(right3)

    def put_bd3(p, rows, value):
        bd3[p, rows] = value * in3[p, rows]

    unpack_level3(y3, 0, put_bd3)

    def ends(v, planes):
        low = tiled((lane < 64).astype(jnp.int32), v.shape[1], 128) > 0
        v[0] = jnp.where(low, 0.0, pltpu.roll(v[planes], 64, 1))
        v[planes + 1] = jnp.where(low, pltpu.roll(v[1], 64, 1), 0.0)

    lanes3 = jnp.concatenate([lane & 63] * 4, axis=0)
    rows3 = iota((32, 128), 0)
    edges3 = (rows3 == 0, rows3 == 31, lanes3 == 0, lanes3 == 63)
    rows4 = iota((16, 128), 0)
    edges4 = (rows4 == 0, rows4 == 15, None, None)
    bd3_at = lambda p: bd3[p]
    wd3_at = lambda p: wd3[p]
    bd4_at = lambda p: bd4[p]
    wd4_at = lambda p: wd4[p]

    def half3(colour):
        ends(v3, 16)
        half_sweep(v3, bd3_at, wd3_at, 1, 17, colour, edges3, 16, 1)

    def half4(colour):
        ends(v4, 8)
        half_sweep(v4, bd4_at, wd4_at, 1, 9, colour, edges4, 8, 1)

    first_half(v3, bd3_at, 1, 17, 16, 1)
    half3(1)
    half3(0)
    half3(1)
    ends(v3, 16)

    def residual3(k):
        total = None
        for p in (2 * k, 2 * k + 1):
            c, s = neighbours(v3, p + 1, edges3)
            diagonal = 6.0 * 0.25**3 * c3[0, p] + c3[1, p]
            value = diagonal * (bd3[p] - c + wd3[p] * s)
            total = value if total is None else total + value
        return total

    coarse = coarsen_level3(residual3)
    for k in range(8):
        bd4[k] = coarse[16 * k : 16 * k + 16] * in4[k]
    first_half(v4, bd4_at, 1, 9, 8, 1)
    half4(1)

    def sweep4(i, carry):
        half4(0)
        half4(1)
        return carry

    lax.fori_loop(1, COARSE, sweep4, 0)

    from_fourth = jnp.where(
        ((row_i >> 6) == (lane_i >> 6)) & (((lane_i & 63) >> 1) == (row_i & 63)), 1.0, 0.0
    ).astype(F32)
    wide = jnp.concatenate([v4[1 + k] for k in range(8)], axis=0)
    wide = dot(wide, from_fourth)
    work[pl.ds(0, 128, stride=2), :] = wide
    work[pl.ds(1, 128, stride=2), :] = wide

    def add3(k, carry):
        correction = work[pl.ds(32 * k, 32), :]
        v3[1 + 2 * k] = v3[1 + 2 * k] + correction
        v3[2 + 2 * k] = v3[2 + 2 * k] + correction
        return carry

    for i in range(8):
        add3(i, 0)
    half3(0)
    half3(1)
    half3(0)
    half3(1)

    from_third = jnp.where((lane_i >> 1) == (row_i & 63), 1.0, 0.0).astype(F32)
    lane_half = tiled(lane >> 6, 32, 128)
    picked = []
    for i in range(10):
        z = 2 * gz - 4 + i
        inside = jnp.where(z >= 0, 1, 0) * jnp.where(z < 32, 1, 0)
        z = jnp.clip(z, 0, 31)
        index, half = z & 15, z >> 4
        keep = jnp.where(lane_half == half, inside, 0) > 0
        picked.append(jnp.where(keep, v3[1 + index], 0.0))
    wide = dot(jnp.concatenate(picked, axis=0), from_third)
    work[pl.ds(0, 320, stride=2), :] = wide
    work[pl.ds(1, 320, stride=2), :] = wide
    own_row = pl.multiple_of(8 * gy, 8)
    next_row = pl.multiple_of(8 * jnp.minimum(gy + 1, sizes[1] - 1), 8)
    before_row = pl.multiple_of(8 * jnp.maximum(gy - 1, 0), 8)

    def add2(i, carry):
        parts = [work[pl.ds(64 * i + row, 8), :] for row in (own_row, next_row, before_row)]
        correction = jnp.where(rows2 > 0, jnp.concatenate(parts, axis=0), 0.0)
        vp2[2 * i] = vp2[2 * i] + correction
        vp2[2 * i + 1] = vp2[2 * i + 1] + correction
        return carry

    for i in range(10):
        add2(i, 0)
    half_sweep(vp2, bd2_at, wd2_at, 2, 18, 0, edges2, B2)
    half_sweep(vp2, bd2_at, wd2_at, 3, 17, 1, edges2, B2)
    half_sweep(vp2, bd2_at, wd2_at, 4, 16, 0, edges2, B2)
    half_sweep(vp2, bd2_at, wd2_at, 5, 15, 1, edges2, B2)

    def spread(wide, rows):
        for h in (0, 1):
            part = wide[:, 128 * h : 128 * h + 128]
            work2[h, pl.ds(0, rows, stride=2), :] = part
            work2[h, pl.ds(1, rows, stride=2), :] = part

    def copied(base, rows):
        return jnp.concatenate([work2[h, pl.ds(base, rows), :] for h in (0, 1)], axis=1)

    wide_i, wide_l = iota((128, 256), 0), iota((128, 256), 1)
    from_second = jnp.where((wide_l >> 1) == wide_i, 1.0, 0.0).astype(F32)
    picked = []
    for p in range(5, 15):
        picked += [vp2[p, 0:8], jnp.where(low4, vp2[p, 8:16], vp2[p, 16:24])]
    wide = dot(jnp.concatenate(picked, axis=0), from_second)
    spread(wide, 160)

    def add1(i, carry):
        correction = copied(32 * i, 32)
        vp1[2 + 2 * i] = vp1[2 + 2 * i] + correction
        vp1[3 + 2 * i] = vp1[3 + 2 * i] + correction
        return carry

    for i in range(10):
        add1(i, 0)
    half_sweep(vp1, bd1_at, wd1_at, 3, 21, 0, edges1, B1)
    half_sweep(vp1, bd1_at, wd1_at, 4, 20, 1, edges1, B1)
    half_sweep(vp1, bd1_at, wd1_at, 5, 19, 0, edges1, B1)
    half_sweep(vp1, bd1_at, wd1_at, 6, 18, 1, edges1, B1)

    first_i, first_l = iota((256, 256), 0), iota((256, 256), 1)
    column = jnp.where(first_l < NX + 4, first_l, jnp.where(first_l >= 2 * NX - 4, first_l - 2 * NX, -1024))
    from_first = jnp.where(((gx * NX + column) >> 1) == first_i, 1.0, 0.0).astype(F32)
    tile_low2 = jnp.concatenate([sub, sub], axis=1) < 2
    picked = []
    for p in range(6, 18):
        picked += [vp1[p, 0:16], jnp.where(tile_low2, vp1[p, 16:24], pltpu.roll(vp1[p, 24:32], 4, 0))]
    wide = dot(jnp.concatenate(picked, axis=0), from_first)
    spread(wide, 288)

    def add0(i, carry):
        correction = copied(48 * i, 40)
        vp0[0, 2 * i] = vp0[0, 2 * i] + correction
        vp0[0, 2 * i + 1] = vp0[0, 2 * i + 1] + correction
        return carry

    for i in range(12):
        add0(i, 0)
    half_sweep(vp0.at[0], bd0_at, wd0_at, 1, 23, 0, no_edges, B0)
    half_sweep(vp0.at[0], bd0_at, wd0_at, 2, 22, 1, no_edges, B0)
    half_sweep(vp0.at[0], bd0_at, wd0_at, 3, 21, 0, no_edges, B0)
    par = parity_of(NY, NX)

    def last(first, odd, size):
        before, c = vp0[0, first - 1], vp0[0, first]
        for i in range(size):
            p = first + i
            behind = vp0[0, p + 1]
            s = neighbour_sum(before, c, behind, no_edges)
            new = bdw0[0, p, 0:NY, 0:NX] + bdw0[1, p, 0:NY, 0:NX] * s[0:NY, 0:NX]
            out[p - 4] = jnp.where(par == ((odd + i + 1) & 1), new, c[0:NY, 0:NX])
            before, c = c, behind

    blocks(4, 20, B0, last)


def local(sizes, source, labels):
    vmem = lambda *shape: pltpu.VMEM(shape, F32)
    scratch = [
        vmem(16, 32, 128),
        pltpu.VMEM((16, 32, 128), jnp.int32),
        pltpu.SemaphoreType.DMA((2,)),
        vmem(2, 24, 40, 256),
        vmem(1, 24, 40, 256),
        vmem(1, 24, 40, 256),
        vmem(16, 32, 128),
        vmem(2, 16, 8, 128),
        vmem(3, 40, 128),
        vmem(24, 8, 128),
        vmem(2, 40, 128),
        vmem(2, 24, 8, 128),
        vmem(2, 24, 8, 128),
        vmem(2, 32, 128),
        vmem(2, 2, 32, 128),
        vmem(2, 32, 128),
        vmem(2, 2, 8, 128),
        vmem(2, 2, 2, 8, 128),
        vmem(2, 2, 8, 128),
        vmem(2, 2, 40, 128),
        vmem(1, 64, 128),
        vmem(2, 64, 128),
        vmem(sizes[0], 1, 64, 128),
        vmem(sizes[0], 2, 64, 128),
        vmem(2, 24, 32, 256),
        vmem(24, 32, 256),
        vmem(24, 32, 256),
        vmem(24, 32, 256),
        vmem(24, 32, 256),
        vmem(24, 32, 256),
        vmem(24, 32, 256),
        vmem(2, 20, 24, 128),
        vmem(20, 24, 128),
        vmem(20, 24, 128),
        vmem(20, 24, 128),
        vmem(20, 24, 128),
        vmem(20, 24, 128),
        vmem(20, 24, 128),
        vmem(sizes[2], 8, 128),
        vmem(sizes[2], 8, 128),
        vmem(1, 8, 8, 128),
        vmem(2, 8, 8, 128),
        vmem(sizes[1], 1, 8, 8, 128),
        vmem(sizes[1], 2, 8, 8, 128),
        vmem(8, 128),
        vmem(8, 128),
        vmem(2, 16, 32, 128),
        vmem(18, 32, 128),
        vmem(16, 32, 128),
        vmem(16, 32, 128),
        vmem(16, 32, 128),
        vmem(2, 8, 16, 128),
        vmem(10, 16, 128),
        vmem(8, 16, 128),
        vmem(8, 16, 128),
        vmem(8, 16, 128),
        vmem(640, 128),
        vmem(2, 576, 128),
        pltpu.SemaphoreType.REGULAR((2,)),
        pltpu.SemaphoreType.DMA((COPIES,)),
        pltpu.SemaphoreType.DMA((COPIES,)),
    ]
    return pl.pallas_call(
        functools.partial(kernel, sizes),
        out_shape=jax.ShapeDtypeStruct(source.shape, F32),
        in_specs=[pl.BlockSpec(memory_space=pltpu.HBM)] * 2,
        out_specs=pl.BlockSpec(memory_space=pltpu.VMEM),
        scratch_shapes=scratch,
        compiler_params=pltpu.CompilerParams(
            collective_id=0, has_side_effects=True, vmem_limit_bytes=62 * 2**20
        ),
        name="v_cycle",
    )(source, labels)


def solution(mesh):
    sizes = tuple(mesh.shape[name] for name in ("gx", "gy", "gz"))
    return jax.shard_map(
        functools.partial(local, sizes),
        mesh=mesh,
        in_specs=(P("gz", "gy", "gx"), P("gz", "gy", "gx")),
        out_specs=P("gz", "gy", "gx"),
        check_vma=False,
    )
```

```python
import functools

import jax
import jax.numpy as jnp
import numpy as np
from jax import lax
from jax.experimental import pallas as pl
from jax.experimental.pallas import tpu as pltpu
from jax.sharding import PartitionSpec as P

COARSE = 6
SOLUTE_PERMITTIVITY = 0.1
SOLVENT_SCREENING = 0.004

MESH = pl.DeviceIdType.MESH
HIGHEST = lax.Precision.HIGHEST
F32 = jnp.float32
COPIES = 128

B0, B1, B2 = 24, 24, 16

NZ, NY, NX = 16, 32, 128


def iota(shape, dim):
    return lax.broadcasted_iota(jnp.int32, shape, dim)


def tiled(tile, rows, lanes):
    tile = jnp.concatenate([tile] * (rows // 8), axis=0)
    return jnp.concatenate([tile] * (lanes // 128), axis=1)


def dot(a, b):
    return jnp.dot(a, b, precision=HIGHEST, preferred_element_type=F32)


def neighbour_sum(before, c, behind, edges):
    rows, lanes = c.shape
    below, above, left, right = edges
    s = before + behind
    shifted = pltpu.roll(c, 1, 0)
    s = s + (shifted if below is None else jnp.where(below, 0.0, shifted))
    shifted = pltpu.roll(c, rows - 1, 0)
    s = s + (shifted if above is None else jnp.where(above, 0.0, shifted))
    shifted = pltpu.roll(c, 1, 1)
    s = s + (shifted if left is None else jnp.where(left, 0.0, shifted))
    shifted = pltpu.roll(c, lanes - 1, 1)
    s = s + (shifted if right is None else jnp.where(right, 0.0, shifted))
    return s


def neighbours(v, p, edges):
    c = v[p]
    return c, neighbour_sum(v[p - 1], c, v[p + 1], edges)


def parity_of(rows, lanes):
    return tiled((iota((8, 128), 0) + iota((8, 128), 1)) & 1, rows, lanes)


def far_first(size):
    return sorted(range(1, size), key=lambda step: -min(step, size - step))


def blocks(start, stop, block, body):
    count = (stop - start) // block

    def step(i, carry):
        body(start + block * i, start & 1, block)
        return carry

    if count > 1:
        lax.fori_loop(0, count, step, 0)
    elif count == 1:
        body(start, start & 1, block)
    if start + count * block < stop:
        first = start + count * block
        body(first, first & 1, stop - first)


def half_sweep(v, bd, wd, start, stop, colour, edges, block, shift=0):
    par = parity_of(*v.shape[1:])

    def body(first, odd, size):
        before, c = v[first - 1], v[first]
        for i in range(size):
            p = first + i
            behind = v[p + 1]
            s = neighbour_sum(before, c, behind, edges)
            new = bd(p - shift) + wd(p - shift) * s
            v[p] = jnp.where(par == ((odd + i + colour + shift) & 1), new, c)
            before, c = c, behind

    blocks(start, stop, block, body)


def first_half(v, bd, start, stop, block, shift=0):
    par = parity_of(*v.shape[1:])

    def body(first, odd, size):
        for i in range(size):
            p = first + i
            v[p] = jnp.where(par == ((odd + i + shift) & 1), bd(p - shift), 0.0)

    blocks(start, stop, block, body)


def kernel(sizes, *refs):
    (source_hbm, labels_hbm, out, source, labels, isem, bdw0, v0, vp0, d0, tt, ee, tv, ev, sy, syv, sxm0, sxm1, sxm2, sxc0, sxc1, sxc2, sxv, *rest) = refs
    ( pk, pkc, g1, g1c,
     c1, r1, v1, vp1, bd1, wd1, in1, vw1, bdw1, wdw1, c2, r2, v2, vp2, bd2, wd2, in2, z3, z3c, y3s, y3cs, y3, y3c, p3, p3c,
     c3, v3, bd3, wd3, in3, c4, v4, bd4, wd4, in4, work, work2, token, ssem, rsem) = rest
    count = dict(gx=sizes[0], gy=sizes[1], gz=sizes[2])
    gx, gy, gz = lax.axis_index("gx"), lax.axis_index("gy"), lax.axis_index("gz")
    number = [0]

    def device(offset):
        return tuple(
            lax.rem(here + (step + size) % size, size)
            for here, step, size in zip((gx, gy, gz), offset, sizes)
        )

    def send(source_ref, target_ref, offset):
        return send_to(source_ref, target_ref, device(offset))

    def send_to(source_ref, target_ref, target):
        i = number[0]
        number[0] += 1
        copy = pltpu.make_async_remote_copy(
            src_ref=source_ref,
            dst_ref=target_ref,
            send_sem=ssem.at[i],
            recv_sem=rsem.at[i],
            device_id=target,
            device_id_type=MESH,
        )
        copy.start()
        return copy

    def finish(copies):
        for copy in copies:
            copy.wait()

    peers = set()
    for a in (-1, 0, 1):
        for b in (-1, 0, 1):
            for c in (-1, 0, 1):
                peers.add((a, b, c))
    for b in (-1, 0, 1):
        for c in (-2, 2):
            peers.add((0, b, c))
    for i in range(1, sizes[0]):
        peers.add((i, 0, 0))
    for i in range(1, sizes[1]):
        peers.add((0, i, 0))
    peers = sorted({tuple(step % size for step, size in zip(o, sizes)) for o in peers} - {(0, 0, 0)})
    barrier = pltpu.get_barrier_semaphore()
    for offset in peers:
        pl.semaphore_signal(barrier, inc=1, device_id=device(offset), device_id_type=MESH)

    def tokens(level):
        for step in (2 << level, -(2 << level)):
            pl.semaphore_signal(token.at[level], inc=1, device_id=device((0, 0, step)), device_id_type=MESH)

    def wait_tokens(level):
        pl.semaphore_wait(token.at[level], 2)

    loads = [
        pltpu.make_async_copy(labels_hbm, labels, isem.at[0]),
        pltpu.make_async_copy(source_hbm, source, isem.at[1]),
    ]
    for load in loads:
        load.start()

    lane = iota((8, 128), 1)
    sub = iota((8, 128), 0)
    low4 = sub < 4
    x_lo, x_hi = gx > 0, gx < sizes[0] - 1
    y_lo, y_hi = gy > 0, gy < sizes[1] - 1
    z_lo, z_hi = gz > 0, gz < sizes[2] - 1

    def constants(label):
        permittivity = np.array([1.0, SOLUTE_PERMITTIVITY, 1.0], np.float32)
        screening = np.array([SOLVENT_SCREENING, 0.0, 0.0], np.float32)
        diagonal = np.float32(6.0) * permittivity + screening
        inverse = np.float32(1.0) / diagonal
        choose = lambda t: jnp.where(label == 1, t[1], jnp.where(label == 0, t[0], t[2])).astype(F32)
        return choose(inverse), choose(permittivity * inverse), choose(diagonal)

    def gathered_edges(plane, rows=NY, planes=NZ):
        group = tiled(lane >> 3, rows, 128)
        total = jnp.zeros((rows, 128), F32)
        for z in range(planes):
            total = jnp.where(group == z, pltpu.roll(plane(z), (8 * z + 4) % 128, 1), total)
        return total

    def with_corners(edges):
        return jnp.concatenate([edges, jnp.where(low4, edges[0:8], edges[NY - 8 : NY])], axis=0)

    for load in loads:
        load.wait()
    for z in range(NZ):
        inverse, relative, diagonal = constants(labels[z])
        bd = source[z] * inverse
        d0[z] = diagonal
        bdw0[0, z + 4, 0:NY, 0:NX] = bd
        bdw0[1, z + 4, 0:NY, 0:NX] = relative
        tt[0, z] = jnp.where(low4, bd[0:8], pltpu.roll(relative[0:8], 4, 0))
        tt[1, z] = jnp.where(low4, pltpu.roll(relative[NY - 8 : NY], 4, 0), bd[NY - 8 : NY])
    edge_bd = with_corners(gathered_edges(lambda z: bdw0[0, z + 4, 0:NY, 0:NX]))
    edge_wd = with_corners(gathered_edges(lambda z: bdw0[1, z + 4, 0:NY, 0:NX]))
    ee[0], ee[1] = edge_bd, edge_wd
    quarter = tiled(lane >> 5, NY + 8, 128)
    inner = jnp.where(quarter == 1, pltpu.roll(edge_wd, 32, 1), pltpu.roll(edge_wd, 96, 1))
    ee[2] = jnp.where((quarter == 0) | (quarter == 3), edge_bd, inner)

    def slot(step):
        return 1 - step

    def send_halo0(own, target, t_of, same_of, other_of, y_ref, xm_ref, xc_ref):
        copies = []
        for c in (1, -1):
            first = 16 if c == 1 else 4
            copies.append(
                send(
                    own.at[:, pl.ds(first, 4), pl.ds(0, NY), pl.ds(0, NX)],
                    target.at[:, pl.ds(0 if c == 1 else 20, 4), pl.ds(0, NY), pl.ds(0, NX)],
                    (0, 0, c),
                )
            )
        for c in (1, -1, 0):
            edges = other_of if c else same_of
            to = slot(c)
            for a in (1, -1):
                side = 0 if a == 1 else 1
                for b in (1, -1):
                    copies.append(
                        send(
                            edges(pl.ds(NY, 8)),
                            xc_ref[to].at[side, 0 if b == 1 else 1],
                            (a, b, c),
                        )
                    )
            for b in (1, -1):
                side = 0 if b == 1 else 1
                first, size, start = {0: (0, 16, 4), 1: (12, 4, 0), -1: (0, 4, 20)}[c]
                copies.append(send(t_of(b, pl.ds(first, size)), y_ref.at[side, pl.ds(start, size)], (0, b, c)))
            for a in (1, -1):
                side = 0 if a == 1 else 1
                copies.append(send(edges(pl.ds(0, NY)), xm_ref[to].at[side], (a, 0, c)))
        return copies

    in_low_half = (lane & 7) >= 4

    def fill_halo0(target, f, rows_of, columns, starts):
        x_valid = jnp.where(in_low_half, x_hi.astype(jnp.int32), x_lo.astype(jnp.int32))
        y_valid = jnp.where(low4, y_hi.astype(jnp.int32), y_lo.astype(jnp.int32))
        xy_valid = x_valid * y_valid
        edge_lanes = ((lane < 4) | (lane >= 124)).astype(jnp.int32)
        lane_main = tiled(in_low_half.astype(jnp.int32), NY, 128) > 0
        for part, (first, size, z_valid) in enumerate(((0, 4, z_lo), (4, 16, None), (20, 4, z_hi))):
            ok = jnp.int32(1) if z_valid is None else z_valid.astype(jnp.int32)
            (main_right, above_right, below_right), (main_left, above_left, below_left) = columns(part)
            main = jnp.where(lane_main, main_right, main_left)
            main = jnp.where(tiled(x_valid * ok, NY, 128) > 0, main, 0.0)
            above = jnp.where(in_low_half, above_right, above_left)
            below = jnp.where(in_low_half, below_right, below_left)
            corner = jnp.where(xy_valid * ok > 0, jnp.where(low4, above, below), 0.0)
            packed = jnp.concatenate([main, corner], axis=0)
            edges = tiled(edge_lanes, NY + 8, 128) > 0
            row_ok = y_valid * ok > 0
            for i in range(size):
                p = first + i
                rolled = pltpu.roll(packed, (252 - 8 * (starts[part] + i)) % 128, 1)
                target[f, p, :, NX : 2 * NX] = jnp.where(edges, rolled, 0.0)
                target[f, p, NY : NY + 8, 0:NX] = jnp.where(row_ok, rows_of(p), 0.0)
            if z_valid is not None:

                @pl.when(jnp.logical_not(z_valid))
                def _():
                    for i in range(size):
                        target[f, first + i, 0:NY, 0:NX] = jnp.zeros((NY, NX), F32)

    def fill_coefficients0():
        for f in (0, 1):

            def rows_of(p):
                if f == 0:
                    return jnp.where(low4, sy[1, p], sy[0, p])
                return pltpu.roll(jnp.where(low4, sy[0, p], sy[1, p]), 4, 0)

            def columns(part):
                if part == 1:
                    return [(sxm1[s, f], sxc1[s, 1, f], sxc1[s, 0, f]) for s in (1, 0)]
                m, c = (sxm0, sxc0) if part == 0 else (sxm2, sxc2)
                return [(m[s], c[s, 1], c[s, 0]) for s in (1, 0)]

            fill_halo0(bdw0, f, rows_of, columns, ((12, 0, 0), (8, 0, 4))[f])

    x_side = jnp.where(in_low_half, x_hi.astype(jnp.int32), x_lo.astype(jnp.int32))
    y_side = jnp.where(low4, y_hi.astype(jnp.int32), y_lo.astype(jnp.int32))

    def fill_v0():
        right = tiled(in_low_half.astype(jnp.int32), NY + 8, 128) > 0
        valid = tiled(x_side, NY + 8, 128) > 0
        edges = tiled(((lane < 4) | (lane >= 124)).astype(jnp.int32), NY + 8, 128) > 0
        packed = [jnp.where(valid, jnp.where(right, sxv[1, j], sxv[0, j]), 0.0) for j in (0, 1)]
        for p in range(NZ + 8):
            rolled = pltpu.roll(packed[p // 16], 124 - 8 * (p % 16), 1)
            vp0[0, p, :, NX : 2 * NX] = jnp.where(edges, rolled, 0.0)
        for first, inside in ((0, z_lo), (NZ + 4, z_hi)):

            @pl.when(jnp.logical_not(inside))
            def _():
                for p in range(first, first + 4):
                    vp0[0, p] = jnp.zeros((NY + 8, 2 * NX), F32)

    row_i, lane_i = iota((128, 128), 0), iota((128, 128), 1)
    to_low = jnp.where((row_i >> 1) == lane_i, 0.125, 0.0).astype(F32)
    to_high = jnp.where((row_i >> 1) == lane_i - 64, 0.125, 0.0).astype(F32)

    def rows_summed(size):
        half = size // 2
        return work[pl.ds(0, half, stride=2), :] + work[pl.ds(1, half, stride=2), :]

    def pack_level1(target, f):
        summed = rows_summed(256)
        target[f] = dot(summed[0:64], to_low) + dot(summed[64:128], to_high)

    def gather_gx(packed, slots):
        slots[gx] = packed[...]
        return [send(packed, slots.at[gx], (i, 0, 0)) for i in far_first(sizes[0])]

    def unpack_level1(slots, target, f):
        low = tiled((lane < 64).astype(jnp.int32), 16, 128) > 0
        for pair in range(2):
            for p in range(4):
                a = slots[2 * pair, f, pl.ds(16 * p, 16)]
                b = slots[2 * pair + 1, f, pl.ds(16 * p, 16)]
                lanes = slice(128 * pair, 128 * pair + 128)
                target(p, lanes, jnp.where(low, a, pltpu.roll(b, 64, 1)))
                target(p + 4, lanes, jnp.where(low, pltpu.roll(a, 64, 1), b))

    def coefficient(f, z):
        label = labels[z]
        if f == 0:
            return jnp.where(label == 1, SOLUTE_PERMITTIVITY, 1.0).astype(F32)
        return jnp.where(label == 0, SOLVENT_SCREENING, 0.0).astype(F32)

    for f in (0, 1):
        for k in range(8):
            work[32 * k : 32 * k + 32, :] = coefficient(f, 2 * k) + coefficient(f, 2 * k + 1)
        pack_level1(pkc, f)
    pl.semaphore_wait(barrier, len(peers))
    halo0 = send_halo0(
        bdw0,
        bdw0,
        lambda b, planes: tt.at[0 if b == -1 else 1, planes],
        lambda rows: ee.at[pl.ds(0, 2), rows],
        lambda rows: ee.at[2, rows],
        sy,
        (sxm0, sxm1, sxm2),
        (sxc0, sxc1, sxc2),
    )
    coef1 = gather_gx(pkc, g1c)
    tokens(0)

    def send_halo1(own, target, width):
        copies = []
        for c in (0, 1, -1):
            planes = {0: (8, 8, 8), 1: (16 - width, width, 8 - width), -1: (8, width, 16)}[c]
            for b in (0, 1, -1):
                rows = {0: (0, 16, 0), 1: (8, 8, 24), -1: (0, 8, 16)}[b]
                if (b, c) != (0, 0):
                    copies.append(
                        send(
                            own(pl.ds(planes[0], planes[1]), pl.ds(rows[0], rows[1])),
                            target(pl.ds(planes[2], planes[1]), pl.ds(rows[2], rows[1])),
                            (0, b, c),
                        )
                    )
        return copies

    def send_z1(own, target, width):
        return [
            send(
                own(pl.ds(16 - width if c == 1 else 8, width), pl.ds(0, 16)),
                target(pl.ds(8 - width if c == 1 else 16, width), pl.ds(0, 16)),
                (0, 0, c),
            )
            for c in (1, -1)
        ]

    def send_y1(view, width):
        planes = pl.ds(8 - width, 8 + 2 * width)
        return [
            send(view(planes, pl.ds(8 if b == 1 else 0, 8)), view(planes, pl.ds(24 if b == 1 else 16, 8)), (0, b, 0))
            for b in (1, -1)
        ]

    def send_z2(own, target):
        return [
            send(own(pl.ds(8, 4), pl.ds(0, 8)), target(pl.ds(8 - 4 * c, 4), pl.ds(0, 8)), (0, 0, c))
            for c in (2, -2, 1, -1)
        ]

    def send_y2(view):
        planes = pl.ds(0, 20)
        return [
            send(view(planes, pl.ds(0, 8)), view(planes, pl.ds(16 if b == 1 else 8, 8)), (0, b, 0)) for b in (1, -1)
        ]

    def send_halo2(own, target, steps):
        copies = []
        for c in steps:
            for b in (0, 1, -1):
                if (b, c) != (0, 0):
                    copies.append(
                        send(
                            own(pl.ds(8, 4), pl.ds(0, 8)),
                            target(pl.ds(8 - 4 * c, 4), pl.ds({0: 0, 1: 16, -1: 8}[b], 8)),
                            (0, b, c),
                        )
                    )
        return copies

    finish(coef1)
    for f in (0, 1):

        def put(p, lanes, value):
            c1[f, 8 + p, 0:16, lanes] = value

        unpack_level1(g1c, put, f)
    view1 = lambda a, b: c1.at[:, a, b]
    coef1 = send_z1(view1, view1, 5)
    half_i, half_l = iota((256, 128), 0), iota((256, 128), 1)
    to_half = jnp.where((half_i >> 1) == half_l, 0.125, 0.0).astype(F32)

    def coarsen_level1(pair):
        for k in range(4):
            total = pair(k)
            for h in (0, 1):
                work2[h, 16 * k : 16 * k + 16, :] = total[:, 128 * h : 128 * h + 128]
        halves = [work2[h, pl.ds(0, 32, stride=2), :] + work2[h, pl.ds(1, 32, stride=2), :] for h in (0, 1)]
        return dot(jnp.concatenate(halves, axis=1), to_half)

    for f in (0, 1):
        coarse = coarsen_level1(lambda k: c1[f, 8 + 2 * k, 0:16] + c1[f, 9 + 2 * k, 0:16])
        for k in range(4):
            c2[f, 8 + k, 0:8] = coarse[8 * k : 8 * k + 8]

    half_gz = jnp.where(gz >= sizes[2] // 2, 64, 0)

    def to_third(offset):
        return jnp.where((row_i >> 1) == lane_i - offset, 0.125, 0.0).astype(F32)

    def coarsen_level2(pair, matrix):
        for k in range(2):
            work[8 * k : 8 * k + 8, :] = pair(k)
        return dot(rows_summed(16), matrix)

    def gather_gz(piece, slots):
        slots[gz] = piece[...]
        return [send(piece, slots.at[gz], (0, 0, i)) for i in far_first(sizes[2])]

    def gather_gy(packed, target):
        target[gy] = packed[...]
        return [send(packed, target.at[gy], (0, i, 0)) for i in far_first(sizes[1])]

    view2 = lambda a, b: c2.at[:, a, b]
    coef2 = send_z2(view2, view2)
    p3c[...] = coarsen_level2(lambda k: c2[0, 8 + 2 * k, 0:8] + c2[0, 9 + 2 * k, 0:8], to_third(0)) + coarsen_level2(
        lambda k: c2[1, 8 + 2 * k, 0:8] + c2[1, 9 + 2 * k, 0:8], to_third(64)
    )

    finish(halo0)
    wait_tokens(0)
    tokens(1)
    fill_coefficients0()

    bd0_at = lambda p: bdw0[0, p]
    wd0_at = lambda p: bdw0[1, p]
    no_edges = (None,) * 4
    first_half(v0.at[0], bd0_at, 0, 24, B0)
    half_sweep(v0.at[0], bd0_at, wd0_at, 1, 23, 1, no_edges, B0)
    half_sweep(v0.at[0], bd0_at, wd0_at, 2, 22, 0, no_edges, B0)
    half_sweep(v0.at[0], bd0_at, wd0_at, 3, 21, 1, no_edges, B0)

    def residual0(k, carry):
        total = None
        for p in (4 + 2 * k, 5 + 2 * k):
            c, s = neighbours(v0.at[0], p, no_edges)
            value = bdw0[0, p, 0:NY, 0:NX] - c[0:NY, 0:NX] + bdw0[1, p, 0:NY, 0:NX] * s[0:NY, 0:NX]
            value = d0[p - 4] * value
            total = value if total is None else total + value
        work[pl.ds(32 * k, 32), :] = total
        return carry

    for k in range(8):
        residual0(k, 0)
    pack_level1(pk, 0)
    right1 = gather_gx(pk, g1)

    view_v0 = lambda ref, first: ref.at[0, pl.ds(first, 4), pl.ds(0, NY), pl.ds(0, NX)]
    halo_v0 = [
        send(view_v0(v0, 16), view_v0(vp0, 0), (0, 0, 1)),
        send(view_v0(v0, 4), view_v0(vp0, 20), (0, 0, -1)),
    ]
    finish(coef1)
    coef1 = send_y1(view1, 5)
    finish(coef2)
    coef2 = send_y2(view2)
    wait_tokens(1)
    coef3 = gather_gz(p3c, z3c)
    for z in range(NZ):
        vp0[0, z + 4, 0:NY, 0:NX] = v0[0, z + 4, 0:NY, 0:NX]


    def row_valid(rows, own):
        tiles = [jnp.ones((8, 128), jnp.int32)] * (own // 8)
        tiles += [0 * lane + y_hi.astype(jnp.int32), 0 * lane + y_lo.astype(jnp.int32)]
        return jnp.concatenate(tiles, axis=0)

    def plane_valid(p, below, size):
        before = jnp.where(p < below, z_lo.astype(jnp.int32), 1)
        behind = jnp.where(p >= below + size, z_hi.astype(jnp.int32), 1)
        return before * behind

    def coefficients(c_at, wd_at, in_at, planes, scale, valid):
        def body(p, carry):
            weight = c_at(0, p) * scale
            diagonal = 6.0 * weight + c_at(1, p)
            ok = diagonal > 0.0
            if valid is not None:
                ok = ok & (valid(p) > 0)
            inverse = jnp.where(ok, 1.0 / jnp.where(ok, diagonal, 1.0), 0.0)
            in_at[p] = inverse
            wd_at[p] = weight * inverse
            return carry

        for p in range(*planes):
            body(p, 0)

    rows1 = jnp.concatenate([row_valid(32, 16)] * 2, axis=1)
    rows2 = row_valid(24, 8)

    def valid1(p):
        return rows1 * plane_valid(p, 8, 8)

    def valid2(p):
        z = gz * 4 + p - 8
        ok = jnp.where(z >= 0, 1, 0) * jnp.where(z < 4 * sizes[2], 1, 0)
        return rows2 * ok

    finish(right1)

    def put_right(p, lanes, value):
        r1[8 + p, 0:16, lanes] = value

    unpack_level1(g1, put_right, 0)
    view_r1 = lambda a, b: r1.at[a, b]
    right1 = send_halo1(view_r1, view_r1, 5)

    finish(halo_v0)
    for z in range(NZ + 8):
        tv[z] = jnp.where(low4, vp0[0, z, 0:8, 0:NX], vp0[0, z, NY - 8 : NY, 0:NX])
    halo_v0 = [send(tv, syv.at[0 if b == 1 else 1], (0, b, 0)) for b in (1, -1)]
    finish(coef1)
    coefficients(lambda f, p: c1[f, p], wd1, in1, (3, 21), 0.25, valid1)
    finish(coef2)
    coefficients(lambda f, p: c2[f, p], wd2, in2, (2, 18), 0.0625, valid2)

    finish(right1)

    def scaled(target, right, inverse, start, stop):
        def body(p, carry):
            target[p] = right[p] * inverse[p]
            return carry

        for p in range(start, stop):
            body(p, 0)

    scaled(bd1, r1, in1, 3, 21)
    lanes1 = jnp.concatenate([lane, lane + 128], axis=1)
    lanes1 = jnp.concatenate([lanes1] * 4, axis=0)
    edges1 = (None, None, lanes1 == 0, lanes1 == 255)
    bd1_at = lambda p: bd1[p]
    wd1_at = lambda p: wd1[p]
    first_half(v1, bd1_at, 4, 20, B1)
    half_sweep(v1, bd1_at, wd1_at, 5, 19, 1, edges1, B1)
    half_sweep(v1, bd1_at, wd1_at, 6, 18, 0, edges1, B1)
    half_sweep(v1, bd1_at, wd1_at, 7, 17, 1, edges1, B1)

    def residual1(k):
        total = None
        for p in (8 + 2 * k, 9 + 2 * k):
            c, s = neighbours(v1, p, edges1)
            diagonal = 1.5 * c1[0, p, 0:16] + c1[1, p, 0:16]
            value = diagonal * (bd1[p, 0:16] - c[0:16] + wd1[p, 0:16] * s[0:16])
            total = value if total is None else total + value
        return total

    to_third_own = jnp.where((lane_i - half_gz >= 0) & (lane_i - half_gz < 64), to_third(half_gz), 0.0)
    coarse = coarsen_level1(residual1)
    for k in range(4):
        r2[8 + k, 0:8] = coarse[8 * k : 8 * k + 8]
    view_r2 = lambda a, b: r2.at[a, b]
    right2 = send_halo2(view_r2, view_r2, (0, 1, -1))
    right2_far = send_halo2(view_r2, view_r2, (2, -2))
    for k in range(8):
        vp1[8 + k, 0:16] = v1[8 + k, 0:16]
    halo_v1 = send_z1(lambda a, b: v1.at[a, b], lambda a, b: vp1.at[a, b], 6)
    finish(coef3)
    low8 = lane < 64
    for k in range(8):
        a, b = z3c[k], z3c[k + 8]
        y3cs[0, k] = jnp.where(low8, a, pltpu.roll(b, 64, 1))
        y3cs[1, k] = jnp.where(low8, pltpu.roll(a, 64, 1), b)
    coef3 = gather_gy(y3cs, y3c)
    finish(halo_v0)
    for p in range(NZ + 8):
        rows = jnp.where(low4, syv[1, p], syv[0, p])
        vp0[0, p, NY : NY + 8, 0:NX] = jnp.where(y_side > 0, rows, 0.0)
    ev[0] = gathered_edges(lambda z: vp0[0, z, :, 0:NX], NY + 8, 16)
    ev[1] = gathered_edges(lambda z: vp0[0, z + 16, :, 0:NX], NY + 8, 8)
    halo_v0 = [send(ev, sxv.at[0 if a == 1 else 1], (a, 0, 0)) for a in (1, -1)]

    finish(right2)
    scaled(bd2, r2, in2, 4, 16)
    lanes2 = jnp.concatenate([lane] * 3, axis=0)
    edges2 = (None, None, lanes2 == 0, lanes2 == 127)
    bd2_at = lambda p: bd2[p]
    wd2_at = lambda p: wd2[p]
    first_half(v2, bd2_at, 4, 16, B2)
    half_sweep(v2, bd2_at, wd2_at, 5, 15, 1, edges2, B2)
    half_sweep(v2, bd2_at, wd2_at, 6, 14, 0, edges2, B2)
    half_sweep(v2, bd2_at, wd2_at, 7, 13, 1, edges2, B2)

    def residual2(k):
        total = None
        for p in (8 + 2 * k, 9 + 2 * k):
            c, s = neighbours(v2, p, edges2)
            diagonal = 0.375 * c2[0, p, 0:8] + c2[1, p, 0:8]
            value = diagonal * (bd2[p, 0:8] - c[0:8] + wd2[p, 0:8] * s[0:8])
            total = value if total is None else total + value
        return total

    p3[...] = coarsen_level2(residual2, to_third_own)
    right3 = gather_gz(p3, z3)
    for k in range(4):
        vp2[8 + k, 0:8] = v2[8 + k, 0:8]
    halo_v2 = send_z2(lambda a, b: v2.at[a, b], lambda a, b: vp2.at[a, b])
    finish(halo_v1)
    halo_v1 = send_y1(lambda a, b: vp1.at[a, b], 6)

    finish(coef3)

    def unpack_level3(slots, f, put):
        for k in range(8):
            for t in range(4):
                a, b = slots[2 * t, f, k], slots[2 * t + 1, f, k]
                put(2 * k, slice(8 * t, 8 * t + 8), jnp.where(low4, a, pltpu.roll(b, 4, 0)))
                put(2 * k + 1, slice(8 * t, 8 * t + 8), jnp.where(low4, pltpu.roll(a, 4, 0), b))

    for f in (0, 1):

        def put3(p, rows, value):
            c3[f, p, rows] = value

        unpack_level3(y3c, f, put3)
    coefficients(lambda f, p: c3[f, p], wd3, in3, (0, 16), 0.25**3, None)

    to_fourth = jnp.where(
        ((row_i >> 6) == (lane_i >> 6)) & (((row_i & 63) >> 1) == (lane_i & 63)), 0.125, 0.0
    ).astype(F32)

    def coarsen_level3(pair):
        for k in range(8):
            work[32 * k : 32 * k + 32, :] = pair(k)
        return dot(rows_summed(256), to_fourth)

    for f in (0, 1):
        coarse = coarsen_level3(lambda k: c3[f, 2 * k] + c3[f, 2 * k + 1])
        for k in range(8):
            c4[f, k] = coarse[16 * k : 16 * k + 16]
    coefficients(lambda f, p: c4[f, p], wd4, in4, (0, 8), 0.25**4, None)
    finish(right2_far)
    scaled(bd2, r2, in2, 2, 4)
    scaled(bd2, r2, in2, 16, 18)

    def clean(target, valid, start, stop):
        def body(p, carry):
            target[p] = jnp.where(valid(p) > 0, target[p], 0.0)
            return carry

        for p in range(start, stop):
            body(p, 0)

    finish(halo_v0)
    fill_v0()
    finish(halo_v2)
    halo_v2 = send_y2(lambda a, b: vp2.at[a, b])
    finish(halo_v1)
    column1 = 64 * gx - 32 + jnp.concatenate([lane] * 4, axis=0)
    inside1 = jnp.where(column1 >= 0, 1, 0) * jnp.where(column1 < 64 * sizes[0], 1, 0)
    turn = lax.rem(32 + 64 * (sizes[0] - gx), 64 * sizes[0])

    def beside(plane, valid):
        return jnp.where(valid > 0, pltpu.roll(plane, turn, 1)[:, 0:128], 0.0)

    for p in range(2, 22):
        vw1[p] = beside(vp1[p], inside1 * valid1(p)[:, 0:128])
    for p in range(3, 21):
        bdw1[p] = beside(bd1[p], inside1)
        wdw1[p] = beside(wd1[p], inside1)

    finish(right3)
    for k in range(8):
        y3s[0, k] = z3[k] + z3[k + 8]
    right3 = gather_gy(y3s, y3)
    finish(halo_v2)
    clean(vp2, valid2, 0, 20)
    finish(right3)

    def put_bd3(p, rows, value):
        bd3[p, rows] = value * in3[p, rows]

    unpack_level3(y3, 0, put_bd3)

    def ends(v, planes):
        low = tiled((lane < 64).astype(jnp.int32), v.shape[1], 128) > 0
        v[0] = jnp.where(low, 0.0, pltpu.roll(v[planes], 64, 1))
        v[planes + 1] = jnp.where(low, pltpu.roll(v[1], 64, 1), 0.0)

    lanes3 = jnp.concatenate([lane & 63] * 4, axis=0)
    rows3 = iota((32, 128), 0)
    edges3 = (rows3 == 0, rows3 == 31, lanes3 == 0, lanes3 == 63)
    rows4 = iota((16, 128), 0)
    edges4 = (rows4 == 0, rows4 == 15, None, None)
    bd3_at = lambda p: bd3[p]
    wd3_at = lambda p: wd3[p]
    bd4_at = lambda p: bd4[p]
    wd4_at = lambda p: wd4[p]

    def half3(colour):
        ends(v3, 16)
        half_sweep(v3, bd3_at, wd3_at, 1, 17, colour, edges3, 16, 1)

    def half4(colour):
        ends(v4, 8)
        half_sweep(v4, bd4_at, wd4_at, 1, 9, colour, edges4, 8, 1)

    first_half(v3, bd3_at, 1, 17, 16, 1)
    half3(1)
    half3(0)
    half3(1)
    ends(v3, 16)

    def residual3(k):
        total = None
        for p in (2 * k, 2 * k + 1):
            c, s = neighbours(v3, p + 1, edges3)
            diagonal = 6.0 * 0.25**3 * c3[0, p] + c3[1, p]
            value = diagonal * (bd3[p] - c + wd3[p] * s)
            total = value if total is None else total + value
        return total

    coarse = coarsen_level3(residual3)
    for k in range(8):
        bd4[k] = coarse[16 * k : 16 * k + 16] * in4[k]
    first_half(v4, bd4_at, 1, 9, 8, 1)
    half4(1)

    def sweep4(i, carry):
        half4(0)
        half4(1)
        return carry

    lax.fori_loop(1, COARSE, sweep4, 0)

    from_fourth = jnp.where(
        ((row_i >> 6) == (lane_i >> 6)) & (((lane_i & 63) >> 1) == (row_i & 63)), 1.0, 0.0
    ).astype(F32)
    wide = jnp.concatenate([v4[1 + k] for k in range(8)], axis=0)
    wide = dot(wide, from_fourth)
    work[pl.ds(0, 128, stride=2), :] = wide
    work[pl.ds(1, 128, stride=2), :] = wide

    def add3(k, carry):
        correction = work[pl.ds(32 * k, 32), :]
        v3[1 + 2 * k] = v3[1 + 2 * k] + correction
        v3[2 + 2 * k] = v3[2 + 2 * k] + correction
        return carry

    for i in range(8):
        add3(i, 0)
    half3(0)
    half3(1)
    half3(0)
    half3(1)

    from_third = jnp.where((lane_i >> 1) == (row_i & 63), 1.0, 0.0).astype(F32)
    lane_half = tiled(lane >> 6, 32, 128)
    picked = []
    for i in range(10):
        z = 2 * gz - 4 + i
        inside = jnp.where(z >= 0, 1, 0) * jnp.where(z < 32, 1, 0)
        z = jnp.clip(z, 0, 31)
        index, half = z & 15, z >> 4
        keep = jnp.where(lane_half == half, inside, 0) > 0
        picked.append(jnp.where(keep, v3[1 + index], 0.0))
    wide = dot(jnp.concatenate(picked, axis=0), from_third)
    work[pl.ds(0, 320, stride=2), :] = wide
    work[pl.ds(1, 320, stride=2), :] = wide
    own_row = pl.multiple_of(8 * gy, 8)
    next_row = pl.multiple_of(8 * jnp.minimum(gy + 1, sizes[1] - 1), 8)
    before_row = pl.multiple_of(8 * jnp.maximum(gy - 1, 0), 8)

    def add2(i, carry):
        parts = [work[pl.ds(64 * i + row, 8), :] for row in (own_row, next_row, before_row)]
        correction = jnp.where(rows2 > 0, jnp.concatenate(parts, axis=0), 0.0)
        vp2[2 * i] = vp2[2 * i] + correction
        vp2[2 * i + 1] = vp2[2 * i + 1] + correction
        return carry

    for i in range(10):
        add2(i, 0)
    half_sweep(vp2, bd2_at, wd2_at, 2, 18, 0, edges2, B2)
    half_sweep(vp2, bd2_at, wd2_at, 3, 17, 1, edges2, B2)
    half_sweep(vp2, bd2_at, wd2_at, 4, 16, 0, edges2, B2)
    half_sweep(vp2, bd2_at, wd2_at, 5, 15, 1, edges2, B2)

    def copied(base, rows):
        return jnp.concatenate([work2[h, pl.ds(base, rows), :] for h in (0, 1)], axis=1)

    from_second = jnp.where(((64 * gx - 32 + lane_i) >> 1) == row_i, 1.0, 0.0).astype(F32)
    picked = []
    for p in range(5, 15):
        picked += [vp2[p, 0:8], jnp.where(low4, vp2[p, 8:16], vp2[p, 16:24])]
    wide = dot(jnp.concatenate(picked, axis=0), from_second)
    work[pl.ds(0, 160, stride=2), :] = wide
    work[pl.ds(1, 160, stride=2), :] = wide

    def add1(i, carry):
        correction = work[32 * i : 32 * i + 32, :]
        vw1[2 + 2 * i] = vw1[2 + 2 * i] + correction
        vw1[3 + 2 * i] = vw1[3 + 2 * i] + correction
        return carry

    for i in range(10):
        add1(i, 0)
    bdw1_at = lambda p: bdw1[p]
    wdw1_at = lambda p: wdw1[p]
    no_edges = (None,) * 4
    half_sweep(vw1, bdw1_at, wdw1_at, 3, 21, 0, no_edges, B1)
    half_sweep(vw1, bdw1_at, wdw1_at, 4, 20, 1, no_edges, B1)
    half_sweep(vw1, bdw1_at, wdw1_at, 5, 19, 0, no_edges, B1)
    half_sweep(vw1, bdw1_at, wdw1_at, 6, 18, 1, no_edges, B1)

    first_i, first_l = iota((128, 256), 0), iota((128, 256), 1)
    column = jnp.where(first_l < NX + 4, first_l, jnp.where(first_l >= 2 * NX - 4, first_l - 2 * NX, -1024))
    x = jnp.where(column > -1024, gx * NX + column, -1024)
    from_first = jnp.where((x >> 1) == 64 * gx - 32 + first_i, 1.0, 0.0).astype(F32)
    picked = []
    for p in range(6, 18):
        picked += [vw1[p, 0:16], jnp.where(sub < 2, vw1[p, 16:24], pltpu.roll(vw1[p, 24:32], 4, 0))]
    wide = dot(jnp.concatenate(picked, axis=0), from_first)
    for h in (0, 1):
        part = wide[:, 128 * h : 128 * h + 128]
        work2[h, pl.ds(0, 288, stride=2), :] = part
        work2[h, pl.ds(1, 288, stride=2), :] = part

    def add0(i, carry):
        correction = copied(48 * i, 40)
        vp0[0, 2 * i] = vp0[0, 2 * i] + correction
        vp0[0, 2 * i + 1] = vp0[0, 2 * i + 1] + correction
        return carry

    for i in range(12):
        add0(i, 0)
    half_sweep(vp0.at[0], bd0_at, wd0_at, 1, 23, 0, no_edges, B0)
    half_sweep(vp0.at[0], bd0_at, wd0_at, 2, 22, 1, no_edges, B0)
    half_sweep(vp0.at[0], bd0_at, wd0_at, 3, 21, 0, no_edges, B0)
    par = parity_of(NY, NX)

    def last(first, odd, size):
        before, c = vp0[0, first - 1], vp0[0, first]
        for i in range(size):
            p = first + i
            behind = vp0[0, p + 1]
            s = neighbour_sum(before, c, behind, no_edges)
            new = bdw0[0, p, 0:NY, 0:NX] + bdw0[1, p, 0:NY, 0:NX] * s[0:NY, 0:NX]
            out[p - 4] = jnp.where(par == ((odd + i + 1) & 1), new, c[0:NY, 0:NX])
            before, c = c, behind

    blocks(4, 20, B0, last)


def local(sizes, source, labels):
    vmem = lambda *shape: pltpu.VMEM(shape, F32)
    scratch = [
        vmem(16, 32, 128),
        pltpu.VMEM((16, 32, 128), jnp.int32),
        pltpu.SemaphoreType.DMA((2,)),
        vmem(2, 24, 40, 256),
        vmem(1, 24, 40, 256),
        vmem(1, 24, 40, 256),
        vmem(16, 32, 128),
        vmem(2, 16, 8, 128),
        vmem(3, 40, 128),
        vmem(24, 8, 128),
        vmem(2, 40, 128),
        vmem(2, 24, 8, 128),
        vmem(2, 24, 8, 128),
        vmem(2, 32, 128),
        vmem(2, 2, 32, 128),
        vmem(2, 32, 128),
        vmem(2, 2, 8, 128),
        vmem(2, 2, 2, 8, 128),
        vmem(2, 2, 8, 128),
        vmem(2, 2, 40, 128),
        vmem(1, 64, 128),
        vmem(2, 64, 128),
        vmem(sizes[0], 1, 64, 128),
        vmem(sizes[0], 2, 64, 128),
        vmem(2, 24, 32, 256),
        vmem(24, 32, 256),
        vmem(24, 32, 256),
        vmem(24, 32, 256),
        vmem(24, 32, 256),
        vmem(24, 32, 256),
        vmem(24, 32, 256),
        vmem(24, 32, 128),
        vmem(24, 32, 128),
        vmem(24, 32, 128),
        vmem(2, 20, 24, 128),
        vmem(20, 24, 128),
        vmem(20, 24, 128),
        vmem(20, 24, 128),
        vmem(20, 24, 128),
        vmem(20, 24, 128),
        vmem(20, 24, 128),
        vmem(sizes[2], 8, 128),
        vmem(sizes[2], 8, 128),
        vmem(1, 8, 8, 128),
        vmem(2, 8, 8, 128),
        vmem(sizes[1], 1, 8, 8, 128),
        vmem(sizes[1], 2, 8, 8, 128),
        vmem(8, 128),
        vmem(8, 128),
        vmem(2, 16, 32, 128),
        vmem(18, 32, 128),
        vmem(16, 32, 128),
        vmem(16, 32, 128),
        vmem(16, 32, 128),
        vmem(2, 8, 16, 128),
        vmem(10, 16, 128),
        vmem(8, 16, 128),
        vmem(8, 16, 128),
        vmem(8, 16, 128),
        vmem(640, 128),
        vmem(2, 576, 128),
        pltpu.SemaphoreType.REGULAR((2,)),
        pltpu.SemaphoreType.DMA((COPIES,)),
        pltpu.SemaphoreType.DMA((COPIES,)),
    ]
    return pl.pallas_call(
        functools.partial(kernel, sizes),
        out_shape=jax.ShapeDtypeStruct(source.shape, F32),
        in_specs=[pl.BlockSpec(memory_space=pltpu.HBM)] * 2,
        out_specs=pl.BlockSpec(memory_space=pltpu.VMEM),
        scratch_shapes=scratch,
        compiler_params=pltpu.CompilerParams(
            collective_id=0, has_side_effects=True, vmem_limit_bytes=62 * 2**20
        ),
        name="v_cycle",
    )(source, labels)


def solution(mesh):
    sizes = tuple(mesh.shape[name] for name in ("gx", "gy", "gz"))
    return jax.shard_map(
        functools.partial(local, sizes),
        mesh=mesh,
        in_specs=(P("gz", "gy", "gx"), P("gz", "gy", "gx")),
        out_specs=P("gz", "gy", "gx"),
        check_vma=False,
    )
```

```python
import functools

import jax
import jax.numpy as jnp
import numpy as np
from jax import lax
from jax.experimental import pallas as pl
from jax.experimental.pallas import tpu as pltpu
from jax.sharding import PartitionSpec as P

COARSE = 6
SOLUTE_PERMITTIVITY = 0.1
SOLVENT_SCREENING = 0.004

MESH = pl.DeviceIdType.MESH
HIGHEST = lax.Precision.HIGHEST
F32 = jnp.float32
COPIES = 128

B0, B1, B2 = 24, 24, 16

NZ, NY, NX = 16, 32, 128


def iota(shape, dim):
    return lax.broadcasted_iota(jnp.int32, shape, dim)


def tiled(tile, rows, lanes):
    tile = jnp.concatenate([tile] * (rows // 8), axis=0)
    return jnp.concatenate([tile] * (lanes // 128), axis=1)


def dot(a, b):
    return jnp.dot(a, b, precision=HIGHEST, preferred_element_type=F32)


def neighbour_sum(before, c, behind, edges):
    rows, lanes = c.shape
    below, above, left, right = edges
    s = before + behind
    shifted = pltpu.roll(c, 1, 0)
    s = s + (shifted if below is None else jnp.where(below, 0.0, shifted))
    shifted = pltpu.roll(c, rows - 1, 0)
    s = s + (shifted if above is None else jnp.where(above, 0.0, shifted))
    shifted = pltpu.roll(c, 1, 1)
    s = s + (shifted if left is None else jnp.where(left, 0.0, shifted))
    shifted = pltpu.roll(c, lanes - 1, 1)
    s = s + (shifted if right is None else jnp.where(right, 0.0, shifted))
    return s


def neighbours(v, p, edges):
    c = v[p]
    return c, neighbour_sum(v[p - 1], c, v[p + 1], edges)


def parity_of(rows, lanes):
    return tiled((iota((8, 128), 0) + iota((8, 128), 1)) & 1, rows, lanes)


def far_first(size):
    return sorted(range(1, size), key=lambda step: -min(step, size - step))


def blocks(start, stop, block, body):
    count = (stop - start) // block

    def step(i, carry):
        body(start + block * i, start & 1, block)
        return carry

    if count > 1:
        lax.fori_loop(0, count, step, 0)
    elif count == 1:
        body(start, start & 1, block)
    if start + count * block < stop:
        first = start + count * block
        body(first, first & 1, stop - first)


def half_sweep(v, bd, wd, start, stop, colour, edges, block, shift=0):
    par = parity_of(*v.shape[1:])

    def body(first, odd, size):
        before, c = v[first - 1], v[first]
        for i in range(size):
            p = first + i
            behind = v[p + 1]
            s = neighbour_sum(before, c, behind, edges)
            new = bd(p - shift) + wd(p - shift) * s
            v[p] = jnp.where(par == ((odd + i + colour + shift) & 1), new, c)
            before, c = c, behind

    blocks(start, stop, block, body)


def first_half(v, bd, start, stop, block, shift=0):
    par = parity_of(*v.shape[1:])

    def body(first, odd, size):
        for i in range(size):
            p = first + i
            v[p] = jnp.where(par == ((odd + i + shift) & 1), bd(p - shift), 0.0)

    blocks(start, stop, block, body)


def kernel(sizes, *refs):
    (source_hbm, labels_hbm, out, source, labels, isem, bdw0, v0, vp0, d0, tt, ee, tv, ev, sy, syv, sxm0, sxm1, sxm2, sxc0, sxc1, sxc2, sxv, *rest) = refs
    ( pk, pkc, g1, g1c,
     c1, r1, v1, vp1, bd1, wd1, in1, vw1, bdw1, wdw1, c2, r2, v2, vp2, bd2, wd2, in2, z3, z3c, y3s, y3cs, y3, y3c, p3, p3c,
     c3, v3, bd3, wd3, in3, c4, v4, bd4, wd4, in4, work, work2, token, ssem, rsem) = rest
    count = dict(gx=sizes[0], gy=sizes[1], gz=sizes[2])
    gx, gy, gz = lax.axis_index("gx"), lax.axis_index("gy"), lax.axis_index("gz")
    number = [0]

    def device(offset):
        return tuple(
            lax.rem(here + (step + size) % size, size)
            for here, step, size in zip((gx, gy, gz), offset, sizes)
        )

    def send(source_ref, target_ref, offset):
        return send_to(source_ref, target_ref, device(offset))

    def send_to(source_ref, target_ref, target):
        i = number[0]
        number[0] += 1
        copy = pltpu.make_async_remote_copy(
            src_ref=source_ref,
            dst_ref=target_ref,
            send_sem=ssem.at[i],
            recv_sem=rsem.at[i],
            device_id=target,
            device_id_type=MESH,
        )
        copy.start()
        return copy

    def finish(copies):
        for copy in copies:
            copy.wait()

    peers = set()
    for a in (-1, 0, 1):
        for b in (-1, 0, 1):
            for c in (-1, 0, 1):
                peers.add((a, b, c))
    for b in (-1, 0, 1):
        for c in (-2, 2):
            peers.add((0, b, c))
    for i in range(1, sizes[0]):
        peers.add((i, 0, 0))
    for i in range(1, sizes[1]):
        peers.add((0, i, 0))
    peers = sorted({tuple(step % size for step, size in zip(o, sizes)) for o in peers} - {(0, 0, 0)})
    barrier = pltpu.get_barrier_semaphore()
    for offset in peers:
        pl.semaphore_signal(barrier, inc=1, device_id=device(offset), device_id_type=MESH)

    def tokens(level):
        for step in (2 << level, -(2 << level)):
            pl.semaphore_signal(token.at[level], inc=1, device_id=device((0, 0, step)), device_id_type=MESH)

    def wait_tokens(level):
        pl.semaphore_wait(token.at[level], 2)

    loads = [
        pltpu.make_async_copy(labels_hbm, labels, isem.at[0]),
        pltpu.make_async_copy(source_hbm, source, isem.at[1]),
    ]
    for load in loads:
        load.start()

    lane = iota((8, 128), 1)
    sub = iota((8, 128), 0)
    low4 = sub < 4
    x_lo, x_hi = gx > 0, gx < sizes[0] - 1
    y_lo, y_hi = gy > 0, gy < sizes[1] - 1
    z_lo, z_hi = gz > 0, gz < sizes[2] - 1

    def constants(label):
        permittivity = np.array([1.0, SOLUTE_PERMITTIVITY, 1.0], np.float32)
        screening = np.array([SOLVENT_SCREENING, 0.0, 0.0], np.float32)
        diagonal = np.float32(6.0) * permittivity + screening
        inverse = np.float32(1.0) / diagonal
        choose = lambda t: jnp.where(label == 1, t[1], jnp.where(label == 0, t[0], t[2])).astype(F32)
        return choose(inverse), choose(permittivity * inverse), choose(diagonal)

    def gathered_edges(plane, rows=NY, planes=NZ):
        group = tiled(lane >> 3, rows, 128)
        total = jnp.zeros((rows, 128), F32)
        for z in range(planes):
            total = jnp.where(group == z, pltpu.roll(plane(z), (8 * z + 4) % 128, 1), total)
        return total

    def with_corners(edges):
        return jnp.concatenate([edges, jnp.where(low4, edges[0:8], edges[NY - 8 : NY])], axis=0)

    for load in loads:
        load.wait()
    for z in range(NZ):
        inverse, relative, diagonal = constants(labels[z])
        bd = source[z] * inverse
        d0[z] = diagonal
        bdw0[0, z + 4, 0:NY, 0:NX] = bd
        bdw0[1, z + 4, 0:NY, 0:NX] = relative
        tt[0, z] = jnp.where(low4, bd[0:8], pltpu.roll(relative[0:8], 4, 0))
        tt[1, z] = jnp.where(low4, pltpu.roll(relative[NY - 8 : NY], 4, 0), bd[NY - 8 : NY])
    edge_bd = with_corners(gathered_edges(lambda z: bdw0[0, z + 4, 0:NY, 0:NX]))
    edge_wd = with_corners(gathered_edges(lambda z: bdw0[1, z + 4, 0:NY, 0:NX]))
    ee[0], ee[1] = edge_bd, edge_wd
    quarter = tiled(lane >> 5, NY + 8, 128)
    inner = jnp.where(quarter == 1, pltpu.roll(edge_wd, 32, 1), pltpu.roll(edge_wd, 96, 1))
    ee[2] = jnp.where((quarter == 0) | (quarter == 3), edge_bd, inner)

    def slot(step):
        return 1 - step

    def send_halo0(own, target, t_of, same_of, other_of, y_ref, xm_ref, xc_ref):
        copies = []
        for c in (1, -1):
            first = 16 if c == 1 else 4
            copies.append(
                send(
                    own.at[:, pl.ds(first, 4), pl.ds(0, NY), pl.ds(0, NX)],
                    target.at[:, pl.ds(0 if c == 1 else 20, 4), pl.ds(0, NY), pl.ds(0, NX)],
                    (0, 0, c),
                )
            )
        for c in (1, -1, 0):
            edges = other_of if c else same_of
            to = slot(c)
            for a in (1, -1):
                side = 0 if a == 1 else 1
                for b in (1, -1):
                    copies.append(
                        send(
                            edges(pl.ds(NY, 8)),
                            xc_ref[to].at[side, 0 if b == 1 else 1],
                            (a, b, c),
                        )
                    )
            for b in (1, -1):
                side = 0 if b == 1 else 1
                first, size, start = {0: (0, 16, 4), 1: (12, 4, 0), -1: (0, 4, 20)}[c]
                copies.append(send(t_of(b, pl.ds(first, size)), y_ref.at[side, pl.ds(start, size)], (0, b, c)))
            for a in (1, -1):
                side = 0 if a == 1 else 1
                copies.append(send(edges(pl.ds(0, NY)), xm_ref[to].at[side], (a, 0, c)))
        return copies

    in_low_half = (lane & 7) >= 4

    def fill_halo0(target, f, rows_of, columns, starts):
        x_valid = jnp.where(in_low_half, x_hi.astype(jnp.int32), x_lo.astype(jnp.int32))
        y_valid = jnp.where(low4, y_hi.astype(jnp.int32), y_lo.astype(jnp.int32))
        xy_valid = x_valid * y_valid
        edge_lanes = ((lane < 4) | (lane >= 124)).astype(jnp.int32)
        lane_main = tiled(in_low_half.astype(jnp.int32), NY, 128) > 0
        for part, (first, size, z_valid) in enumerate(((0, 4, z_lo), (4, 16, None), (20, 4, z_hi))):
            ok = jnp.int32(1) if z_valid is None else z_valid.astype(jnp.int32)
            (main_right, above_right, below_right), (main_left, above_left, below_left) = columns(part)
            main = jnp.where(lane_main, main_right, main_left)
            main = jnp.where(tiled(x_valid * ok, NY, 128) > 0, main, 0.0)
            above = jnp.where(in_low_half, above_right, above_left)
            below = jnp.where(in_low_half, below_right, below_left)
            corner = jnp.where(xy_valid * ok > 0, jnp.where(low4, above, below), 0.0)
            packed = jnp.concatenate([main, corner], axis=0)
            edges = tiled(edge_lanes, NY + 8, 128) > 0
            row_ok = y_valid * ok > 0
            for i in range(size):
                p = first + i
                rolled = pltpu.roll(packed, (252 - 8 * (starts[part] + i)) % 128, 1)
                target[f, p, :, NX : 2 * NX] = jnp.where(edges, rolled, 0.0)
                target[f, p, NY : NY + 8, 0:NX] = jnp.where(row_ok, rows_of(p), 0.0)
            if z_valid is not None:

                @pl.when(jnp.logical_not(z_valid))
                def _():
                    for i in range(size):
                        target[f, first + i, 0:NY, 0:NX] = jnp.zeros((NY, NX), F32)

    def fill_coefficients0():
        for f in (0, 1):

            def rows_of(p):
                if f == 0:
                    return jnp.where(low4, sy[1, p], sy[0, p])
                return pltpu.roll(jnp.where(low4, sy[0, p], sy[1, p]), 4, 0)

            def columns(part):
                if part == 1:
                    return [(sxm1[s, f], sxc1[s, 1, f], sxc1[s, 0, f]) for s in (1, 0)]
                m, c = (sxm0, sxc0) if part == 0 else (sxm2, sxc2)
                return [(m[s], c[s, 1], c[s, 0]) for s in (1, 0)]

            fill_halo0(bdw0, f, rows_of, columns, ((12, 0, 0), (8, 0, 4))[f])

    x_side = jnp.where(in_low_half, x_hi.astype(jnp.int32), x_lo.astype(jnp.int32))
    y_side = jnp.where(low4, y_hi.astype(jnp.int32), y_lo.astype(jnp.int32))

    def fill_v0():
        right = tiled(in_low_half.astype(jnp.int32), NY + 8, 128) > 0
        valid = tiled(x_side, NY + 8, 128) > 0
        edges = tiled(((lane < 4) | (lane >= 124)).astype(jnp.int32), NY + 8, 128) > 0
        packed = [jnp.where(valid, jnp.where(right, sxv[1, j], sxv[0, j]), 0.0) for j in (0, 1)]
        for p in range(NZ + 8):
            rolled = pltpu.roll(packed[p // 16], 124 - 8 * (p % 16), 1)
            vp0[0, p, :, NX : 2 * NX] = jnp.where(edges, rolled, 0.0)
        for first, inside in ((0, z_lo), (NZ + 4, z_hi)):

            @pl.when(jnp.logical_not(inside))
            def _():
                for p in range(first, first + 4):
                    vp0[0, p] = jnp.zeros((NY + 8, 2 * NX), F32)

    row_i, lane_i = iota((128, 128), 0), iota((128, 128), 1)
    to_low = jnp.where((row_i >> 1) == lane_i, 0.125, 0.0).astype(F32)
    to_high = jnp.where((row_i >> 1) == lane_i - 64, 0.125, 0.0).astype(F32)

    def rows_summed(size):
        half = size // 2
        return work[pl.ds(0, half, stride=2), :] + work[pl.ds(1, half, stride=2), :]

    def pack_level1(target, f):
        summed = rows_summed(256)
        target[f] = dot(summed[0:64], to_low) + dot(summed[64:128], to_high)

    def gather_gx(packed, slots):
        slots[gx] = packed[...]
        return [send(packed, slots.at[gx], (i, 0, 0)) for i in far_first(sizes[0])]

    def unpack_level1(slots, target, f):
        low = tiled((lane < 64).astype(jnp.int32), 16, 128) > 0
        for pair in range(2):
            for p in range(4):
                a = slots[2 * pair, f, pl.ds(16 * p, 16)]
                b = slots[2 * pair + 1, f, pl.ds(16 * p, 16)]
                lanes = slice(128 * pair, 128 * pair + 128)
                target(p, lanes, jnp.where(low, a, pltpu.roll(b, 64, 1)))
                target(p + 4, lanes, jnp.where(low, pltpu.roll(a, 64, 1), b))

    def coefficient(f, z):
        label = labels[z]
        if f == 0:
            return jnp.where(label == 1, SOLUTE_PERMITTIVITY, 1.0).astype(F32)
        return jnp.where(label == 0, SOLVENT_SCREENING, 0.0).astype(F32)

    for f in (0, 1):
        for k in range(8):
            work[32 * k : 32 * k + 32, :] = coefficient(f, 2 * k) + coefficient(f, 2 * k + 1)
        pack_level1(pkc, f)
    pl.semaphore_wait(barrier, len(peers))
    halo0 = send_halo0(
        bdw0,
        bdw0,
        lambda b, planes: tt.at[0 if b == -1 else 1, planes],
        lambda rows: ee.at[pl.ds(0, 2), rows],
        lambda rows: ee.at[2, rows],
        sy,
        (sxm0, sxm1, sxm2),
        (sxc0, sxc1, sxc2),
    )
    coef1 = gather_gx(pkc, g1c)
    tokens(0)

    def send_halo1(own, target, width):
        copies = []
        for c in (0, 1, -1):
            planes = {0: (8, 8, 8), 1: (16 - width, width, 8 - width), -1: (8, width, 16)}[c]
            for b in (0, 1, -1):
                rows = {0: (0, 16, 0), 1: (8, 8, 24), -1: (0, 8, 16)}[b]
                if (b, c) != (0, 0):
                    copies.append(
                        send(
                            own(pl.ds(planes[0], planes[1]), pl.ds(rows[0], rows[1])),
                            target(pl.ds(planes[2], planes[1]), pl.ds(rows[2], rows[1])),
                            (0, b, c),
                        )
                    )
        return copies

    def send_z1(own, target, width):
        return [
            send(
                own(pl.ds(16 - width if c == 1 else 8, width), pl.ds(0, 16)),
                target(pl.ds(8 - width if c == 1 else 16, width), pl.ds(0, 16)),
                (0, 0, c),
            )
            for c in (1, -1)
        ]

    def send_y1(view, width):
        planes = pl.ds(8 - width, 8 + 2 * width)
        return [
            send(view(planes, pl.ds(8 if b == 1 else 0, 8)), view(planes, pl.ds(24 if b == 1 else 16, 8)), (0, b, 0))
            for b in (1, -1)
        ]

    def send_z2(own, target):
        return [
            send(own(pl.ds(8, 4), pl.ds(0, 8)), target(pl.ds(8 - 4 * c, 4), pl.ds(0, 8)), (0, 0, c))
            for c in (2, -2, 1, -1)
        ]

    def send_y2(view):
        planes = pl.ds(0, 20)
        return [
            send(view(planes, pl.ds(0, 8)), view(planes, pl.ds(16 if b == 1 else 8, 8)), (0, b, 0)) for b in (1, -1)
        ]

    def send_halo2(own, target, steps):
        copies = []
        for c in steps:
            for b in (0, 1, -1):
                if (b, c) != (0, 0):
                    copies.append(
                        send(
                            own(pl.ds(8, 4), pl.ds(0, 8)),
                            target(pl.ds(8 - 4 * c, 4), pl.ds({0: 0, 1: 16, -1: 8}[b], 8)),
                            (0, b, c),
                        )
                    )
        return copies

    finish(coef1)
    for f in (0, 1):

        def put(p, lanes, value):
            c1[f, 8 + p, 0:16, lanes] = value

        unpack_level1(g1c, put, f)
    view1 = lambda a, b: c1.at[:, a, b]
    coef1 = send_z1(view1, view1, 5)
    half_i, half_l = iota((256, 128), 0), iota((256, 128), 1)
    to_half = jnp.where((half_i >> 1) == half_l, 0.125, 0.0).astype(F32)

    def coarsen_level1(pair):
        for k in range(4):
            total = pair(k)
            for h in (0, 1):
                work2[h, 16 * k : 16 * k + 16, :] = total[:, 128 * h : 128 * h + 128]
        halves = [work2[h, pl.ds(0, 32, stride=2), :] + work2[h, pl.ds(1, 32, stride=2), :] for h in (0, 1)]
        return dot(jnp.concatenate(halves, axis=1), to_half)

    for f in (0, 1):
        coarse = coarsen_level1(lambda k: c1[f, 8 + 2 * k, 0:16] + c1[f, 9 + 2 * k, 0:16])
        for k in range(4):
            c2[f, 8 + k, 0:8] = coarse[8 * k : 8 * k + 8]

    half_gz = jnp.where(gz >= sizes[2] // 2, 64, 0)

    def to_third(offset):
        return jnp.where((row_i >> 1) == lane_i - offset, 0.125, 0.0).astype(F32)

    def coarsen_level2(pair, matrix):
        for k in range(2):
            work[8 * k : 8 * k + 8, :] = pair(k)
        return dot(rows_summed(16), matrix)

    def gather_gz(piece, slots):
        slots[gz] = piece[...]
        return [send(piece, slots.at[gz], (0, 0, i)) for i in far_first(sizes[2])]

    def gather_gy(packed, target):
        target[gy] = packed[...]
        return [send(packed, target.at[gy], (0, i, 0)) for i in far_first(sizes[1])]

    view2 = lambda a, b: c2.at[:, a, b]
    coef2 = send_z2(view2, view2)
    p3c[...] = coarsen_level2(lambda k: c2[0, 8 + 2 * k, 0:8] + c2[0, 9 + 2 * k, 0:8], to_third(0)) + coarsen_level2(
        lambda k: c2[1, 8 + 2 * k, 0:8] + c2[1, 9 + 2 * k, 0:8], to_third(64)
    )

    finish(halo0)
    wait_tokens(0)
    tokens(1)
    fill_coefficients0()

    bd0_at = lambda p: bdw0[0, p]
    wd0_at = lambda p: bdw0[1, p]
    no_edges = (None,) * 4
    first_half(v0.at[0], bd0_at, 0, 24, B0)
    half_sweep(v0.at[0], bd0_at, wd0_at, 1, 23, 1, no_edges, B0)
    half_sweep(v0.at[0], bd0_at, wd0_at, 2, 22, 0, no_edges, B0)
    half_sweep(v0.at[0], bd0_at, wd0_at, 3, 21, 1, no_edges, B0)

    def residual0(k, carry):
        total = None
        for p in (4 + 2 * k, 5 + 2 * k):
            c, s = neighbours(v0.at[0], p, no_edges)
            value = bdw0[0, p, 0:NY, 0:NX] - c[0:NY, 0:NX] + bdw0[1, p, 0:NY, 0:NX] * s[0:NY, 0:NX]
            value = d0[p - 4] * value
            total = value if total is None else total + value
        work[pl.ds(32 * k, 32), :] = total
        return carry

    for k in range(8):
        residual0(k, 0)
    pack_level1(pk, 0)
    right1 = gather_gx(pk, g1)

    view_v0 = lambda ref, first: ref.at[0, pl.ds(first, 4), pl.ds(0, NY), pl.ds(0, NX)]
    halo_v0 = [
        send(view_v0(v0, 16), view_v0(vp0, 0), (0, 0, 1)),
        send(view_v0(v0, 4), view_v0(vp0, 20), (0, 0, -1)),
    ]
    finish(coef1)
    coef1 = send_y1(view1, 5)
    finish(coef2)
    coef2 = send_y2(view2)
    wait_tokens(1)
    coef3 = gather_gz(p3c, z3c)
    for z in range(NZ):
        vp0[0, z + 4, 0:NY, 0:NX] = v0[0, z + 4, 0:NY, 0:NX]


    def row_valid(rows, own):
        tiles = [jnp.ones((8, 128), jnp.int32)] * (own // 8)
        tiles += [0 * lane + y_hi.astype(jnp.int32), 0 * lane + y_lo.astype(jnp.int32)]
        return jnp.concatenate(tiles, axis=0)

    def plane_valid(p, below, size):
        before = jnp.where(p < below, z_lo.astype(jnp.int32), 1)
        behind = jnp.where(p >= below + size, z_hi.astype(jnp.int32), 1)
        return before * behind

    def coefficients(c_at, wd_at, in_at, planes, scale, valid):
        def body(p, carry):
            weight = c_at(0, p) * scale
            diagonal = 6.0 * weight + c_at(1, p)
            ok = diagonal > 0.0
            if valid is not None:
                ok = ok & (valid(p) > 0)
            inverse = jnp.where(ok, 1.0 / jnp.where(ok, diagonal, 1.0), 0.0)
            in_at[p] = inverse
            wd_at[p] = weight * inverse
            return carry

        for p in range(*planes):
            body(p, 0)

    rows1 = jnp.concatenate([row_valid(32, 16)] * 2, axis=1)
    rows2 = row_valid(24, 8)

    def valid1(p):
        return rows1 * plane_valid(p, 8, 8)

    def valid2(p):
        z = gz * 4 + p - 8
        ok = jnp.where(z >= 0, 1, 0) * jnp.where(z < 4 * sizes[2], 1, 0)
        return rows2 * ok

    finish(right1)

    def put_right(p, lanes, value):
        r1[8 + p, 0:16, lanes] = value

    unpack_level1(g1, put_right, 0)
    view_r1 = lambda a, b: r1.at[a, b]
    right1 = send_halo1(view_r1, view_r1, 5)

    finish(coef1)
    coefficients(lambda f, p: c1[f, p], wd1, in1, (3, 21), 0.25, valid1)
    finish(coef2)
    coefficients(lambda f, p: c2[f, p], wd2, in2, (2, 18), 0.0625, valid2)

    finish(halo_v0)
    for z in range(NZ + 8):
        tv[z] = jnp.where(low4, vp0[0, z, 0:8, 0:NX], vp0[0, z, NY - 8 : NY, 0:NX])
    halo_v0 = [send(tv, syv.at[0 if b == 1 else 1], (0, b, 0)) for b in (1, -1)]

    finish(right1)

    def scaled(target, right, inverse, start, stop):
        def body(p, carry):
            target[p] = right[p] * inverse[p]
            return carry

        for p in range(start, stop):
            body(p, 0)

    scaled(bd1, r1, in1, 3, 21)
    lanes1 = jnp.concatenate([lane, lane + 128], axis=1)
    lanes1 = jnp.concatenate([lanes1] * 4, axis=0)
    edges1 = (None, None, lanes1 == 0, lanes1 == 255)
    bd1_at = lambda p: bd1[p]
    wd1_at = lambda p: wd1[p]
    first_half(v1, bd1_at, 4, 20, B1)
    half_sweep(v1, bd1_at, wd1_at, 5, 19, 1, edges1, B1)
    half_sweep(v1, bd1_at, wd1_at, 6, 18, 0, edges1, B1)
    half_sweep(v1, bd1_at, wd1_at, 7, 17, 1, edges1, B1)

    def residual1(k):
        total = None
        for p in (8 + 2 * k, 9 + 2 * k):
            c, s = neighbours(v1, p, edges1)
            diagonal = 1.5 * c1[0, p, 0:16] + c1[1, p, 0:16]
            value = diagonal * (bd1[p, 0:16] - c[0:16] + wd1[p, 0:16] * s[0:16])
            total = value if total is None else total + value
        return total

    to_third_own = jnp.where((lane_i - half_gz >= 0) & (lane_i - half_gz < 64), to_third(half_gz), 0.0)
    coarse = coarsen_level1(residual1)
    for k in range(4):
        r2[8 + k, 0:8] = coarse[8 * k : 8 * k + 8]
    view_r2 = lambda a, b: r2.at[a, b]
    right2 = send_halo2(view_r2, view_r2, (0, 1, -1))
    right2_far = send_halo2(view_r2, view_r2, (2, -2))
    for k in range(8):
        vp1[8 + k, 0:16] = v1[8 + k, 0:16]
    halo_v1 = send_z1(lambda a, b: v1.at[a, b], lambda a, b: vp1.at[a, b], 6)
    finish(coef3)
    low8 = lane < 64
    for k in range(8):
        a, b = z3c[k], z3c[k + 8]
        y3cs[0, k] = jnp.where(low8, a, pltpu.roll(b, 64, 1))
        y3cs[1, k] = jnp.where(low8, pltpu.roll(a, 64, 1), b)
    coef3 = gather_gy(y3cs, y3c)
    finish(halo_v0)
    for p in range(NZ + 8):
        rows = jnp.where(low4, syv[1, p], syv[0, p])
        vp0[0, p, NY : NY + 8, 0:NX] = jnp.where(y_side > 0, rows, 0.0)
    ev[0] = gathered_edges(lambda z: vp0[0, z, :, 0:NX], NY + 8, 16)
    ev[1] = gathered_edges(lambda z: vp0[0, z + 16, :, 0:NX], NY + 8, 8)
    halo_v0 = [send(ev, sxv.at[0 if a == 1 else 1], (a, 0, 0)) for a in (1, -1)]

    finish(right2)
    scaled(bd2, r2, in2, 4, 16)
    lanes2 = jnp.concatenate([lane] * 3, axis=0)
    edges2 = (None, None, lanes2 == 0, lanes2 == 127)
    bd2_at = lambda p: bd2[p]
    wd2_at = lambda p: wd2[p]
    first_half(v2, bd2_at, 4, 16, B2)
    half_sweep(v2, bd2_at, wd2_at, 5, 15, 1, edges2, B2)
    half_sweep(v2, bd2_at, wd2_at, 6, 14, 0, edges2, B2)
    half_sweep(v2, bd2_at, wd2_at, 7, 13, 1, edges2, B2)

    def residual2(k):
        total = None
        for p in (8 + 2 * k, 9 + 2 * k):
            c, s = neighbours(v2, p, edges2)
            diagonal = 0.375 * c2[0, p, 0:8] + c2[1, p, 0:8]
            value = diagonal * (bd2[p, 0:8] - c[0:8] + wd2[p, 0:8] * s[0:8])
            total = value if total is None else total + value
        return total

    p3[...] = coarsen_level2(residual2, to_third_own)
    right3 = gather_gz(p3, z3)
    for k in range(4):
        vp2[8 + k, 0:8] = v2[8 + k, 0:8]
    halo_v2 = send_z2(lambda a, b: v2.at[a, b], lambda a, b: vp2.at[a, b])
    finish(halo_v1)
    halo_v1 = send_y1(lambda a, b: vp1.at[a, b], 6)

    finish(coef3)

    def unpack_level3(slots, f, put):
        for k in range(8):
            for t in range(4):
                a, b = slots[2 * t, f, k], slots[2 * t + 1, f, k]
                put(2 * k, slice(8 * t, 8 * t + 8), jnp.where(low4, a, pltpu.roll(b, 4, 0)))
                put(2 * k + 1, slice(8 * t, 8 * t + 8), jnp.where(low4, pltpu.roll(a, 4, 0), b))

    for f in (0, 1):

        def put3(p, rows, value):
            c3[f, p, rows] = value

        unpack_level3(y3c, f, put3)
    coefficients(lambda f, p: c3[f, p], wd3, in3, (0, 16), 0.25**3, None)

    to_fourth = jnp.where(
        ((row_i >> 6) == (lane_i >> 6)) & (((row_i & 63) >> 1) == (lane_i & 63)), 0.125, 0.0
    ).astype(F32)

    def coarsen_level3(pair):
        for k in range(8):
            work[32 * k : 32 * k + 32, :] = pair(k)
        return dot(rows_summed(256), to_fourth)

    for f in (0, 1):
        coarse = coarsen_level3(lambda k: c3[f, 2 * k] + c3[f, 2 * k + 1])
        for k in range(8):
            c4[f, k] = coarse[16 * k : 16 * k + 16]
    coefficients(lambda f, p: c4[f, p], wd4, in4, (0, 8), 0.25**4, None)
    finish(right2_far)
    scaled(bd2, r2, in2, 2, 4)
    scaled(bd2, r2, in2, 16, 18)

    def clean(target, valid, start, stop):
        def body(p, carry):
            target[p] = jnp.where(valid(p) > 0, target[p], 0.0)
            return carry

        for p in range(start, stop):
            body(p, 0)

    finish(halo_v0)
    fill_v0()
    finish(halo_v2)
    halo_v2 = send_y2(lambda a, b: vp2.at[a, b])
    finish(right3)
    for k in range(8):
        y3s[0, k] = z3[k] + z3[k + 8]
    right3 = gather_gy(y3s, y3)
    finish(halo_v1)
    column1 = 64 * gx - 32 + jnp.concatenate([lane] * 4, axis=0)
    inside1 = jnp.where(column1 >= 0, 1, 0) * jnp.where(column1 < 64 * sizes[0], 1, 0)
    turn = lax.rem(32 + 64 * (sizes[0] - gx), 64 * sizes[0])

    def beside(plane, valid):
        return jnp.where(valid > 0, pltpu.roll(plane, turn, 1)[:, 0:128], 0.0)

    for p in range(2, 22):
        vw1[p] = beside(vp1[p], inside1 * valid1(p)[:, 0:128])
    for p in range(3, 21):
        bdw1[p] = beside(bd1[p], inside1)
        wdw1[p] = beside(wd1[p], inside1)
    finish(halo_v2)
    clean(vp2, valid2, 0, 20)
    finish(right3)

    def put_bd3(p, rows, value):
        bd3[p, rows] = value * in3[p, rows]

    unpack_level3(y3, 0, put_bd3)

    def ends(v, planes):
        low = tiled((lane < 64).astype(jnp.int32), v.shape[1], 128) > 0
        v[0] = jnp.where(low, 0.0, pltpu.roll(v[planes], 64, 1))
        v[planes + 1] = jnp.where(low, pltpu.roll(v[1], 64, 1), 0.0)

    lanes3 = jnp.concatenate([lane & 63] * 4, axis=0)
    rows3 = iota((32, 128), 0)
    edges3 = (rows3 == 0, rows3 == 31, lanes3 == 0, lanes3 == 63)
    rows4 = iota((16, 128), 0)
    edges4 = (rows4 == 0, rows4 == 15, None, None)
    bd3_at = lambda p: bd3[p]
    wd3_at = lambda p: wd3[p]
    bd4_at = lambda p: bd4[p]
    wd4_at = lambda p: wd4[p]

    def half3(colour):
        ends(v3, 16)
        half_sweep(v3, bd3_at, wd3_at, 1, 17, colour, edges3, 16, 1)

    def half4(colour):
        ends(v4, 8)
        half_sweep(v4, bd4_at, wd4_at, 1, 9, colour, edges4, 8, 1)

    first_half(v3, bd3_at, 1, 17, 16, 1)
    half3(1)
    half3(0)
    half3(1)
    ends(v3, 16)

    def residual3(k):
        total = None
        for p in (2 * k, 2 * k + 1):
            c, s = neighbours(v3, p + 1, edges3)
            diagonal = 6.0 * 0.25**3 * c3[0, p] + c3[1, p]
            value = diagonal * (bd3[p] - c + wd3[p] * s)
            total = value if total is None else total + value
        return total

    coarse = coarsen_level3(residual3)
    for k in range(8):
        bd4[k] = coarse[16 * k : 16 * k + 16] * in4[k]
    first_half(v4, bd4_at, 1, 9, 8, 1)
    half4(1)

    def sweep4(i, carry):
        half4(0)
        half4(1)
        return carry

    lax.fori_loop(1, COARSE, sweep4, 0)

    from_fourth = jnp.where(
        ((row_i >> 6) == (lane_i >> 6)) & (((lane_i & 63) >> 1) == (row_i & 63)), 1.0, 0.0
    ).astype(F32)
    wide = jnp.concatenate([v4[1 + k] for k in range(8)], axis=0)
    wide = dot(wide, from_fourth)
    work[pl.ds(0, 128, stride=2), :] = wide
    work[pl.ds(1, 128, stride=2), :] = wide

    def add3(k, carry):
        correction = work[pl.ds(32 * k, 32), :]
        v3[1 + 2 * k] = v3[1 + 2 * k] + correction
        v3[2 + 2 * k] = v3[2 + 2 * k] + correction
        return carry

    for i in range(8):
        add3(i, 0)
    half3(0)
    half3(1)
    half3(0)
    half3(1)

    from_third = jnp.where((lane_i >> 1) == (row_i & 63), 1.0, 0.0).astype(F32)
    lane_half = tiled(lane >> 6, 32, 128)
    picked = []
    for i in range(10):
        z = 2 * gz - 4 + i
        inside = jnp.where(z >= 0, 1, 0) * jnp.where(z < 32, 1, 0)
        z = jnp.clip(z, 0, 31)
        index, half = z & 15, z >> 4
        keep = jnp.where(lane_half == half, inside, 0) > 0
        picked.append(jnp.where(keep, v3[1 + index], 0.0))
    wide = dot(jnp.concatenate(picked, axis=0), from_third)
    work[pl.ds(0, 320, stride=2), :] = wide
    work[pl.ds(1, 320, stride=2), :] = wide
    own_row = pl.multiple_of(8 * gy, 8)
    next_row = pl.multiple_of(8 * jnp.minimum(gy + 1, sizes[1] - 1), 8)
    before_row = pl.multiple_of(8 * jnp.maximum(gy - 1, 0), 8)

    def add2(i, carry):
        parts = [work[pl.ds(64 * i + row, 8), :] for row in (own_row, next_row, before_row)]
        correction = jnp.where(rows2 > 0, jnp.concatenate(parts, axis=0), 0.0)
        vp2[2 * i] = vp2[2 * i] + correction
        vp2[2 * i + 1] = vp2[2 * i + 1] + correction
        return carry

    for i in range(10):
        add2(i, 0)
    half_sweep(vp2, bd2_at, wd2_at, 2, 18, 0, edges2, B2)
    half_sweep(vp2, bd2_at, wd2_at, 3, 17, 1, edges2, B2)
    half_sweep(vp2, bd2_at, wd2_at, 4, 16, 0, edges2, B2)
    half_sweep(vp2, bd2_at, wd2_at, 5, 15, 1, edges2, B2)

    def copied(base, rows):
        return jnp.concatenate([work2[h, pl.ds(base, rows), :] for h in (0, 1)], axis=1)

    from_second = jnp.where(((64 * gx - 32 + lane_i) >> 1) == row_i, 1.0, 0.0).astype(F32)
    picked = []
    for p in range(5, 15):
        picked += [vp2[p, 0:8], jnp.where(low4, vp2[p, 8:16], vp2[p, 16:24])]
    wide = dot(jnp.concatenate(picked, axis=0), from_second)
    work[pl.ds(0, 160, stride=2), :] = wide
    work[pl.ds(1, 160, stride=2), :] = wide

    def add1(i, carry):
        correction = work[32 * i : 32 * i + 32, :]
        vw1[2 + 2 * i] = vw1[2 + 2 * i] + correction
        vw1[3 + 2 * i] = vw1[3 + 2 * i] + correction
        return carry

    for i in range(10):
        add1(i, 0)
    bdw1_at = lambda p: bdw1[p]
    wdw1_at = lambda p: wdw1[p]
    no_edges = (None,) * 4
    half_sweep(vw1, bdw1_at, wdw1_at, 3, 21, 0, no_edges, B1)
    half_sweep(vw1, bdw1_at, wdw1_at, 4, 20, 1, no_edges, B1)
    half_sweep(vw1, bdw1_at, wdw1_at, 5, 19, 0, no_edges, B1)
    half_sweep(vw1, bdw1_at, wdw1_at, 6, 18, 1, no_edges, B1)

    first_i, first_l = iota((128, 256), 0), iota((128, 256), 1)
    column = jnp.where(first_l < NX + 4, first_l, jnp.where(first_l >= 2 * NX - 4, first_l - 2 * NX, -1024))
    x = jnp.where(column > -1024, gx * NX + column, -1024)
    from_first = jnp.where((x >> 1) == 64 * gx - 32 + first_i, 1.0, 0.0).astype(F32)
    picked = []
    for p in range(6, 18):
        picked += [vw1[p, 0:16], jnp.where(sub < 2, vw1[p, 16:24], pltpu.roll(vw1[p, 24:32], 4, 0))]
    wide = dot(jnp.concatenate(picked, axis=0), from_first)
    for h in (0, 1):
        part = wide[:, 128 * h : 128 * h + 128]
        work2[h, pl.ds(0, 288, stride=2), :] = part
        work2[h, pl.ds(1, 288, stride=2), :] = part

    def add0(i, carry):
        correction = copied(48 * i, 40)
        vp0[0, 2 * i] = vp0[0, 2 * i] + correction
        vp0[0, 2 * i + 1] = vp0[0, 2 * i + 1] + correction
        return carry

    for i in range(12):
        add0(i, 0)
    half_sweep(vp0.at[0], bd0_at, wd0_at, 1, 23, 0, no_edges, B0)
    half_sweep(vp0.at[0], bd0_at, wd0_at, 2, 22, 1, no_edges, B0)
    half_sweep(vp0.at[0], bd0_at, wd0_at, 3, 21, 0, no_edges, B0)
    par = parity_of(NY, NX)

    def last(first, odd, size):
        before, c = vp0[0, first - 1], vp0[0, first]
        for i in range(size):
            p = first + i
            behind = vp0[0, p + 1]
            s = neighbour_sum(before, c, behind, no_edges)
            new = bdw0[0, p, 0:NY, 0:NX] + bdw0[1, p, 0:NY, 0:NX] * s[0:NY, 0:NX]
            out[p - 4] = jnp.where(par == ((odd + i + 1) & 1), new, c[0:NY, 0:NX])
            before, c = c, behind

    blocks(4, 20, B0, last)


def local(sizes, source, labels):
    vmem = lambda *shape: pltpu.VMEM(shape, F32)
    scratch = [
        vmem(16, 32, 128),
        pltpu.VMEM((16, 32, 128), jnp.int32),
        pltpu.SemaphoreType.DMA((2,)),
        vmem(2, 24, 40, 256),
        vmem(1, 24, 40, 256),
        vmem(1, 24, 40, 256),
        vmem(16, 32, 128),
        vmem(2, 16, 8, 128),
        vmem(3, 40, 128),
        vmem(24, 8, 128),
        vmem(2, 40, 128),
        vmem(2, 24, 8, 128),
        vmem(2, 24, 8, 128),
        vmem(2, 32, 128),
        vmem(2, 2, 32, 128),
        vmem(2, 32, 128),
        vmem(2, 2, 8, 128),
        vmem(2, 2, 2, 8, 128),
        vmem(2, 2, 8, 128),
        vmem(2, 2, 40, 128),
        vmem(1, 64, 128),
        vmem(2, 64, 128),
        vmem(sizes[0], 1, 64, 128),
        vmem(sizes[0], 2, 64, 128),
        vmem(2, 24, 32, 256),
        vmem(24, 32, 256),
        vmem(24, 32, 256),
        vmem(24, 32, 256),
        vmem(24, 32, 256),
        vmem(24, 32, 256),
        vmem(24, 32, 256),
        vmem(24, 32, 128),
        vmem(24, 32, 128),
        vmem(24, 32, 128),
        vmem(2, 20, 24, 128),
        vmem(20, 24, 128),
        vmem(20, 24, 128),
        vmem(20, 24, 128),
        vmem(20, 24, 128),
        vmem(20, 24, 128),
        vmem(20, 24, 128),
        vmem(sizes[2], 8, 128),
        vmem(sizes[2], 8, 128),
        vmem(1, 8, 8, 128),
        vmem(2, 8, 8, 128),
        vmem(sizes[1], 1, 8, 8, 128),
        vmem(sizes[1], 2, 8, 8, 128),
        vmem(8, 128),
        vmem(8, 128),
        vmem(2, 16, 32, 128),
        vmem(18, 32, 128),
        vmem(16, 32, 128),
        vmem(16, 32, 128),
        vmem(16, 32, 128),
        vmem(2, 8, 16, 128),
        vmem(10, 16, 128),
        vmem(8, 16, 128),
        vmem(8, 16, 128),
        vmem(8, 16, 128),
        vmem(648, 128),
        vmem(2, 584, 128),
        pltpu.SemaphoreType.REGULAR((2,)),
        pltpu.SemaphoreType.DMA((COPIES,)),
        pltpu.SemaphoreType.DMA((COPIES,)),
    ]
    return pl.pallas_call(
        functools.partial(kernel, sizes),
        out_shape=jax.ShapeDtypeStruct(source.shape, F32),
        in_specs=[pl.BlockSpec(memory_space=pltpu.HBM)] * 2,
        out_specs=pl.BlockSpec(memory_space=pltpu.VMEM),
        scratch_shapes=scratch,
        compiler_params=pltpu.CompilerParams(
            collective_id=0, has_side_effects=True, vmem_limit_bytes=62 * 2**20
        ),
        name="v_cycle",
    )(source, labels)


def solution(mesh):
    sizes = tuple(mesh.shape[name] for name in ("gx", "gy", "gz"))
    return jax.shard_map(
        functools.partial(local, sizes),
        mesh=mesh,
        in_specs=(P("gz", "gy", "gx"), P("gz", "gy", "gx")),
        out_specs=P("gz", "gy", "gx"),
        check_vma=False,
    )
```
